32 devices in a mesh: wide: 8 (over y, x, core), narrow: 4 (over z).
Axes of the slice: x: 2, y: 2, z: 4, core: 2. Of those that a mesh axis runs over, the one named last changes fastest.
Arguments:
- hidden_in: bfloat16 [32, 512, 1024], P(('wide', 'narrow')), may hold values from -6 to 6
- memory: bfloat16 [32, 2, 588, 1024], P(('wide', 'narrow')), may hold values from -6 to 6
- segment_ids: int32 [32, 512], P(('wide', 'narrow')), may hold values from 0 to 3, never falling along the last dimension, each value on 1 to 256 neighbouring positions
- image_ids: int32 [32, 4], P(('wide', 'narrow')), may hold values from 0 to 1
- attn_in: bfloat16 [6, 1024, 1024], P(None, 'narrow'), may hold values from -0.1875 to 0.1875
- attn_out: bfloat16 [2, 1024, 1024], P(None, 'narrow'), may hold values from -1.5 to 1.5
- mlp_in: bfloat16 [1024, 4096], P('narrow'), may hold values from -0.1875 to 0.1875
- mlp_out: bfloat16 [4096, 1024], P('narrow'), may hold values from -0.09375 to 0.09375
- gains: bfloat16 [3, 1024], P(None, 'narrow'), may hold values from 0.5 to 1.5
- shifts: bfloat16 [10, 1024], P(None, 'narrow'), may hold values from -3 to 3
- mlp_bias: bfloat16 [4096], P('narrow'), may hold values from -3 to 3
- cotangent: bfloat16 [32, 512, 1024], P(('wide', 'narrow')), may hold values from -6 to 6
Outputs:
- layer_out: bfloat16 [32, 512, 1024], P(('wide', 'narrow'))
- grad_input: float32 [32, 512, 1024], P(('wide', 'narrow'))
- grad_memory: float32 [32, 2, 588, 1024], P(('wide', 'narrow'))
- grad_attn_in: float32 [6, 1024, 1024], P(None, 'narrow')
- grad_attn_out: float32 [2, 1024, 1024], P(None, 'narrow')
- grad_mlp_in: float32 [1024, 4096], P('narrow')
- grad_mlp_out: float32 [4096, 1024], P('narrow')
- grad_gains: float32 [3, 1024], P(None, 'narrow')
- grad_shifts: float32 [10, 1024], P(None, 'narrow')
- grad_mlp_bias: float32 [4096], P('narrow')
The draws below stay inside these ranges and needn't reach their ends.
Inputs may be any that keep to these rules, and one draw needn't show every extreme that they name: `segment_ids`: in each row the page id never falls; each of the 4 pages holds 1 to 256 tokens, and one holds exactly 256.
All inputs are finite; a program needn't handle non-finite values.
Results may differ from the reference program's by a relative error of at most 0.017.
Values may be sent and summed in bfloat16 or wider, within the bound.
A program may use at most 384 MiB of HBM per device.

```python
import math
import jax
import jax.numpy as jnp
import numpy as np
from jax import lax

D = 1024
HEADS = 16
FF = 4096
MEM = 588
ROW_DEV = 512
SEG_ROW = 4
IMG_ROW = 2
HEAD_DIM = 64
ROWS = 32


def plant(array, key, least, top_value):
    extent = array.shape
    index_at = [jax.random.randint(jax.random.fold_in(key, axis), (), 0, extent[axis]) for axis in range(len(extent))]
    array = array.at[tuple(index_at)].set(least)
    longest = extent.index(max(extent))
    index_at[longest] = (index_at[longest] + 1) % extent[longest]
    return array.at[tuple(index_at)].set(top_value)


def block_levels(stream_key, dims, split, least, largest):
    factor_of, own = 1.0, jax.random.fold_in(stream_key, 6)
    for dim, blocks in split:
        steps = jnp.exp(jax.random.uniform(jax.random.fold_in(own, dim), (blocks,), jnp.float32, least / len(split), largest / len(split)))
        factor_of = factor_of * jnp.repeat(steps, dims[dim] // blocks).reshape([-1 if axis == dim else 1 for axis in range(len(dims))])
    return factor_of


def split_up(amount, total, reach, slope):
    portions = [(1 << 20) // math.isqrt(standing ** slope) + 1 for standing in range(2, amount + 1)]
    rest, holding = total - reach - (amount - 1), [1] * (amount - 1)
    while rest > 0:
        movable = [i for i in range(amount - 1) if holding[i] < reach]
        whole, remaining = sum([portions[i] for i in movable]), rest
        for i in movable:
            more = min(reach - holding[i], max(1, remaining * portions[i] // whole), rest)
            holding[i] = holding[i] + more
            rest = rest - more
    return np.array([reach] + holding)


def uneven(key, amount, total, reach, skew):
    if amount == 2:
        one = jax.random.randint(key, (), max(1, total - reach), min(reach, total - 1) + 1)
        return jnp.stack([one, total - one])
    lengths = jnp.asarray(split_up(amount, total, reach, skew), jnp.int32)
    twos = (amount - 1) // 2
    source_of, receiver = lengths[1:1 + 2 * twos:2], lengths[2:2 + 2 * twos:2]
    room = jnp.minimum(source_of - 1, reach - receiver)
    shifted = jax.random.randint(jax.random.fold_in(key, 1), (twos,), 0, 1 << 20) % (room + 1)
    lengths = lengths.at[1:1 + 2 * twos:2].set(source_of - shifted).at[2:2 + 2 * twos:2].set(receiver + shifted)
    return lengths[jax.random.permutation(jax.random.fold_in(key, 2), amount)]


def scatter_about(own_key, dims, scale, most, split=(), held_as=jnp.bfloat16):
    level = block_levels(own_key, dims, split, -0.22, 0.18) if split else 1.0
    values = jax.random.normal(own_key, dims, jnp.float32) * scale * level
    return jnp.minimum(jnp.maximum(values, -most), most).astype(held_as)


def setup_inputs(seed: int = 0) -> dict:
    key_of = jax.random.split(jax.random.key(seed), 13)
    return {
        "hidden_in": scatter_about(key_of[0], (ROWS, ROW_DEV, D), 1.0, 6.0, ((0, 32),)),
        "memory": scatter_about(key_of[1], (ROWS, IMG_ROW, MEM, D), 1.0, 6.0, ((0, 32),)),
        "segment_ids": jax.vmap(lambda own: jnp.searchsorted(jnp.cumsum(uneven(own, SEG_ROW, ROW_DEV, ROW_DEV // 2, 2)), jnp.arange(ROW_DEV), side="right"))(jax.random.split(key_of[2], ROWS)).reshape((ROWS, ROW_DEV)).astype(jnp.int32),
        "image_ids": plant(jax.random.randint(key_of[3], (ROWS, SEG_ROW), 0, IMG_ROW), jax.random.fold_in(key_of[3], 1), 0, IMG_ROW - 1).astype(jnp.int32),
        "attn_in": scatter_about(key_of[4], (6, D, D), D ** -0.5, 0.1875, ((1, 4),)),
        "attn_out": scatter_about(key_of[5], (2, D, D), (D // 64) ** -0.5, 1.5, ((1, 4),)),
        "mlp_in": scatter_about(key_of[6], (D, FF), D ** -0.5, 0.1875, ((0, 4),)),
        "mlp_out": scatter_about(key_of[7], (FF, D), FF ** -0.5, 0.09375, ((0, 4),)),
        "gains": jnp.clip(1.0 + 0.1 * jax.random.normal(key_of[8], (3, D), jnp.float32), 0.5, 1.5).astype(jnp.bfloat16),
        "shifts": scatter_about(key_of[9], (10, D), 0.5, 3.0, ((1, 4),)),
        "mlp_bias": scatter_about(key_of[10], (FF,), 0.5, 3.0, ((0, 4),)),
        "cotangent": scatter_about(key_of[11], (ROWS, ROW_DEV, D), 1.0, 6.0, ((0, 32),)),
    }


@jax.custom_vjp
def low(v):
    return lax.optimization_barrier(v.astype(jnp.bfloat16)).astype(jnp.float32)

@jax.custom_vjp
def low_back(v):
    return v

def low_keep(v):
    return (low(v), None)

def low_pass(kept, grad):
    return (grad,)

def back_keep(v):
    return (v, None)

def back_low(kept, grad):
    return (low(grad),)
low.defvjp(low_keep, low_pass)
low_back.defvjp(back_keep, back_low)
norm_eps = 1e-05
masked_score = -1e+30

def rounded_both(values):
    return low_back(low(values))

def matmul(left, right):
    return jnp.dot(left, right, precision=lax.Precision.HIGHEST)

def layer_norm(values, gain, shift):
    centered = values - lax.optimization_barrier(jnp.mean(values, axis=-1, keepdims=True))
    variance = lax.optimization_barrier(jnp.mean(centered * centered, axis=-1, keepdims=True))
    return centered * lax.rsqrt(variance + norm_eps) * gain + shift

def attention(queries, keys_all, values_all, allowed):
    rows = queries.shape[0]
    head_q = queries.reshape(rows, HEADS, HEAD_DIM)
    head_k = keys_all.reshape(keys_all.shape[0], HEADS, HEAD_DIM)
    head_v = values_all.reshape(values_all.shape[0], HEADS, HEAD_DIM)
    scores = low_back(jnp.einsum('qhe,khe->hqk', head_q, head_k, precision=lax.Precision.HIGHEST))
    scores = jnp.where(allowed[None], scores, masked_score)
    top = lax.optimization_barrier(jnp.max(scores, axis=-1, keepdims=True))
    expo = jnp.exp(scores - top)
    probs = low(expo / lax.optimization_barrier(jnp.sum(expo, axis=-1, keepdims=True)))
    mixed = jnp.einsum('hqk,khe->qhe', probs, head_v, precision=lax.Precision.HIGHEST)
    return rounded_both(mixed.reshape(rows, HEADS * HEAD_DIM))

def row_forward(tokens, memories, segments, images, params):
    attn_in, attn_out, mlp_in, mlp_out, gains, shifts, mlp_bias = params
    scale = HEAD_DIM ** (-0.5)
    rows = tokens.shape[0]
    normed_one = low(layer_norm(tokens, gains[0], shifts[6]))
    self_query = rounded_both((matmul(normed_one, attn_in[0]) + shifts[0]) * scale)
    self_keys = rounded_both(matmul(normed_one, attn_in[1]))
    self_values = rounded_both(matmul(normed_one, attn_in[2]) + shifts[1])
    position = jnp.arange(rows)
    self_allowed = (segments[:, None] == segments[None, :]) & (position[None, :] <= position[:, None])
    self_mix = attention(self_query, self_keys, self_values, self_allowed)
    after_self = tokens + low_back(matmul(self_mix, attn_out[0])) + shifts[2]
    normed_two = low(layer_norm(after_self, gains[1], shifts[7]))
    cross_query = rounded_both((matmul(normed_two, attn_in[3]) + shifts[3]) * scale)
    mem_flat = memories.reshape(IMG_ROW * MEM, D)
    cross_keys = rounded_both(matmul(mem_flat, attn_in[4]))
    cross_values = rounded_both(matmul(mem_flat, attn_in[5]) + shifts[4])
    token_image = lax.optimization_barrier(jnp.sum(jnp.where(segments[:, None] == jnp.arange(SEG_ROW)[None, :], images[None, :], 0), axis=1))
    key_image = jnp.arange(IMG_ROW * MEM) // MEM
    cross_mix = attention(cross_query, cross_keys, cross_values, token_image[:, None] == key_image[None, :])
    after_cross = after_self + low_back(matmul(cross_mix, attn_out[1])) + shifts[5]
    normed_three = low(layer_norm(after_cross, gains[2], shifts[8]))
    pre_act = low_back(matmul(normed_three, mlp_in) + mlp_bias)
    activated = low(jax.nn.gelu(pre_act, approximate=False))
    return after_cross + low_back(matmul(activated, mlp_out)) + shifts[9]

def reference(hidden_in, memory, segment_ids, image_ids, attn_in, attn_out, mlp_in, mlp_out, gains, shifts, mlp_bias, cotangent):
    params = tuple((item.astype(jnp.float32) for item in (attn_in, attn_out, mlp_in, mlp_out, gains, shifts, mlp_bias)))
    tokens = hidden_in.astype(jnp.float32)
    memories = memory.astype(jnp.float32)

    def forward(tokens, memories, params):

        def one_row(items):
            return jax.checkpoint(row_forward)(items[0], items[1], items[2], items[3], params)
        return lax.map(one_row, (tokens, memories, segment_ids, image_ids))
    result, pullback = jax.vjp(forward, tokens, memories, params)
    grad_tokens, grad_memories, grad_params = pullback(cotangent.astype(jnp.float32))
    return (result.astype(jnp.bfloat16), grad_tokens, grad_memories, grad_params[0], grad_params[1], grad_params[2], grad_params[3], grad_params[4], grad_params[5], grad_params[6])
```

```python
import functools

import jax
import jax.numpy as jnp
from jax import lax
from jax.experimental import pallas as pl
from jax.experimental.pallas import tpu as pltpu
from jax.sharding import PartitionSpec as P

MESH = pl.DeviceIdType.MESH
F32 = jnp.float32
BF16 = jnp.bfloat16
MIB = 1 << 20


class Geometry:
    def __init__(self, mesh, width):
        self.wide = mesh.shape["wide"]
        self.narrow = mesh.shape["narrow"]
        self.a_count = self.wide // 4
        self.width = width
        self.rows = width // self.narrow
        self.core_rows = self.rows // 2
        self.piece_rows = self.core_rows // self.a_count
        self.half = width // 2
        self.quarter = width // 4

    def place(self):
        w = lax.axis_index("wide")
        n = lax.axis_index("narrow")
        self.w, self.n = w, n
        self.a, self.b, self.c = w // 4, lax.rem(w // 2, 2), lax.rem(w, 2)
        self.core_at = pl.multiple_of(self.c * self.core_rows, self.core_rows)
        self.b_at = pl.multiple_of(self.b * self.quarter, self.quarter)
        self.mine = self.piece_at(self.a, self.c)
        self.other_core = (w + 1 - 2 * self.c, n)
        self.b_peer = (w + 2 - 4 * self.b, n)

    def piece_at(self, a, c):
        return pl.multiple_of(c * self.core_rows + a * self.piece_rows, self.piece_rows)

    def a_of(self, step):
        return lax.rem(self.a + step, self.a_count)

    def a_peer(self, step):
        return (self.w + 4 * (self.a_of(step) - self.a), self.n)

    def z_of(self, step):
        return lax.rem(self.n + step, self.narrow)

    def z_peer(self, step):
        return (self.w, self.z_of(step))

    def greet(self):
        barrier = pltpu.get_barrier_semaphore()
        peers = [self.other_core, self.b_peer]
        peers += [self.a_peer(i) for i in range(1, self.a_count)]
        peers += [self.z_peer(i) for i in range(1, self.narrow)]
        for peer in peers:
            pl.semaphore_signal(barrier, inc=1, device_id=peer, device_id_type=MESH)
        pl.semaphore_wait(barrier, len(peers))


def remote(src, dst, send, recv, peer):
    return pltpu.make_async_remote_copy(
        src_ref=src, dst_ref=dst, send_sem=send, recv_sem=recv, device_id=peer, device_id_type=MESH
    )


class Gather:
    def __init__(self, geo, own, ring, send, recv):
        self.geo, self.own, self.ring, self.send, self.recv = geo, own, ring, send, recv
        self.open = []

    @staticmethod
    def sems(geo):
        return 2 * (geo.narrow - 1) + 2 * geo.a_count + 1

    def copy(self, u, slot, src, dst, peer):
        return remote(src, dst, self.send.at[u, slot], self.recv.at[u, slot], peer)

    def z_copies(self, u):
        g = self.geo
        rows = pl.ds(g.mine, g.piece_rows)
        out = []
        for k in range(1, g.narrow):
            for h in range(2):
                cols = pl.ds(pl.multiple_of(h * g.half + g.b_at, g.quarter), g.quarter)
                out.append(
                    self.copy(
                        u,
                        2 * (k - 1) + h,
                        self.own.at[u, rows, cols],
                        self.ring.at[u, g.narrow - k - 1, rows, cols],
                        g.z_peer(k),
                    )
                )
        return out

    def p1_copies(self, u):
        g = self.geo
        base = 2 * (g.narrow - 1)
        rows = pl.ds(g.mine, g.piece_rows)
        low = self.ring.at[u, :, rows, pl.ds(g.b_at, g.quarter)]
        high = self.ring.at[u, :, rows, pl.ds(pl.multiple_of(g.half + g.b_at, g.quarter), g.quarter)]
        out = [self.copy(u, base + i - 1, low, low, g.a_peer(i)) for i in range(1, g.a_count)]
        return out + [self.copy(u, base + g.a_count - 1, high, high, g.b_peer)]

    def p2_copies(self, u):
        g = self.geo
        base = 2 * (g.narrow - 1) + g.a_count
        low = self.ring.at[u, :, pl.ds(g.core_at, g.core_rows), pl.ds(g.b_at, g.quarter)]
        high = self.ring.at[u, :, pl.ds(g.mine, g.piece_rows), pl.ds(g.half, g.half)]
        out = [self.copy(u, base + i - 1, high, high, g.a_peer(i)) for i in range(1, g.a_count)]
        return out + [self.copy(u, base + g.a_count - 1, low, low, g.b_peer)]

    def c_copies(self, u):
        g = self.geo
        base = 2 * (g.narrow - 1) + 2 * g.a_count
        part = self.ring.at[u, :, pl.ds(g.core_at, g.core_rows), :]
        return [self.copy(u, base, part, part, g.other_core)]

    def begin(self, copies):
        for copy in copies:
            copy.start()
            self.open.append(copy)

    def event(self, kind, u):
        if kind == 0:
            self.begin(self.z_copies(u))
        elif kind == 1:
            for copy in self.z_copies(u):
                copy.wait_recv()
            self.begin(self.p1_copies(u))
        elif kind == 2:
            for copy in self.p1_copies(u):
                copy.wait_recv()
            self.begin(self.p2_copies(u))
        elif kind == 3:
            for copy in self.p2_copies(u):
                copy.wait_recv()
            self.begin(self.c_copies(u))
        else:
            for copy in self.c_copies(u):
                copy.wait_recv()

    def finish(self):
        for copy in self.open:
            copy.wait_send()


def add_rows(dst, parts, tile):
    count, rows = dst.shape[0], dst.shape[1]
    tile = min(tile, rows)
    per = rows // tile

    def body(i, carry):
        k, r = i // per, pl.multiple_of(lax.rem(i, per) * tile, tile)
        total = parts[0](k, r, tile).astype(F32)
        for part in parts[1:]:
            total = total + part(k, r, tile).astype(F32)
        dst[k, pl.ds(r, tile), :] = total.astype(dst.dtype)
        return carry

    lax.fori_loop(0, count * per, body, 0)


class Reduce:
    slots = 3
    gslots = 3

    def __init__(self, geo, bufs):
        self.geo = geo
        (
            self.gbuf, self.rc, self.s1, self.p1a, self.p1b, self.s2a, self.s2b, self.p2a, self.p2b,
            self.s3, self.zr, self.out, self.send, self.recv, self.credit,
        ) = bufs
        self.order = {}
        self.open = {}
        self.units = self.out.shape[0]

    @classmethod
    def scratch(cls, geo, units):
        g, n, w = geo, geo.narrow, geo.width
        peers = max(g.a_count - 1, 1)
        count = 1 + 4 * g.a_count + (n - 1) + 1
        return [
            pltpu.VMEM((cls.gslots, n, g.rows, w), BF16),
            pltpu.VMEM((cls.slots, n, g.core_rows, w), BF16),
            pltpu.VMEM((cls.slots, n, g.core_rows, w), BF16),
            pltpu.VMEM((units, peers, n, g.piece_rows, g.half), BF16),
            pltpu.VMEM((units, n, g.core_rows, g.quarter), BF16),
            pltpu.VMEM((cls.slots, n, g.piece_rows, g.half), BF16),
            pltpu.VMEM((cls.slots, n, g.core_rows, g.quarter), BF16),
            pltpu.VMEM((units, n, g.piece_rows, g.quarter), BF16),
            pltpu.VMEM((units, peers, n, g.piece_rows, g.quarter), BF16),
            pltpu.VMEM((cls.slots, n, g.piece_rows, g.half), BF16),
            pltpu.VMEM((units, n - 1, g.piece_rows, g.half), BF16),
        ], [
            pltpu.SemaphoreType.DMA((units, count)),
            pltpu.SemaphoreType.DMA((units, count)),
            pltpu.SemaphoreType.REGULAR,
        ]

    def copy(self, u, slot, src, dst, peer):
        return remote(src, dst, self.send.at[u, slot], self.recv.at[u, slot], peer)

    def copies(self, kind, u):
        g = self.geo
        q = self.order[u]
        slot, gslot = q % self.slots, q % self.gslots
        na = g.a_count
        steps = range(1, na)
        low_b = pl.ds(g.b_at, g.quarter)
        peer_b = pl.multiple_of((1 - g.b) * g.quarter, g.quarter)
        mine = pl.ds(g.mine, g.piece_rows)
        core = pl.ds(g.core_at, g.core_rows)

        def in_core(a):
            return pl.ds(pl.multiple_of(a * g.piece_rows, g.piece_rows), g.piece_rows)

        if kind == 0:
            other = pl.ds(pl.multiple_of((1 - g.c) * g.core_rows, g.core_rows), g.core_rows)
            return [self.copy(u, 0, self.gbuf.at[gslot, :, other, :], self.rc.at[slot], g.other_core)]
        if kind == 1:
            out = [
                self.copy(
                    u, i, self.s1.at[slot, :, in_core(g.a_of(i)), pl.ds(0, g.half)],
                    self.p1a.at[u, na - i - 1], g.a_peer(i),
                )
                for i in steps
            ]
            cols = pl.ds(pl.multiple_of(g.half + peer_b, g.quarter), g.quarter)
            return out + [self.copy(u, na, self.s1.at[slot, :, :, cols], self.p1b.at[u], g.b_peer)]
        if kind == 2:
            out = [
                self.copy(
                    u, na + i, self.s2b.at[slot, :, in_core(g.a_of(i)), :],
                    self.p2b.at[u, na - i - 1], g.a_peer(i),
                )
                for i in steps
            ]
            cols = pl.ds(peer_b, g.quarter)
            return out + [self.copy(u, 2 * na, self.s2a.at[slot, :, :, cols], self.p2a.at[u], g.b_peer)]
        if kind == 3:
            return [
                self.copy(
                    u, 2 * na + k, self.s3.at[slot, g.z_of(k)], self.zr.at[u, g.narrow - k - 1], g.z_peer(k)
                )
                for k in range(1, g.narrow)
            ]
        base = 2 * na + g.narrow
        if kind == 4:
            low = self.out.at[u, mine, low_b]
            high = self.out.at[u, mine, pl.ds(pl.multiple_of(g.half + g.b_at, g.quarter), g.quarter)]
            out = [self.copy(u, base + i - 1, low, low, g.a_peer(i)) for i in steps]
            return out + [self.copy(u, base + na - 1, high, high, g.b_peer)]
        base += na
        if kind == 5:
            low = self.out.at[u, core, low_b]
            high = self.out.at[u, mine, pl.ds(g.half, g.half)]
            out = [self.copy(u, base + i - 1, high, high, g.a_peer(i)) for i in steps]
            return out + [self.copy(u, base + na - 1, low, low, g.b_peer)]
        base += na
        part = self.out.at[u, core, :]
        return [self.copy(u, base, part, part, g.other_core)]

    def begin(self, kind, u):
        copies = self.copies(kind, u)
        for copy in copies:
            copy.start()
        self.open[kind, u] = copies

    def arrived(self, kind, u):
        for copy in self.copies(kind, u):
            copy.wait_recv()

    def sent(self, kind, q):
        for (k, u), copies in list(self.open.items()):
            if k == kind and self.order[u] == q:
                for copy in copies:
                    copy.wait_send()
                del self.open[k, u]

    def slot_for(self, u):
        q = len(self.order)
        self.order[u] = q
        self.sent(0, q - self.gslots)
        return q % self.gslots

    def event(self, kind, u):
        g = self.geo
        q = self.order[u]
        slot, gslot = q % self.slots, q % self.gslots
        na = g.a_count
        if kind == 0:
            if q >= self.slots:
                pl.semaphore_wait(self.credit, 1)
            self.begin(0, u)
            return
        self.arrived(kind - 1, u)
        self.sent(kind, q - self.slots)
        if kind == 1:
            add_rows(
                self.s1.at[slot],
                [
                    lambda k, r, t: self.gbuf[gslot, k, pl.ds(pl.multiple_of(g.core_at + r, 16), t), :],
                    lambda k, r, t: self.rc[slot, k, pl.ds(r, t), :],
                ],
                32,
            )
            if q + self.slots < self.units:
                pl.semaphore_signal(self.credit, inc=1, device_id=g.other_core, device_id_type=MESH)
        elif kind == 2:
            own = g.a * g.piece_rows
            add_rows(
                self.s2a.at[slot],
                [lambda k, r, t: self.s1[slot, k, pl.ds(pl.multiple_of(own + r, 16), t), pl.ds(0, g.half)]]
                + [lambda k, r, t, i=i: self.p1a[u, i, k, pl.ds(r, t), :] for i in range(na - 1)],
                32,
            )
            cols = pl.ds(pl.multiple_of(g.half + g.b_at, g.quarter), g.quarter)
            add_rows(
                self.s2b.at[slot],
                [
                    lambda k, r, t: self.s1[slot, k, pl.ds(r, t), cols],
                    lambda k, r, t: self.p1b[u, k, pl.ds(r, t), :],
                ],
                64,
            )
        elif kind == 3:
            own = g.a * g.piece_rows
            cols = pl.ds(g.b_at, g.quarter)
            add_rows(
                self.s3.at[slot, :, :, pl.ds(0, g.quarter)],
                [
                    lambda k, r, t: self.s2a[slot, k, pl.ds(r, t), cols],
                    lambda k, r, t: self.p2a[u, k, pl.ds(r, t), :],
                ],
                64,
            )
            add_rows(
                self.s3.at[slot, :, :, pl.ds(g.quarter, g.quarter)],
                [lambda k, r, t: self.s2b[slot, k, pl.ds(pl.multiple_of(own + r, 16), t), :]]
                + [lambda k, r, t, i=i: self.p2b[u, i, k, pl.ds(r, t), :] for i in range(na - 1)],
                64,
            )
        elif kind == 4:
            total = self.s3[slot, g.n].astype(F32)
            for k in range(g.narrow - 1):
                total = total + self.zr[u, k].astype(F32)
            total = total.astype(BF16)
            mine = pl.ds(g.mine, g.piece_rows)
            self.out[u, mine, pl.ds(g.b_at, g.quarter)] = total[:, : g.quarter]
            cols = pl.ds(pl.multiple_of(g.half + g.b_at, g.quarter), g.quarter)
            self.out[u, mine, cols] = total[:, g.quarter :]
        if kind < 7:
            self.begin(kind, u)

    def finish(self):
        for copies in self.open.values():
            for copy in copies:
                copy.wait_send()
        self.open = {}


def pack_weights(geo, attn_in, attn_out, mlp_in, mlp_out):
    n, rows, width = geo.narrow, geo.rows, geo.width
    up = mlp_in.reshape(rows, n, -1, rows).transpose(2, 0, 1, 3).reshape(-1, rows, width)
    down = mlp_out.reshape(-1, rows, width)
    return jnp.concatenate([attn_in, attn_out, up, down], axis=0)


def unpack_grads(geo, total, attn_in, attn_out):
    n, rows, width = geo.narrow, geo.rows, geo.width
    total = total.astype(F32)
    i, o = attn_in.shape[0], attn_out.shape[0]
    ups = (total.shape[0] - i - o) // 2
    up = total[i + o : i + o + ups].reshape(ups, rows, n, rows).transpose(1, 2, 0, 3)
    return (
        total[:i], total[i : i + o], up.reshape(rows, -1), total[i + o + ups :].reshape(-1, width),
    )


def gather_weights(geo, own):
    units, rows, width = own.shape
    n = geo.narrow
    count = Gather.sems(geo)

    def kernel(own_ref, ring_ref, send, recv):
        geo.place()
        geo.greet()
        gather = Gather(geo, own_ref, ring_ref, send, recv)
        gather.event(0, 0)
        for s in range(units + 4):
            if s + 1 < units:
                gather.event(0, s + 1)
            for kind in range(1, 5):
                u = s - kind + 1
                if 0 <= u < units:
                    gather.event(kind, u)
        gather.finish()

    return pl.pallas_call(
        kernel,
        out_shape=jax.ShapeDtypeStruct((units, n - 1, rows, width), BF16),
        in_specs=[pl.BlockSpec(memory_space=pltpu.HBM)],
        out_specs=pl.BlockSpec(memory_space=pltpu.HBM),
        scratch_shapes=[pltpu.SemaphoreType.DMA((units, count)), pltpu.SemaphoreType.DMA((units, count))],
        compiler_params=pltpu.CompilerParams(collective_id=0, has_side_effects=True),
    )(own)


def reduce_grads(geo, grads):
    units, n, rows, width = grads.shape
    vmem, sems = Reduce.scratch(geo, units)

    def kernel(grads_ref, out_ref, *bufs):
        load = bufs[-1]
        geo.place()
        geo.greet()
        red = Reduce(geo, list(bufs[: len(vmem)]) + [out_ref] + list(bufs[len(vmem) : -1]))
        for s in range(units + 7):
            if s < units:
                slot = red.slot_for(s)
                copy = pltpu.make_async_copy(grads_ref.at[s], red.gbuf.at[slot], load)
                copy.start()
                copy.wait()
            for kind in range(8):
                u = s - kind
                if 0 <= u < units:
                    red.event(kind, u)
        red.finish()

    return pl.pallas_call(
        kernel,
        out_shape=jax.ShapeDtypeStruct((units, rows, width), BF16),
        in_specs=[pl.BlockSpec(memory_space=pltpu.HBM)],
        out_specs=pl.BlockSpec(memory_space=pltpu.VMEM),
        scratch_shapes=vmem + sems + [pltpu.SemaphoreType.DMA],
        compiler_params=pltpu.CompilerParams(
            collective_id=1, has_side_effects=True, vmem_limit_bytes=58 * MIB
        ),
    )(grads)


HEADS = 16


norm_eps = 1e-05
masked_score = -1e30


def layer_norm(values, gain, shift):
    centered = values - jnp.mean(values, axis=-1, keepdims=True)
    variance = jnp.mean(centered * centered, axis=-1, keepdims=True)
    return centered * lax.rsqrt(variance + norm_eps) * gain + shift


def gelu_exact(values):
    return jax.nn.gelu(values, approximate=False)


def matmul(left, right):
    return jnp.dot(left, right, preferred_element_type=jnp.float32)


def left_grad(left, right):
    return jnp.einsum("ra,rb->ab", left, right, preferred_element_type=jnp.float32)


def right_grad(grad, weight):
    return jnp.einsum("rb,ab->ra", grad, weight, preferred_element_type=jnp.float32)


def split_heads(values, heads):
    return values.reshape(values.shape[0], heads, values.shape[1] // heads)


def self_mask(segments):

    def allowed(start, block):
        query_pos = start + lax.iota(jnp.int32, block)
        key_pos = lax.iota(jnp.int32, segments.shape[0])
        return (segments[:, None] == segments[None, :]) & (key_pos[None, :] <= query_pos[:, None])

    return allowed


def cross_mask(token_image, key_image):

    def allowed(start, block):
        return token_image[:, None] == key_image[None, :]

    return allowed


def attention_forward(queries, keys_all, values_all, allowed, block):

    def one_block(block_index):
        start = block_index * block
        scores = jnp.einsum("qhe,khe->hqk", queries, keys_all, preferred_element_type=jnp.float32)
        scores = jnp.where(allowed(start, block)[None], scores, masked_score)
        top = jnp.max(scores, axis=-1, keepdims=True)
        expo = jnp.exp(scores - top)
        total = jnp.sum(expo, axis=-1, keepdims=True)
        probs = (expo / total).astype(jnp.bfloat16)
        mixed = jnp.einsum("hqk,khe->qhe", probs, values_all, preferred_element_type=jnp.float32)
        return (mixed.astype(jnp.bfloat16), (top + jnp.log(total))[..., 0])

    count = queries.shape[0] // block
    mixed, log_total = lax.map(one_block, lax.iota(jnp.int32, count))
    return (mixed.reshape(queries.shape), log_total)


def attention_backward(queries, keys_all, values_all, grad_mixed, log_total, allowed, block):

    def one_block(carry, block_index):
        acc_keys, acc_values = carry
        start = block_index * block
        scores = jnp.einsum("qhe,khe->hqk", queries, keys_all, preferred_element_type=jnp.float32)
        scores = jnp.where(allowed(start, block)[None], scores, masked_score)
        probs = jnp.exp(scores - log_total[block_index][..., None])
        acc_values = acc_values + jnp.einsum(
            "hqk,qhe->khe",
            probs.astype(jnp.bfloat16),
            grad_mixed,
            preferred_element_type=jnp.float32,
        )
        grad_probs = jnp.einsum(
            "qhe,khe->hqk", grad_mixed, values_all, preferred_element_type=jnp.float32
        )
        inner = jnp.sum(probs * grad_probs, axis=-1, keepdims=True)
        grad_scores = (probs * (grad_probs - inner)).astype(jnp.bfloat16)
        grad_query = jnp.einsum(
            "hqk,khe->qhe", grad_scores, keys_all, preferred_element_type=jnp.float32
        )
        acc_keys = acc_keys + jnp.einsum(
            "hqk,qhe->khe", grad_scores, queries, preferred_element_type=jnp.float32
        )
        return ((acc_keys, acc_values), grad_query.astype(jnp.bfloat16))

    count = queries.shape[0] // block
    zeros = jnp.zeros(keys_all.shape, jnp.float32)
    (acc_keys, acc_values), grad_query = lax.scan(
        one_block, (zeros, zeros), lax.iota(jnp.int32, count)
    )
    return (
        grad_query.reshape(queries.shape),
        acc_keys.astype(jnp.bfloat16),
        acc_values.astype(jnp.bfloat16),
    )


def per_device(
    mesh,
    hidden_in,
    memory,
    segment_ids,
    image_ids,
    attn_in,
    attn_out,
    mlp_in,
    mlp_out,
    gains,
    shifts,
    mlp_bias,
    cotangent,
):
    geo = Geometry(mesh, hidden_in.shape[2])
    own = pack_weights(geo, attn_in, attn_out, mlp_in, mlp_out)
    ring = gather_weights(geo, own)
    place = lax.axis_index("narrow")
    full = jnp.concatenate([own[:, None], ring], axis=1)
    full = jnp.take(full, lax.rem(jnp.arange(geo.narrow) - place + geo.narrow, geo.narrow), axis=1)
    full = full.reshape(full.shape[0], geo.width, geo.width)
    n_in, n_out = attn_in.shape[0], attn_out.shape[0]
    n_up = (full.shape[0] - n_in - n_out) // 2
    w_in, w_out = full[:n_in], full[n_in : n_in + n_out]
    w_up = full[n_in + n_out : n_in + n_out + n_up].transpose(1, 0, 2).reshape(geo.width, -1)
    w_down = full[n_in + n_out + n_up :].reshape(-1, geo.width)
    gain_all = lax.all_gather(gains, "narrow", axis=1, tiled=True).astype(jnp.float32)
    shift_all = lax.all_gather(shifts, "narrow", axis=1, tiled=True).astype(jnp.float32)
    up_bias = lax.all_gather(mlp_bias.reshape(n_up, -1), "narrow", axis=1, tiled=True).reshape(-1).astype(jnp.float32)
    tokens = hidden_in[0].astype(jnp.float32)
    rows, width = tokens.shape
    heads = HEADS
    scale = (width // heads) ** (-0.5)
    block = min(512, rows)
    segments = segment_ids[0]
    seg_count = image_ids.shape[1]
    token_image = jnp.sum(
        jnp.where(
            segments[:, None] == lax.iota(jnp.int32, seg_count)[None, :], image_ids[0][None, :], 0
        ),
        axis=1,
    )
    mem_flat = memory[0].reshape(-1, width)
    key_image = lax.iota(jnp.int32, mem_flat.shape[0]) // memory.shape[2]
    mask_self = self_mask(segments)
    mask_cross = cross_mask(token_image, key_image)
    normed_one = layer_norm(tokens, gain_all[0], shift_all[6]).astype(jnp.bfloat16)
    self_query = ((matmul(normed_one, w_in[0]) + shift_all[0]) * scale).astype(jnp.bfloat16)
    self_keys = matmul(normed_one, w_in[1]).astype(jnp.bfloat16)
    self_values = (matmul(normed_one, w_in[2]) + shift_all[1]).astype(jnp.bfloat16)
    self_mix, self_total = attention_forward(
        split_heads(self_query, heads),
        split_heads(self_keys, heads),
        split_heads(self_values, heads),
        mask_self,
        block,
    )
    self_mix = self_mix.reshape(rows, width)
    after_self = tokens + matmul(self_mix, w_out[0]) + shift_all[2]
    normed_two = layer_norm(after_self, gain_all[1], shift_all[7]).astype(jnp.bfloat16)
    cross_query = ((matmul(normed_two, w_in[3]) + shift_all[3]) * scale).astype(jnp.bfloat16)
    cross_keys = matmul(mem_flat, w_in[4]).astype(jnp.bfloat16)
    cross_values = (matmul(mem_flat, w_in[5]) + shift_all[4]).astype(jnp.bfloat16)
    cross_mix, cross_total = attention_forward(
        split_heads(cross_query, heads),
        split_heads(cross_keys, heads),
        split_heads(cross_values, heads),
        mask_cross,
        block,
    )
    cross_mix = cross_mix.reshape(rows, width)
    after_cross = after_self + matmul(cross_mix, w_out[1]) + shift_all[5]
    normed_three = layer_norm(after_cross, gain_all[2], shift_all[8]).astype(jnp.bfloat16)
    pre_act = matmul(normed_three, w_up) + up_bias
    activated = gelu_exact(pre_act).astype(jnp.bfloat16)
    result = after_cross + matmul(activated, w_down) + shift_all[9]
    grad_result = cotangent[0].astype(jnp.float32)
    grad_shift9 = jnp.sum(grad_result, axis=0)
    grad_low = grad_result.astype(jnp.bfloat16)
    grad_down = left_grad(activated, grad_low)
    grad_act = right_grad(grad_low, w_down)
    grad_pre = jax.vjp(gelu_exact, pre_act)[1](grad_act)[0].astype(jnp.bfloat16)
    grad_up_bias = jnp.sum(grad_pre.astype(jnp.float32), axis=0)
    grad_up = left_grad(normed_three, grad_pre)
    grad_norm_three = right_grad(grad_pre, w_up)
    norm_pull = jax.vjp(layer_norm, after_cross, gain_all[2], shift_all[8])[1]
    grad_from_norm, grad_gain3, grad_shift8 = norm_pull(grad_norm_three)
    grad_cross_res = grad_result + grad_from_norm
    grad_shift5 = jnp.sum(grad_cross_res, axis=0)
    grad_branch = grad_cross_res.astype(jnp.bfloat16)
    grad_out_cross = left_grad(cross_mix, grad_branch)
    grad_cross_mix = right_grad(grad_branch, w_out[1]).astype(jnp.bfloat16)
    grad_cq, grad_ck, grad_cv = attention_backward(
        split_heads(cross_query, heads),
        split_heads(cross_keys, heads),
        split_heads(cross_values, heads),
        split_heads(grad_cross_mix, heads),
        cross_total,
        mask_cross,
        block,
    )
    grad_cq = (grad_cq.reshape(rows, width).astype(jnp.float32) * scale).astype(jnp.bfloat16)
    grad_ck = grad_ck.reshape(-1, width)
    grad_cv = grad_cv.reshape(-1, width)
    grad_in3 = left_grad(normed_two, grad_cq)
    grad_shift3 = jnp.sum(grad_cq.astype(jnp.float32), axis=0)
    grad_in4 = left_grad(mem_flat, grad_ck)
    grad_in5 = left_grad(mem_flat, grad_cv)
    grad_shift4 = jnp.sum(grad_cv.astype(jnp.float32), axis=0)
    grad_mem_flat = right_grad(grad_ck, w_in[4]) + right_grad(grad_cv, w_in[5])
    grad_norm_two = right_grad(grad_cq, w_in[3])
    norm_pull = jax.vjp(layer_norm, after_self, gain_all[1], shift_all[7])[1]
    grad_from_norm, grad_gain2, grad_shift7 = norm_pull(grad_norm_two)
    grad_self_res = grad_cross_res + grad_from_norm
    grad_shift2 = jnp.sum(grad_self_res, axis=0)
    grad_branch = grad_self_res.astype(jnp.bfloat16)
    grad_out_self = left_grad(self_mix, grad_branch)
    grad_self_mix = right_grad(grad_branch, w_out[0]).astype(jnp.bfloat16)
    grad_sq, grad_sk, grad_sv = attention_backward(
        split_heads(self_query, heads),
        split_heads(self_keys, heads),
        split_heads(self_values, heads),
        split_heads(grad_self_mix, heads),
        self_total,
        mask_self,
        block,
    )
    grad_sq = (grad_sq.reshape(rows, width).astype(jnp.float32) * scale).astype(jnp.bfloat16)
    grad_sk = grad_sk.reshape(rows, width)
    grad_sv = grad_sv.reshape(rows, width)
    grad_in0 = left_grad(normed_one, grad_sq)
    grad_shift0 = jnp.sum(grad_sq.astype(jnp.float32), axis=0)
    grad_in1 = left_grad(normed_one, grad_sk)
    grad_in2 = left_grad(normed_one, grad_sv)
    grad_shift1 = jnp.sum(grad_sv.astype(jnp.float32), axis=0)
    grad_norm_one = (
        right_grad(grad_sq, w_in[0]) + right_grad(grad_sk, w_in[1]) + right_grad(grad_sv, w_in[2])
    )
    norm_pull = jax.vjp(layer_norm, tokens, gain_all[0], shift_all[6])[1]
    grad_from_norm, grad_gain1, grad_shift6 = norm_pull(grad_norm_one)
    grad_tokens = grad_self_res + grad_from_norm
    grad_gains = jnp.stack([grad_gain1, grad_gain2, grad_gain3])
    grad_shifts = jnp.stack(
        [
            grad_shift0,
            grad_shift1,
            grad_shift2,
            grad_shift3,
            grad_shift4,
            grad_shift5,
            grad_shift6,
            grad_shift7,
            grad_shift8,
            grad_shift9,
        ]
    )
    blocks = [grad_in0, grad_in1, grad_in2, grad_in3, grad_in4, grad_in5, grad_out_self, grad_out_cross]
    width = geo.width
    blocks += [grad_up[:, j * width : (j + 1) * width] for j in range(n_up)]
    blocks += [grad_down[j * width : (j + 1) * width] for j in range(n_up)]
    grads = jnp.stack([g.astype(jnp.bfloat16) for g in blocks])
    grads = grads.reshape(len(blocks), geo.narrow, geo.rows, width)
    summed = reduce_grads(geo, grads)
    bias_parts = grad_up_bias.reshape(n_up, -1)
    owned = (
        lax.psum_scatter(grad_gains, "narrow", scatter_dimension=1, tiled=True),
        lax.psum_scatter(grad_shifts, "narrow", scatter_dimension=1, tiled=True),
        lax.psum_scatter(bias_parts, "narrow", scatter_dimension=1, tiled=True),
    )
    small = lax.psum(owned, "wide")
    totals = unpack_grads(geo, summed, attn_in, attn_out) + (small[0], small[1], small[2].reshape(-1))
    return (
        result.astype(jnp.bfloat16)[None],
        grad_tokens[None],
        grad_mem_flat.reshape(memory.shape),
        totals[0],
        totals[1],
        totals[2],
        totals[3],
        totals[4],
        totals[5],
        totals[6],
    )


def solution(mesh):
    return jax.shard_map(
        functools.partial(per_device, mesh),
        mesh=mesh,
        in_specs=(
            P(("wide", "narrow"), None, None),
            P(("wide", "narrow"), None, None, None),
            P(("wide", "narrow"), None),
            P(("wide", "narrow"), None),
            P(None, "narrow", None),
            P(None, "narrow", None),
            P("narrow", None),
            P("narrow", None),
            P(None, "narrow"),
            P(None, "narrow"),
            P("narrow"),
            P(("wide", "narrow"), None, None),
        ),
        out_specs=(
            P(("wide", "narrow"), None, None),
            P(("wide", "narrow"), None, None),
            P(("wide", "narrow"), None, None, None),
            P(None, "narrow", None),
            P(None, "narrow", None),
            P("narrow", None),
            P("narrow", None),
            P(None, "narrow"),
            P(None, "narrow"),
            P("narrow"),
        ),
        check_vma=False,
    )
```

```python
import functools

import jax
import jax.numpy as jnp
from jax import lax
from jax.experimental import pallas as pl
from jax.experimental.pallas import tpu as pltpu
from jax.sharding import PartitionSpec as P

HEADS = 16
MESH = pl.DeviceIdType.MESH
F32 = jnp.float32
BF16 = jnp.bfloat16
MIB = 1 << 20
EPS = 1e-5
MASKED = -1e30
SMALL = 24
ROOT_HALF = 0.7071067811865476
ROOT_TWO_PI = 0.3989422804014327
HBM = pl.BlockSpec(memory_space=pltpu.HBM)
VMEM = pl.BlockSpec(memory_space=pltpu.VMEM)
SMEM = pl.BlockSpec(memory_space=pltpu.SMEM)


class Geometry:
    def __init__(self, mesh, width, n_in, n_out, hidden):
        self.wide = mesh.shape["wide"]
        self.narrow = mesh.shape["narrow"]
        self.a_count = self.wide // 4
        self.width = width
        self.rows = width // self.narrow
        self.core_rows = self.rows // 2
        self.piece_rows = self.core_rows // self.a_count
        self.half = width // 2
        self.quarter = width // 4
        self.n_in, self.n_out, self.n_up = n_in, n_out, hidden // width
        self.up_at = n_in + n_out
        self.down_at = self.up_at + self.n_up
        self.units = self.down_at + self.n_up

    def place(self):
        w = lax.axis_index("wide")
        n = lax.axis_index("narrow")
        self.w, self.n = w, n
        self.a, self.b, self.c = w // 4, lax.rem(w // 2, 2), lax.rem(w, 2)
        self.core_at = pl.multiple_of(self.c * self.core_rows, self.core_rows)
        self.b_at = pl.multiple_of(self.b * self.quarter, self.quarter)
        self.mine = pl.multiple_of(self.c * self.core_rows + self.a * self.piece_rows, self.piece_rows)
        self.other_core = (w + 1 - 2 * self.c, n)
        self.b_peer = (w + 2 - 4 * self.b, n)

    def a_of(self, step):
        return lax.rem(self.a + step, self.a_count)

    def a_peer(self, step):
        return (self.w + 4 * (self.a_of(step) - self.a), self.n)

    def z_of(self, step):
        return lax.rem(self.n + step, self.narrow)

    def z_peer(self, step):
        return (self.w, self.z_of(step))

    def greet(self):
        barrier = pltpu.get_barrier_semaphore()
        peers = [self.other_core, self.b_peer]
        peers += [self.a_peer(i) for i in range(1, self.a_count)]
        peers += [self.z_peer(i) for i in range(1, self.narrow)]
        for peer in peers:
            pl.semaphore_signal(barrier, inc=1, device_id=peer, device_id_type=MESH)
        pl.semaphore_wait(barrier, len(peers))


def remote(src, dst, send, recv, peer):
    return pltpu.make_async_remote_copy(
        src_ref=src, dst_ref=dst, send_sem=send, recv_sem=recv, device_id=peer, device_id_type=MESH
    )


class Shard:
    def __init__(self, geo, attn_in, attn_out, up, down):
        self.geo, self.attn_in, self.attn_out, self.up, self.down = geo, attn_in, attn_out, up, down

    def at(self, u, row=0, rows=None, cols=None):
        g = self.geo
        rows = rows or g.rows
        if cols is None:
            cols = pl.ds(0, g.width)
        if u < g.n_in:
            return self.attn_in.at[u, pl.ds(row, rows), cols]
        if u < g.up_at:
            return self.attn_out.at[u - g.n_in, pl.ds(row, rows), cols]
        if u < g.down_at:
            return self.up.at[u - g.up_at, pl.ds(row, rows), cols]
        start = (u - g.down_at) * g.rows + row
        if not isinstance(start, int):
            start = pl.multiple_of(start, g.piece_rows)
        return self.down.at[pl.ds(start, rows), cols]


class Gather:
    def __init__(self, geo, shard, ring, send, recv):
        self.geo, self.shard, self.ring, self.send, self.recv = geo, shard, ring, send, recv
        self.open = []

    @staticmethod
    def sems(geo):
        return 2 * (geo.narrow - 1) + 2 * geo.a_count + 1

    def copies(self, kind, u):
        g = self.geo

        def copy(slot, src, dst, peer):
            return remote(src, dst, self.send.at[u, slot], self.recv.at[u, slot], peer)

        mine = pl.ds(g.mine, g.piece_rows)
        low_b = pl.ds(g.b_at, g.quarter)
        high_b = pl.ds(pl.multiple_of(g.half + g.b_at, g.quarter), g.quarter)
        core = pl.ds(g.core_at, g.core_rows)
        if kind == 0:
            out = []
            for k in range(1, g.narrow):
                for h, cols in enumerate((low_b, high_b)):
                    src = self.shard.at(u, g.mine, g.piece_rows, cols)
                    dst = self.ring.at[u, g.narrow - k - 1, mine, cols]
                    out.append(copy(2 * (k - 1) + h, src, dst, g.z_peer(k)))
            return out
        base = 2 * (g.narrow - 1)
        steps = range(1, g.a_count)
        if kind == 1:
            low = self.ring.at[u, :, mine, low_b]
            high = self.ring.at[u, :, mine, high_b]
            out = [copy(base + i - 1, low, low, g.a_peer(i)) for i in steps]
            return out + [copy(base + g.a_count - 1, high, high, g.b_peer)]
        base += g.a_count
        if kind == 2:
            low = self.ring.at[u, :, core, low_b]
            high = self.ring.at[u, :, mine, pl.ds(g.half, g.half)]
            out = [copy(base + i - 1, high, high, g.a_peer(i)) for i in steps]
            return out + [copy(base + g.a_count - 1, low, low, g.b_peer)]
        part = self.ring.at[u, :, core, :]
        return [copy(base + g.a_count, part, part, g.other_core)]

    def event(self, kind, u):
        if kind > 0:
            for copy in self.copies(kind - 1, u):
                copy.wait_recv()
        if kind < 4:
            for copy in self.copies(kind, u):
                copy.start()
            self.open.append((kind, u))

    def finish(self):
        for kind, u in self.open:
            for copy in self.copies(kind, u):
                copy.wait_send()


def add_rows(dst, parts, tile):
    count, rows = dst.shape[0], dst.shape[1]
    tile = min(tile, rows)
    per = rows // tile

    def body(i, carry):
        k, r = i // per, pl.multiple_of(lax.rem(i, per) * tile, tile)
        total = parts[0](k, r, tile).astype(F32)
        for part in parts[1:]:
            total = total + part(k, r, tile).astype(F32)
        dst[k, pl.ds(r, tile), :] = total.astype(dst.dtype)
        return carry

    lax.fori_loop(0, count * per, body, 0)


class Reduce:
    slots = 2
    depth = 8

    def __init__(self, geo, bufs, out, order):
        self.geo, self.out, self.order = geo, out, order
        (
            self.gbuf, self.rc, self.s1, self.p1a, self.p1b, self.s2a, self.s2b, self.p2a, self.p2b,
            self.s3, self.zr, self.fin, self.send, self.recv, self.local, self.credit,
        ) = bufs
        self.open = set()

    @classmethod
    def scratch(cls, geo):
        g, n, w, units = geo, geo.narrow, geo.width, geo.units
        peers = max(g.a_count - 1, 1)
        count = 1 + 4 * g.a_count + (n - 1) + 1
        return [
            pltpu.VMEM((cls.slots, n, g.rows, w), BF16),
            pltpu.VMEM((cls.slots, n, g.core_rows, w), BF16),
            pltpu.VMEM((cls.slots, n, g.core_rows, w), BF16),
            pltpu.VMEM((units, peers, n, g.piece_rows, g.half), BF16),
            pltpu.VMEM((units, n, g.core_rows, g.quarter), BF16),
            pltpu.VMEM((cls.slots, n, g.piece_rows, g.half), BF16),
            pltpu.VMEM((cls.slots, n, g.core_rows, g.quarter), BF16),
            pltpu.VMEM((units, n, g.piece_rows, g.quarter), BF16),
            pltpu.VMEM((units, peers, n, g.piece_rows, g.quarter), BF16),
            pltpu.VMEM((cls.slots, n, g.piece_rows, g.half), BF16),
            pltpu.VMEM((units, n - 1, g.piece_rows, g.half), BF16),
            pltpu.VMEM((cls.slots, g.piece_rows, g.half), BF16),
            pltpu.SemaphoreType.DMA((units, count)),
            pltpu.SemaphoreType.DMA((units, count)),
            pltpu.SemaphoreType.DMA((2,)),
            pltpu.SemaphoreType.REGULAR,
        ]

    def copies(self, kind, q):
        g = self.geo
        u, slot = self.order[q], q % self.slots
        na = g.a_count
        steps = range(1, na)
        mine = pl.ds(g.mine, g.piece_rows)
        core = pl.ds(g.core_at, g.core_rows)
        low_b = pl.ds(g.b_at, g.quarter)
        high_b = pl.ds(pl.multiple_of(g.half + g.b_at, g.quarter), g.quarter)
        peer_b = pl.multiple_of((1 - g.b) * g.quarter, g.quarter)

        def copy(s, src, dst, peer):
            return remote(src, dst, self.send.at[q, s], self.recv.at[q, s], peer)

        def in_core(a):
            return pl.ds(pl.multiple_of(a * g.piece_rows, g.piece_rows), g.piece_rows)

        if kind == 0:
            other = pl.ds(pl.multiple_of((1 - g.c) * g.core_rows, g.core_rows), g.core_rows)
            return [copy(0, self.gbuf.at[slot, :, other, :], self.rc.at[slot], g.other_core)]
        if kind == 1:
            s1 = self.s1
            out = [
                copy(i, s1.at[slot, :, in_core(g.a_of(i)), pl.ds(0, g.half)], self.p1a.at[q, na - i - 1], g.a_peer(i))
                for i in steps
            ]
            cols = pl.ds(pl.multiple_of(g.half + peer_b, g.quarter), g.quarter)
            return out + [copy(na, s1.at[slot, :, :, cols], self.p1b.at[q], g.b_peer)]
        if kind == 2:
            out = [
                copy(na + i, self.s2b.at[slot, :, in_core(g.a_of(i)), :], self.p2b.at[q, na - i - 1], g.a_peer(i))
                for i in steps
            ]
            return out + [copy(2 * na, self.s2a.at[slot, :, :, pl.ds(peer_b, g.quarter)], self.p2a.at[q], g.b_peer)]
        if kind == 3:
            return [
                copy(2 * na + k, self.s3.at[slot, g.z_of(k)], self.zr.at[q, g.narrow - k - 1], g.z_peer(k))
                for k in range(1, g.narrow)
            ]
        base = 2 * na + g.narrow
        if kind == 4:
            low, high = self.out.at[u, mine, low_b], self.out.at[u, mine, high_b]
            out = [copy(base + i - 1, low, low, g.a_peer(i)) for i in steps]
            return out + [copy(base + na - 1, high, high, g.b_peer)]
        base += na
        if kind == 5:
            low, high = self.out.at[u, core, low_b], self.out.at[u, mine, pl.ds(g.half, g.half)]
            out = [copy(base + i - 1, high, high, g.a_peer(i)) for i in steps]
            return out + [copy(base + na - 1, low, low, g.b_peer)]
        part = self.out.at[u, core, :]
        return [copy(base + na, part, part, g.other_core)]

    def begin(self, kind, q):
        for copy in self.copies(kind, q):
            copy.start()
        self.open.add((kind, q))

    def arrived(self, kind, q):
        for copy in self.copies(kind, q):
            copy.wait_recv()

    def sent(self, kind, q):
        if (kind, q) in self.open:
            for copy in self.copies(kind, q):
                copy.wait_send()
            self.open.remove((kind, q))

    def event(self, kind, q):
        g = self.geo
        slot = q % self.slots
        na = g.a_count
        if kind == 0:
            if q >= self.slots:
                pl.semaphore_wait(self.credit, 1)
            self.begin(0, q)
            return
        self.arrived(kind - 1, q)
        self.sent(kind, q - self.slots)
        own = pl.multiple_of(g.a * g.piece_rows, g.piece_rows)
        low_b = pl.ds(g.b_at, g.quarter)
        high_b = pl.ds(pl.multiple_of(g.half + g.b_at, g.quarter), g.quarter)
        if kind == 1:
            add_rows(
                self.s1.at[slot],
                [
                    lambda k, r, t: self.gbuf[slot, k, pl.ds(pl.multiple_of(g.core_at + r, 16), t), :],
                    lambda k, r, t: self.rc[slot, k, pl.ds(r, t), :],
                ],
                32,
            )
            if q + self.slots < g.units:
                pl.semaphore_signal(self.credit, inc=1, device_id=g.other_core, device_id_type=MESH)
        elif kind == 2:
            add_rows(
                self.s2a.at[slot],
                [lambda k, r, t: self.s1[slot, k, pl.ds(pl.multiple_of(own + r, 16), t), pl.ds(0, g.half)]]
                + [lambda k, r, t, i=i: self.p1a[q, i, k, pl.ds(r, t), :] for i in range(na - 1)],
                64,
            )
            add_rows(
                self.s2b.at[slot],
                [
                    lambda k, r, t: self.s1[slot, k, pl.ds(r, t), high_b],
                    lambda k, r, t: self.p1b[q, k, pl.ds(r, t), :],
                ],
                128,
            )
        elif kind == 3:
            add_rows(
                self.s3.at[slot, :, :, pl.ds(0, g.quarter)],
                [
                    lambda k, r, t: self.s2a[slot, k, pl.ds(r, t), low_b],
                    lambda k, r, t: self.p2a[q, k, pl.ds(r, t), :],
                ],
                64,
            )
            add_rows(
                self.s3.at[slot, :, :, pl.ds(g.quarter, g.quarter)],
                [lambda k, r, t: self.s2b[slot, k, pl.ds(pl.multiple_of(own + r, 16), t), :]]
                + [lambda k, r, t, i=i: self.p2b[q, i, k, pl.ds(r, t), :] for i in range(na - 1)],
                64,
            )
        elif kind == 4:
            total = self.s3[slot, g.n].astype(F32)
            for k in range(g.narrow - 1):
                total = total + self.zr[q, k].astype(F32)
            self.fin[slot] = total.astype(BF16)
            mine = pl.ds(g.mine, g.piece_rows)
            u = self.order[q]
            stores = [
                pltpu.make_async_copy(
                    self.fin.at[slot, :, pl.ds(h * g.quarter, g.quarter)], self.out.at[u, mine, cols], self.local.at[h]
                )
                for h, cols in enumerate((low_b, high_b))
            ]
            for store in stores:
                store.start()
            for store in stores:
                store.wait()
        if kind < 7:
            self.begin(kind, q)

    def finish(self):
        for kind, q in sorted(self.open):
            for copy in self.copies(kind, q):
                copy.wait_send()
        self.open = set()


class Weights:
    def __init__(self, geo, shard, ring, buf, sem):
        self.geo, self.shard, self.ring, self.buf, self.sem = geo, shard, ring, buf, sem

    def copies(self, u, slot):
        g = self.geo
        out = []
        for k in range(g.narrow):
            src = self.shard.at(u) if k == 0 else self.ring.at[u, k - 1]
            rows = pl.ds(pl.multiple_of(g.z_of(k) * g.rows, g.rows), g.rows)
            out.append(pltpu.make_async_copy(src, self.buf.at[slot, rows, :], self.sem.at[slot, k]))
        return out

    def start(self, u, slot):
        for copy in self.copies(u, slot):
            copy.start()

    def wait(self, u, slot):
        for copy in self.copies(u, slot):
            copy.wait()
        return self.buf.at[slot]


def dot_nn(left, right):
    return jnp.dot(left, right, preferred_element_type=F32)


def dot_nt(left, right):
    return lax.dot_general(left, right, (((1,), (1,)), ((), ())), preferred_element_type=F32)


def dot_tn(left, right):
    return lax.dot_general(left, right, (((0,), (0,)), ((), ())), preferred_element_type=F32)


def over(count, body):
    def step(i, carry):
        body(i)
        return carry

    lax.fori_loop(0, count, step, 0)


def tiles(total, tile, body):
    over(total // tile, lambda i: body(pl.ds(pl.multiple_of(i * tile, tile), tile)))


def normalized(x):
    centered = x - jnp.mean(x, axis=-1, keepdims=True)
    variance = jnp.mean(centered * centered, axis=-1, keepdims=True)
    scale = lax.rsqrt(variance + EPS)
    return centered * scale, scale


def pair_cols(i):
    return pl.ds(pl.multiple_of(i * 128, 128), 128)


def lane_half(rows):
    return lax.broadcasted_iota(jnp.int32, (rows, 128), 1) // 64


def keep_half(values, side, half):
    return jnp.where(side == half, values, jnp.zeros_like(values))


def put_lane(ref, rows, lane, column):
    lanes = lax.broadcasted_iota(jnp.int32, (column.shape[0], 128), 1)
    ref[rows, :] = jnp.where(lanes == lane, column, ref[rows, :])


def take_lane(ref, rows, lane):
    values = ref[rows, :]
    lanes = lax.broadcasted_iota(jnp.int32, values.shape, 1)
    return jnp.sum(jnp.where(lanes == lane, values, 0.0), axis=-1, keepdims=True)


def softmax(scores):
    top = jnp.max(scores, axis=-1, keepdims=True)
    expo = jnp.exp(scores - top)
    total = jnp.sum(expo, axis=-1, keepdims=True)
    return (expo * (1.0 / total)).astype(BF16), top + jnp.log(total)


def fill_self_bias(bias, seg_col, seg_row):
    tokens = bias.shape[0]

    def body(rows):
        count = rows.size
        query = rows.start + lax.broadcasted_iota(jnp.int32, (count, tokens), 0)
        key = lax.broadcasted_iota(jnp.int32, (count, tokens), 1)
        allowed = (seg_col[rows, :] == seg_row[...]) & (key <= query)
        bias[rows, :] = jnp.where(allowed, 0.0, MASKED)

    tiles(tokens, 128, body)


def second_image(seg_col, images, rows):
    pages = seg_col[rows, :]
    image = jnp.zeros_like(pages)
    for page in range(images.shape[1]):
        image = jnp.where(pages == page, images[0, page], image)
    return image


def self_forward(i, q, k, v, bias, o, lse):
    cols = pair_cols(i)
    tokens = q.shape[0]
    block = tokens // 2
    side = lane_half(block)
    for at in range(0, tokens, block):
        rows, keys = pl.ds(at, block), pl.ds(0, at + block)
        queries, key, value = q[rows, cols], k[keys, cols], v[keys, cols]
        mixed = []
        for half in range(2):
            scores = dot_nt(keep_half(queries, side, half), key) + bias[rows, keys]
            probs, total = softmax(scores)
            put_lane(lse, rows, 2 * i + half, total)
            mixed.append(dot_nn(probs, value))
        o[rows, cols] = jnp.where(side == 0, mixed[0], mixed[1]).astype(BF16)


def self_backward(i, q, k, v, do, o, bias, lse):
    cols = pair_cols(i)
    tokens = q.shape[0]
    block = tokens // 2
    side = lane_half(block)
    grads_k, grads_v, grads_q = [], [], []
    for at in range(0, tokens, block):
        rows, keys = pl.ds(at, block), pl.ds(0, at + block)
        queries, key, value, grad, mix = q[rows, cols], k[keys, cols], v[keys, cols], do[rows, cols], o[rows, cols]
        product = grad.astype(F32) * mix.astype(F32)
        parts, grad_k, grad_v = [], 0.0, 0.0
        for half in range(2):
            own_q, own_g = keep_half(queries, side, half), keep_half(grad, side, half)
            scores = dot_nt(own_q, key) + bias[rows, keys]
            probs = jnp.exp(scores - take_lane(lse, rows, 2 * i + half))
            inner = jnp.sum(keep_half(product, side, half), axis=-1, keepdims=True)
            slopes = (probs * (dot_nt(own_g, value) - inner)).astype(BF16)
            parts.append(dot_nn(slopes, key))
            grad_k = grad_k + dot_tn(slopes, own_q)
            grad_v = grad_v + dot_tn(probs.astype(BF16), own_g)
        grads_q.append((rows, jnp.where(side == 0, parts[0], parts[1])))
        grads_k.append(grad_k)
        grads_v.append(grad_v)
    low = pl.ds(0, block)
    high = pl.ds(block, block)
    k[low, cols] = (grads_k[0] + grads_k[1][:block]).astype(BF16)
    k[high, cols] = grads_k[1][block:].astype(BF16)
    v[low, cols] = (grads_v[0] + grads_v[1][:block]).astype(BF16)
    v[high, cols] = grads_v[1][block:].astype(BF16)
    for rows, grad in grads_q:
        q[rows, cols] = grad.astype(BF16)


def both_images(ref, cols):
    keys = ref.shape[0] // 2
    return jnp.concatenate([ref[pl.ds(0, keys), cols], ref[pl.ds(keys, keys), cols]], axis=1)


def by_image(values, second):
    zero = jnp.zeros_like(values)
    return jnp.concatenate([jnp.where(second, zero, values), jnp.where(second, values, zero)], axis=1)


def pick_image(values, second):
    return jnp.where(second, values[:, 128:], values[:, :128])


def cross_forward(i, q, k, v, second_at, key_bias, o, lse, block=256):
    cols = pair_cols(i)
    key, value = both_images(k, cols), both_images(v, cols)
    side = lane_half(block)
    for at in range(0, q.shape[0], block):
        rows = pl.ds(at, block)
        queries = q[rows, cols]
        second = second_at[rows, :] == 1
        mixed = []
        for half in range(2):
            scores = dot_nt(by_image(keep_half(queries, side, half), second), key) + key_bias
            probs, total = softmax(scores)
            put_lane(lse, rows, 2 * i + half, total)
            mixed.append(pick_image(dot_nn(probs, value), second))
        o[rows, cols] = jnp.where(side == 0, mixed[0], mixed[1]).astype(BF16)


def cross_backward(i, q, k, v, do, o, second_at, key_bias, lse, block=256):
    cols = pair_cols(i)
    key, value = both_images(k, cols), both_images(v, cols)
    side = lane_half(block)
    grad_k, grad_v, grads_q = 0.0, 0.0, []
    for at in range(0, q.shape[0], block):
        rows = pl.ds(at, block)
        queries, grad, mix = q[rows, cols], do[rows, cols], o[rows, cols]
        second = second_at[rows, :] == 1
        product = grad.astype(F32) * mix.astype(F32)
        parts = []
        for half in range(2):
            own_q = by_image(keep_half(queries, side, half), second)
            own_g = by_image(keep_half(grad, side, half), second)
            scores = dot_nt(own_q, key) + key_bias
            probs = jnp.exp(scores - take_lane(lse, rows, 2 * i + half))
            inner = jnp.sum(keep_half(product, side, half), axis=-1, keepdims=True)
            slopes = (probs * (dot_nt(own_g, value) - inner)).astype(BF16)
            parts.append(pick_image(dot_nn(slopes, key), second))
            grad_k = grad_k + dot_tn(slopes, own_q)
            grad_v = grad_v + dot_tn(probs.astype(BF16), own_g)
        grads_q.append((rows, jnp.where(side == 0, parts[0], parts[1])))
    keys = k.shape[0] // 2
    for ref, total in ((k, grad_k), (v, grad_v)):
        ref[pl.ds(0, keys), cols] = total[:, :128].astype(BF16)
        ref[pl.ds(keys, keys), cols] = total[:, 128:].astype(BF16)
    for rows, grad in grads_q:
        q[rows, cols] = grad.astype(BF16)


class Saver:
    def __init__(self, sems):
        self.sems, self.open, self.used = sems, {}, 0

    def save(self, src, dst):
        at = self.used
        self.used += 1
        pltpu.make_async_copy(src, dst, self.sems.at[at]).start()
        self.open[at] = (src, dst)
        return at

    def wait(self, at):
        if at in self.open:
            src, dst = self.open.pop(at)
            pltpu.make_async_copy(src, dst, self.sems.at[at]).wait()

    def finish(self):
        for at in list(self.open):
            self.wait(at)


def forward(geo, tokens_in, memory, mem_tokens, seg_col, seg_row, images, attn_in, attn_out, mlp_in, mlp_out, small):
    tokens, width = tokens_in.shape
    keys = memory.shape[0]
    units, n = geo.units, geo.narrow
    first, cross_at = geo.n_in, geo.n_in + 1
    order = [0, 1, 2, first, 3, 4, 5, cross_at] + list(range(geo.up_at, units))
    wslots = 4
    scale = (width // HEADS) ** -0.5
    ups = geo.n_up
    f32, b16 = functools.partial(jax.ShapeDtypeStruct, dtype=F32), functools.partial(jax.ShapeDtypeStruct, dtype=BF16)

    def kernel(
        x_ref, mem_ref, seg_col, seg_row, images, ai, ao, mi, mo, small_ref,
        ring, up_own, layer_out, acts_out, kv_out, mlp_out_acts, xs_out, lse_out, vec,
        wbuf, x0, xs, acc, acts, kv, mlp_acts, mem, bias, second, low_out, small_buf,
        gsend, grecv, ssend, srecv, wsem, lsem, upsem, osem,
    ):
        g = geo
        g.place()
        load_x = pltpu.make_async_copy(x_ref, x0, lsem.at[0])
        load_m = pltpu.make_async_copy(mem_ref, mem, lsem.at[1])
        load_x.start()
        load_m.start()

        def pack(j, k):
            cols = pl.ds(k * ups * g.rows + j * g.rows, g.rows)
            return pltpu.make_async_copy(
                mi.at[:, cols], up_own.at[j, :, pl.ds(k * g.rows, g.rows)], upsem.at[j, k]
            )

        g.greet()
        shard = Shard(g, ai, ao, up_own, mo)
        gather = Gather(g, shard, ring, gsend, grecv)
        weights = Weights(g, shard, ring, wbuf, wsem)

        def small_copy(k):
            return remote(small_ref, small_buf.at[n - k - 1], ssend.at[k - 1], srecv.at[k - 1], g.z_peer(k))

        for k in range(1, n):
            small_copy(k).start()
        gather.event(0, order[0])
        gather.event(0, order[1])
        for j in range(ups):
            for k in range(n):
                pack(j, k).start()
        saver = Saver(osem)
        cursor = [0]
        used = [0]

        def step():
            s = cursor[0]
            cursor[0] += 1
            if s + 2 < units:
                u = order[s + 2]
                if g.up_at <= u < g.down_at:
                    for k in range(n):
                        pack(u - g.up_at, k).wait()
                gather.event(0, u)
            for kind in range(1, 5):
                q = s - kind + 1
                if 0 <= q < units:
                    gather.event(kind, order[q])
                    if kind == 4:
                        assert q - wslots < used[0]
                        weights.start(order[q], q % wslots)

        def weight():
            q = used[0]
            while cursor[0] <= q + 3:
                step()
            return weights.wait(order[q], q % wslots)

        def done():
            used[0] += 1

        def project(left, finish, tile=512, row_tile=640):
            w = weight()
            row_tile = min(row_tile, left.shape[0])
            tiles(width, tile, lambda cols: tiles(
                left.shape[0], row_tile, lambda rows: finish(dot_nn(left[rows, :], w[:, cols]), rows, cols)
            ))
            done()

        def looped(count, body, hooks):
            def inner(i):
                body(i)
                for at in hooks:
                    @pl.when(i == at)
                    def _():
                        step()

            over(count, inner)

        h1, q, k, v, o, h2, q2, o2, h3 = (acts.at[i] for i in range(9))
        for k_ in range(1, n):
            small_copy(k_).wait_recv()
        place_n = [small_ref] + [small_buf.at[i] for i in range(n - 1)]
        for i in range(n):
            vec[:, pl.ds(pl.multiple_of(g.z_of(i) * g.rows, g.rows), g.rows)] = place_n[i][...]

        def gain(i):
            return vec[pl.ds(i, 1), :]

        def shift(i, cols=slice(None)):
            return vec[pl.ds(3 + i, 1), cols]

        def norm(read, h, gain_at, shift_at):
            def body(rows):
                unit, _ = normalized(read(rows))
                h[rows, :] = (unit * gain(gain_at) + shift(shift_at)).astype(BF16)

            tiles(tokens, 64, body)

        fill_self_bias(bias, seg_col, seg_row)
        load_x.wait()
        step()
        norm(lambda rows: x0[rows, :].astype(F32), h1, 0, 6)
        second[...] = jnp.broadcast_to(second_image(seg_col, images, pl.ds(0, tokens)), second.shape)
        lse_out[...] = jnp.zeros_like(lse_out)

        def put(ref, shift_at=None, factor=None):
            def finish(value, rows, cols):
                if shift_at is not None:
                    value = value + shift(shift_at, cols)
                if factor is not None:
                    value = value * factor
                ref[rows, cols] = value.astype(BF16)

            return finish

        def save_act(i):
            saver.save(acts.at[i], acts_out.at[i])

        project(h1, put(q, 0, scale))
        project(h1, put(k))
        project(h1, put(v, 1))
        for i in range(4):
            save_act(i)
        self_lse, cross_lse = lse_out.at[0], lse_out.at[1]
        looped(HEADS // 2, lambda i: self_forward(i, q, k, v, bias, o, self_lse), (2, 6))
        save_act(4)
        x1, x2 = xs.at[0], xs.at[1]

        def after_self(value, rows, cols):
            x1[rows, cols] = x0[rows, cols].astype(F32) + value + shift(2, cols)

        project(o, after_self)
        saver.save(x1, xs_out.at[0])
        norm(lambda rows: x1[rows, :], h2, 1, 7)
        save_act(5)
        project(h2, put(q2, 3, scale))
        save_act(6)
        load_m.wait()
        k2, v2 = kv.at[0], kv.at[1]
        project(mem, put(k2))
        project(mem, put(v2, 4))
        saver.save(k2, kv_out.at[0])
        saver.save(v2, kv_out.at[1])
        per_image = keys // 2
        key_bias = jnp.where(lax.broadcasted_iota(jnp.int32, (1, per_image), 1) < mem_tokens, 0.0, MASKED)
        looped(
            HEADS // 2, lambda i: cross_forward(i, q2, k2, v2, second, key_bias, o2, cross_lse), (1, 4, 6)
        )
        save_act(7)

        def after_cross(value, rows, cols):
            x2[rows, cols] = x1[rows, cols] + value + shift(5, cols)

        project(o2, after_cross)
        saver.save(x2, xs_out.at[1])
        norm(lambda rows: x2[rows, :], h3, 2, 8)
        save_act(8)
        for j in range(ups):
            def activate(value, rows, cols, j=j):
                z = value + vec[pl.ds(13 + j, 1), cols]
                cdf = 0.5 + 0.5 * lax.erf(z * ROOT_HALF)
                mlp_acts[0, j, rows, cols] = (z * cdf).astype(BF16)
                slope = cdf + z * (jnp.exp(-0.5 * z * z) * ROOT_TWO_PI)
                mlp_acts[1, j, rows, cols] = slope.astype(BF16)

            project(h3, activate, 256)
            saver.save(mlp_acts.at[0, j], mlp_out_acts.at[0, j])
            saver.save(mlp_acts.at[1, j], mlp_out_acts.at[1, j])
        for j in range(ups):
            def add(value, rows, cols, j=j):
                base = x2[rows, cols] + shift(9, cols) if j == 0 else acc[rows, cols]
                if j < ups - 1:
                    acc[rows, cols] = base + value
                else:
                    low_out[rows, cols] = (base + value).astype(BF16)

            project(mlp_acts.at[0, j], add)
        saver.save(low_out, layer_out)
        while cursor[0] < units + 3:
            step()
        saver.finish()
        gather.finish()
        for k_ in range(1, n):
            small_copy(k_).wait_send()

    count = Gather.sems(geo)
    dma = pltpu.SemaphoreType.DMA
    return pl.pallas_call(
        kernel,
        out_shape=[
            b16((units, n - 1, geo.rows, width)),
            b16((ups, geo.rows, width)),
            b16((tokens, width)),
            b16((9, tokens, width)),
            b16((2, keys, width)),
            b16((2, ups, tokens, width)),
            f32((2, tokens, width)),
            f32((2, tokens, 128)),
            f32((SMALL, width)),
        ],
        in_specs=[HBM, HBM, VMEM, VMEM, SMEM, HBM, HBM, HBM, HBM, VMEM],
        out_specs=[HBM] * 7 + [VMEM] * 2,
        scratch_shapes=[
            pltpu.VMEM((wslots, width, width), BF16),
            pltpu.VMEM((tokens, width), BF16),
            pltpu.VMEM((2, tokens, width), F32),
            pltpu.VMEM((tokens, width), F32),
            pltpu.VMEM((9, tokens, width), BF16),
            pltpu.VMEM((2, keys, width), BF16),
            pltpu.VMEM((2, ups, tokens, width), BF16),
            pltpu.VMEM((keys, width), BF16),
            pltpu.VMEM((tokens, tokens), F32),
            pltpu.VMEM((tokens, 128), jnp.int32),
            pltpu.VMEM((tokens, width), BF16),
            pltpu.VMEM((n - 1, SMALL, geo.rows), F32),
            dma((units, count)),
            dma((units, count)),
            dma((n - 1,)),
            dma((n - 1,)),
            dma((wslots, n)),
            dma((2,)),
            dma((ups, n)),
            dma((32,)),
        ],
        compiler_params=pltpu.CompilerParams(
            collective_id=0, has_side_effects=True, vmem_limit_bytes=58 * MIB
        ),
    )(tokens_in, memory, seg_col, seg_row, images, attn_in, attn_out, mlp_in, mlp_out, small)


def backward(geo, mem_tokens, tokens_in, cotangent, memory, seg_col, seg_row, images, attn_in, attn_out, mlp_out, saved):
    ring, up_own, acts, kv_acts, mlp_acts, xs, lse_all, vectors = saved
    tokens, width = cotangent.shape
    keys = memory.shape[0]
    units, n, ups = geo.units, geo.narrow, geo.n_up
    first, cross_at = geo.n_in, geo.n_in + 1
    order = list(range(geo.down_at, units)) + list(range(geo.up_at, geo.down_at))
    order += [cross_at, 3, 4, 5, first, 0, 1, 2]
    fetch = [geo.down_at + j for j in range(ups)] + [geo.up_at + j for j in range(ups)]
    fetch += [cross_at, 3, 4, 5, first, 0, 1, 2]
    scale = (width // HEADS) ** -0.5
    per_image = keys // 2
    f32, b16 = functools.partial(jax.ShapeDtypeStruct, dtype=F32), functools.partial(jax.ShapeDtypeStruct, dtype=BF16)

    def kernel(*refs):
        (
            x_ref, g_ref, mem_ref, seg_col, seg_row, images, ai, ao, mo,
            ring, up_own, acts_in, kv_in, mlp_in_acts, xs_in, lse, vec,
            out, dx_out, dmem_out, small_out, dz_out, gb_out, gq_out, gkv_out,
        ) = refs[:25]
        scratch = list(refs[25:])
        (
            wbuf, lhs, rhs, pool, kv, dxs, xbuf, gm, bias, second, sums,
            zsmall, tsmall, core_small, b_small, a_small,
            wsem, lsem, osem, gmsem, opsem, ssend, srecv,
        ) = scratch[:23]
        g = geo
        g.place()
        gy, do, tile_q, tile_o, gq = (pool.at[i] for i in range(5))
        dz = [kv.at[j % 2, pl.ds(j // 2 * tokens, tokens)] for j in range(ups)]
        slope = [do, tile_q]
        acc, dx = dxs.at[0], dxs.at[1]

        def load(pairs):
            copies = [pltpu.make_async_copy(src, dst, lsem.at[i]) for i, (src, dst) in enumerate(pairs)]
            for copy in copies:
                copy.start()
            return copies

        def wait(copies):
            for copy in copies:
                copy.wait()

        shard = Shard(g, ai, ao, up_own, mo)
        weights = Weights(g, shard, ring, wbuf, wsem)
        fetched = [0, 0]

        def prefetch():
            if fetched[0] < len(fetch):
                weights.start(fetch[fetched[0]], fetched[0] % 2)
                fetched[0] += 1

        def weight(u):
            at = fetched[1]
            assert fetch[at] == u
            fetched[1] += 1
            return weights.wait(u, at % 2)

        start = load([(g_ref, gy), (mlp_in_acts.at[1, 0], slope[0])])
        prefetch()
        prefetch()
        g.greet()
        red = Reduce(g, scratch[23:], out, order)
        h1, h2, o2, h3, o1 = acts_in.at[0], acts_in.at[5], acts_in.at[7], acts_in.at[8], acts_in.at[4]
        operands = {}
        for j in range(ups):
            operands[g.down_at + j] = (mlp_in_acts.at[0, j], g_ref)
            operands[g.up_at + j] = (h3, dz_out.at[j])
        operands[cross_at] = (o2, gb_out.at[0])
        operands[3] = (h2, gq_out.at[0])
        operands[4] = (mem_ref, gkv_out.at[0])
        operands[5] = (mem_ref, gkv_out.at[1])
        operands[first] = (o1, gb_out.at[1])
        for i in range(3):
            operands[i] = (h1, gq_out.at[1 + i])
        saver = Saver(osem)
        ready = {u: () for u in range(g.down_at, units)}
        cursor = [0]

        def produce(q):
            u = order[q]
            assert u in ready
            for at in ready[u]:
                saver.wait(at)
            left, right = operands[u]
            count = left.shape[0]
            copies = [
                pltpu.make_async_copy(left, lhs.at[pl.ds(0, count), :], opsem.at[0]),
                pltpu.make_async_copy(right, rhs.at[pl.ds(0, count), :], opsem.at[1]),
            ]
            for copy in copies:
                copy.start()
            for copy in copies:
                copy.wait()
            red.sent(0, q - red.slots)
            slot = q % red.slots
            blocks = (width // 2) // g.rows

            def block(i):
                cols = pl.ds(pl.multiple_of(i * (width // 2), width // 2), width // 2)
                value = dot_tn(lhs[pl.ds(0, count), cols], rhs[pl.ds(0, count), :])
                red.gbuf[slot, pl.ds(i * blocks, blocks)] = value.astype(BF16).reshape(blocks, g.rows, width)

            over(2, block)

        def step():
            s = cursor[0]
            cursor[0] += 1
            if s < units:
                produce(s)
            for kind in range(8):
                q = s - kind
                if 0 <= q < units:
                    red.event(kind, q)

        def looped(count, body, hooks):
            def inner(i):
                body(i)
                for at in hooks:
                    @pl.when(i == at)
                    def _():
                        step()

            over(count, inner)

        def gain(i):
            return vec[pl.ds(i, 1), :]

        def column_sum(ref, row, count=tokens, tile=64):
            def body(i, total):
                part = ref[pl.ds(pl.multiple_of(i * tile, tile), tile), :].astype(F32)
                return total + jnp.sum(part, axis=0, keepdims=True)

            sums[pl.ds(row, 1), :] = lax.fori_loop(0, count // tile, body, jnp.zeros((1, width), F32))

        def norm_back(read_x, read_base, gain_at, shift_at, base_shift, low, write):
            tile = 64

            def body(i, totals):
                rows = pl.ds(pl.multiple_of(i * tile, tile), tile)
                grad = acc[rows, :]
                unit, factor = normalized(read_x(rows))
                d_unit = grad * gain(gain_at)
                mean = jnp.mean(d_unit, axis=-1, keepdims=True)
                along = jnp.mean(d_unit * unit, axis=-1, keepdims=True)
                total = read_base(rows) + factor * (d_unit - mean - unit * along)
                write(rows, total)
                if low is not None:
                    low[rows, :] = total.astype(BF16)
                return (
                    totals[0] + jnp.sum(grad * unit, axis=0, keepdims=True),
                    totals[1] + jnp.sum(grad, axis=0, keepdims=True),
                    totals[2] + jnp.sum(total, axis=0, keepdims=True),
                )

            zero = jnp.zeros((1, width), F32)
            d_gain, d_shift, d_base = lax.fori_loop(0, tokens // tile, body, (zero, zero, zero))
            sums[pl.ds(gain_at, 1), :] = d_gain
            sums[pl.ds(3 + shift_at, 1), :] = d_shift
            if base_shift is not None:
                sums[pl.ds(3 + base_shift, 1), :] = d_base

        def back_project(grad, u, begin, tile=512):
            w = weight(u)

            def body(cols):
                value = dot_nt(grad[...], w[cols, :])
                acc[:, cols] = value if begin else acc[:, cols] + value

            tiles(width, tile, body)
            prefetch()

        def branch_grad(w, low, cols):
            do[:, cols] = dot_nt(low[...], w[cols, :]).astype(BF16)

        small_open = []

        def small_copy(at, src, dst, peer):
            copy = remote(src, dst, ssend.at[at], srecv.at[at], peer)
            copy.start()
            small_open.append(copy)
            return copy

        def small_total():
            spots = [pl.ds(pl.multiple_of(g.z_of(k) * g.rows, g.rows), g.rows) for k in range(n)]
            copies = [small_copy(k - 1, sums.at[:, spots[k]], zsmall.at[n - k - 1], g.z_peer(k)) for k in range(1, n)]
            for copy in copies:
                copy.wait_recv()
            total = sums[:, spots[0]]
            for k in range(n - 1):
                total = total + zsmall[k]
            tsmall[0] = total
            small_copy(n - 1, tsmall.at[0], core_small, g.other_core).wait_recv()
            tsmall[1] = tsmall[0] + core_small[...]
            small_copy(n, tsmall.at[1], b_small, g.b_peer).wait_recv()
            tsmall[2] = tsmall[1] + b_small[...]
            a_small[g.a] = tsmall[2]
            copies = []
            for i in range(1, g.a_count):
                copies.append(small_copy(n + i, tsmall.at[2], a_small.at[g.a], g.a_peer(i)))
            for copy in copies:
                copy.wait_recv()
            total = a_small[0]
            for i in range(1, g.a_count):
                total = total + a_small[i]
            small_out[...] = total

        sums[...] = jnp.zeros_like(sums)
        wait(start)
        step()
        column_sum(gy, 3 + 9)
        for j in range(ups):
            w = weight(g.down_at + j)
            following = load([(mlp_in_acts.at[1, j + 1], slope[(j + 1) % 2])]) if j + 1 < ups else []

            def body(cols, j=j, w=w):
                value = (dot_nt(gy[...], w[cols, :]) * slope[j % 2][:, cols].astype(F32)).astype(BF16)
                dz[j][:, cols] = value
                sums[pl.ds(13 + j, 1), cols] = jnp.sum(value.astype(F32), axis=0, keepdims=True)

            tiles(width, 256, body)
            prefetch()
            at = saver.save(dz[j], dz_out.at[j])
            ready[g.up_at + j] = (at,)
            wait(following)
            if j == ups // 2 - 1:
                step()
        load_x2 = pltpu.make_async_copy(xs_in.at[1], xbuf, lsem.at[6])
        load_x2.start()
        step()
        for j in range(ups):
            back_project(dz[j], g.up_at + j, j == 0)
        step()
        load_x2.wait()

        def put_dx(rows, total):
            dx[rows, :] = total

        gb = tile_o
        norm_back(lambda r: xbuf[r, :], lambda r: gy[r, :].astype(F32), 2, 8, 5, gb, put_dx)
        at = saver.save(gb, gb_out.at[0])
        ready[cross_at] = (at,)
        for j in range(ups):
            saver.wait(ready[g.up_at + j][0])
        loads = load([
            (xs_in.at[0], xbuf), (acts_in.at[6], tile_q), (kv_in.at[0], kv.at[0]), (kv_in.at[1], kv.at[1]),
        ])
        w = weight(cross_at)
        tiles(width, 512, functools.partial(branch_grad, w, gb))
        prefetch()
        step()
        saver.wait(at)
        wait(loads)
        wait(load([(o2, tile_o)]))
        second[...] = jnp.broadcast_to(second_image(seg_col, images, pl.ds(0, tokens)), second.shape)
        key_bias = jnp.where(lax.broadcasted_iota(jnp.int32, (1, per_image), 1) < mem_tokens, 0.0, MASKED)
        k2, v2 = kv.at[0], kv.at[1]
        looped(
            HEADS // 2,
            lambda i: cross_backward(i, tile_q, k2, v2, do, tile_o, second, key_bias, lse.at[1]),
            (0, 2, 4, 6),
        )
        ready[4] = (saver.save(k2, gkv_out.at[0]),)
        ready[5] = (saver.save(v2, gkv_out.at[1]),)

        def scaled(src, dst, row):
            def body(i, total):
                rows = pl.ds(pl.multiple_of(i * 64, 64), 64)
                value = src[rows, :].astype(F32) * scale
                dst[rows, :] = value.astype(BF16)
                return total + jnp.sum(value, axis=0, keepdims=True)

            sums[pl.ds(row, 1), :] = lax.fori_loop(0, tokens // 64, body, jnp.zeros((1, width), F32))

        scaled(tile_q, gq, 3 + 3)
        ready[3] = (saver.save(gq, gq_out.at[0]),)
        back_project(gq, 3, True)
        step()
        column_sum(v2, 3 + 4, keys)
        w4 = weight(4)
        w5 = weight(5)
        mem_tile, mem_rows = 256, per_image
        spots = [(r, c) for r in range(keys // mem_rows) for c in range(width // mem_tile)]

        def gm_copy(i):
            r, c = spots[i]
            dst = dmem_out.at[pl.ds(r * mem_rows, mem_rows), pl.ds(c * mem_tile, mem_tile)]
            return pltpu.make_async_copy(gm.at[i % 2], dst, gmsem.at[i % 2])

        for i, (r, c) in enumerate(spots):
            rows, cols = pl.ds(r * mem_rows, mem_rows), pl.ds(c * mem_tile, mem_tile)
            if i >= 2:
                gm_copy(i - 2).wait()
            gm[i % 2] = dot_nt(k2[rows, :], w4[cols, :]) + dot_nt(v2[rows, :], w5[cols, :])
            gm_copy(i).start()
        for i in range(max(len(spots) - 2, 0), len(spots)):
            gm_copy(i).wait()
        prefetch()
        prefetch()
        step()
        gb = tile_o
        norm_back(lambda r: xbuf[r, :], lambda r: dx[r, :], 1, 7, 2, gb, put_dx)
        at = saver.save(gb, gb_out.at[1])
        ready[first] = (at,)
        for kind in (3, 4, 5):
            saver.wait(ready[kind][0])
        q1, k1, v1 = tile_q, kv.at[0, pl.ds(0, tokens)], kv.at[1, pl.ds(0, tokens)]
        loads = load([(acts_in.at[1], q1), (acts_in.at[2], k1), (acts_in.at[3], v1)])
        w = weight(first)
        tiles(width, 512, functools.partial(branch_grad, w, gb))
        prefetch()
        fill_self_bias(bias, seg_col, seg_row)
        step()
        saver.wait(at)
        wait(loads)
        wait(load([(o1, tile_o)]))
        looped(
            HEADS // 2,
            lambda i: self_backward(i, q1, k1, v1, do, tile_o, bias, lse.at[0]),
            (3,),
        )
        loads = load([(x_ref, tile_o)])
        scaled(q1, gq, 3 + 0)
        ready[0] = (saver.save(gq, gq_out.at[1]),)
        ready[1] = (saver.save(k1, gq_out.at[2]),)
        ready[2] = (saver.save(v1, gq_out.at[3]),)
        column_sum(v1, 3 + 1)
        step()
        back_project(gq, 0, True)
        back_project(k1, 1, False)
        back_project(v1, 2, False)
        wait(loads)
        step()
        norm_back(lambda r: tile_o[r, :].astype(F32), lambda r: dx[r, :], 0, 6, None, None, put_dx)
        saver.save(dx, dx_out)
        step()
        small_total()
        while cursor[0] < units + Reduce.depth - 1:
            step()
        saver.finish()
        red.finish()
        for copy in small_open:
            copy.wait_send()

    small_steps = n - 1 + 2 + max(geo.a_count - 1, 1)
    dma = pltpu.SemaphoreType.DMA
    tile = (tokens, width)
    return pl.pallas_call(
        kernel,
        out_shape=[
            b16((units, geo.rows, width)),
            f32(tile),
            f32((keys, width)),
            f32((SMALL, geo.rows)),
            b16((ups,) + tile),
            b16((2,) + tile),
            b16((4,) + tile),
            b16((2, keys, width)),
        ],
        in_specs=[HBM] * 3 + [VMEM, VMEM, SMEM] + [HBM] * 9 + [VMEM] * 2,
        out_specs=[HBM] * 3 + [VMEM] + [HBM] * 4,
        scratch_shapes=[
            pltpu.VMEM((2, width, width), BF16),
            pltpu.VMEM((keys, width), BF16),
            pltpu.VMEM((keys, width), BF16),
            pltpu.VMEM((5,) + tile, BF16),
            pltpu.VMEM((2, keys, width), BF16),
            pltpu.VMEM((2,) + tile, F32),
            pltpu.VMEM(tile, F32),
            pltpu.VMEM((2, per_image, width // 4), F32),
            pltpu.VMEM((tokens, tokens), F32),
            pltpu.VMEM((tokens, 128), jnp.int32),
            pltpu.VMEM((SMALL, width), F32),
            pltpu.VMEM((n - 1, SMALL, geo.rows), F32),
            pltpu.VMEM((3, SMALL, geo.rows), F32),
            pltpu.VMEM((SMALL, geo.rows), F32),
            pltpu.VMEM((SMALL, geo.rows), F32),
            pltpu.VMEM((geo.a_count, SMALL, geo.rows), F32),
            dma((2, n)),
            dma((8,)),
            dma((32,)),
            dma((2,)),
            dma((2,)),
            dma((small_steps,)),
            dma((small_steps,)),
        ]
        + Reduce.scratch(geo),
        compiler_params=pltpu.CompilerParams(
            collective_id=1, has_side_effects=True, vmem_limit_bytes=60 * MIB
        ),
    )(
        tokens_in, cotangent, memory, seg_col, seg_row, images, attn_in, attn_out, mlp_out,
        ring, up_own, acts, kv_acts, mlp_acts, xs, lse_all, vectors,
    )


def per_device(
    mesh, hidden_in, memory, segment_ids, image_ids, attn_in, attn_out, mlp_in, mlp_out, gains, shifts, mlp_bias,
    cotangent,
):
    width = hidden_in.shape[2]
    n_in, n_out = attn_in.shape[0], attn_out.shape[0]
    geo = Geometry(mesh, width, n_in, n_out, mlp_in.shape[1])
    rows, n = geo.rows, geo.narrow
    images, mem_tokens = memory.shape[1], memory.shape[2]
    per_image = -(-mem_tokens // 128) * 128
    padded = jnp.pad(memory[0], ((0, 0), (0, per_image - mem_tokens), (0, 0))).reshape(images * per_image, width)
    small = jnp.concatenate([gains, shifts, mlp_bias.reshape(geo.n_up, rows)], axis=0).astype(F32)
    used = small.shape[0]
    small = jnp.pad(small, ((0, SMALL - used), (0, 0)))
    seg_col, seg_row = segment_ids.reshape(-1, 1), segment_ids
    ring, up_own, layer_out, acts, kv, mlp_acts, xs, lse, vec = forward(
        geo, hidden_in[0], padded, mem_tokens, seg_col, seg_row, image_ids, attn_in, attn_out, mlp_in, mlp_out, small
    )
    total, dx, dmem, small_total, *_ = backward(
        geo, mem_tokens, hidden_in[0], cotangent[0], padded, seg_col, seg_row, image_ids, attn_in, attn_out, mlp_out,
        (ring, up_own, acts, kv, mlp_acts, xs, lse, vec),
    )
    up = total[geo.up_at : geo.down_at].reshape(geo.n_up, rows, n, rows).transpose(1, 2, 0, 3)
    return (
        layer_out[None],
        dx[None],
        dmem.reshape(images, per_image, width)[None, :, :mem_tokens],
        total[:n_in].astype(F32),
        total[n_in : geo.up_at].astype(F32),
        up.reshape(rows, -1).astype(F32),
        total[geo.down_at :].reshape(-1, width).astype(F32),
        small_total[:3],
        small_total[3:13],
        small_total[13:used].reshape(-1),
    )


def solution(mesh):
    split = ("wide", "narrow")
    return jax.shard_map(
        functools.partial(per_device, mesh),
        mesh=mesh,
        in_specs=(
            P(split, None, None), P(split, None, None, None), P(split, None), P(split, None), P(None, "narrow", None),
            P(None, "narrow", None), P("narrow", None), P("narrow", None), P(None, "narrow"), P(None, "narrow"),
            P("narrow"), P(split, None, None),
        ),
        out_specs=(
            P(split, None, None), P(split, None, None), P(split, None, None, None), P(None, "narrow", None),
            P(None, "narrow", None), P("narrow", None), P("narrow", None), P(None, "narrow"), P(None, "narrow"),
            P("narrow"),
        ),
        check_vma=False,
    )
```

```python
import functools

import jax
import jax.numpy as jnp
from jax import lax
from jax.experimental import pallas as pl
from jax.experimental.pallas import tpu as pltpu
from jax.sharding import PartitionSpec as P

HEADS = 16
MESH = pl.DeviceIdType.MESH
F32 = jnp.float32
BF16 = jnp.bfloat16
MIB = 1 << 20
EPS = 1e-5
MASKED = -1e30
SMALL = 24
ROOT_HALF = 0.7071067811865476
ROOT_TWO_PI = 0.3989422804014327
HBM = pl.BlockSpec(memory_space=pltpu.HBM)
VMEM = pl.BlockSpec(memory_space=pltpu.VMEM)
SMEM = pl.BlockSpec(memory_space=pltpu.SMEM)


class Geometry:
    def __init__(self, mesh, width, n_in, n_out, hidden):
        self.wide = mesh.shape["wide"]
        self.narrow = mesh.shape["narrow"]
        self.a_count = self.wide // 4
        self.width = width
        self.rows = width // self.narrow
        self.core_rows = self.rows // 2
        self.piece_rows = self.core_rows // self.a_count
        self.half = width // 2
        self.quarter = width // 4
        self.n_in, self.n_out, self.n_up = n_in, n_out, hidden // width
        self.up_at = n_in + n_out
        self.down_at = self.up_at + self.n_up
        self.units = self.down_at + self.n_up

    def place(self):
        w = lax.axis_index("wide")
        n = lax.axis_index("narrow")
        self.w, self.n = w, n
        self.a, self.b, self.c = w // 4, lax.rem(w // 2, 2), lax.rem(w, 2)
        self.core_at = pl.multiple_of(self.c * self.core_rows, self.core_rows)
        self.b_at = pl.multiple_of(self.b * self.quarter, self.quarter)
        self.mine = pl.multiple_of(self.c * self.core_rows + self.a * self.piece_rows, self.piece_rows)
        self.other_core = (w + 1 - 2 * self.c, n)
        self.b_peer = (w + 2 - 4 * self.b, n)

    def a_of(self, step):
        return lax.rem(self.a + step, self.a_count)

    def a_peer(self, step):
        return (self.w + 4 * (self.a_of(step) - self.a), self.n)

    def z_of(self, step):
        return lax.rem(self.n + step, self.narrow)

    def z_peer(self, step):
        return (self.w, self.z_of(step))

    def greet(self):
        barrier = pltpu.get_barrier_semaphore()
        peers = [self.other_core, self.b_peer]
        peers += [self.a_peer(i) for i in range(1, self.a_count)]
        peers += [self.z_peer(i) for i in range(1, self.narrow)]
        for peer in peers:
            pl.semaphore_signal(barrier, inc=1, device_id=peer, device_id_type=MESH)
        pl.semaphore_wait(barrier, len(peers))


def remote(src, dst, send, recv, peer):
    return pltpu.make_async_remote_copy(
        src_ref=src, dst_ref=dst, send_sem=send, recv_sem=recv, device_id=peer, device_id_type=MESH
    )


class Shard:
    def __init__(self, geo, attn_in, attn_out, up, down):
        self.geo, self.attn_in, self.attn_out, self.up, self.down = geo, attn_in, attn_out, up, down

    def parts(self, u, row, rows, col, cols):
        g = self.geo
        at = pl.ds(row, rows)
        if u < g.n_in:
            return [(self.attn_in.at[u, at, pl.ds(col, cols)], 0, cols)]
        if u < g.up_at:
            return [(self.attn_out.at[u - g.n_in, at, pl.ds(col, cols)], 0, cols)]
        if u < g.down_at:
            j, out = u - g.up_at, []
            for p in range(cols // g.rows):
                start = (col // g.rows + p) * (g.n_up * g.rows) + j * g.rows
                if not isinstance(start, int):
                    start = pl.multiple_of(start, g.rows)
                out.append((self.up.at[at, pl.ds(start, g.rows)], p * g.rows, g.rows))
            return out
        start = (u - g.down_at) * g.rows + row
        if not isinstance(start, int):
            start = pl.multiple_of(start, g.piece_rows)
        return [(self.down.at[pl.ds(start, rows), pl.ds(col, cols)], 0, cols)]


class Gather:
    def __init__(self, geo, shard, ring, send, recv):
        self.geo, self.shard, self.ring, self.send, self.recv = geo, shard, ring, send, recv
        self.open = []

    lags = (0, 1, 3, 4)

    @staticmethod
    def z_sems(geo):
        return 2 * (geo.narrow - 1) * (geo.quarter // geo.rows)

    @classmethod
    def sems(cls, geo):
        return cls.z_sems(geo) + 2 * geo.a_count + 1

    def copies(self, kind, u):
        g = self.geo

        def copy(slot, src, dst, peer):
            return remote(src, dst, self.send.at[u, slot], self.recv.at[u, slot], peer)

        mine = pl.ds(g.mine, g.piece_rows)
        low_b = pl.ds(g.b_at, g.quarter)
        high_b = pl.ds(pl.multiple_of(g.half + g.b_at, g.quarter), g.quarter)
        core = pl.ds(g.core_at, g.core_rows)
        if kind == 0:
            out = []
            for k in range(1, g.narrow):
                for start in (low_b.start, high_b.start):
                    for src, col, cols in self.shard.parts(u, g.mine, g.piece_rows, start, g.quarter):
                        cols = pl.ds(pl.multiple_of(start + col, g.rows), cols)
                        dst = self.ring.at[u, g.narrow - k - 1, mine, cols]
                        out.append(copy(len(out), src, dst, g.z_peer(k)))
            return out
        base = self.z_sems(g)
        steps = range(1, g.a_count)
        if kind == 1:
            low = self.ring.at[u, :, mine, low_b]
            high = self.ring.at[u, :, mine, high_b]
            out = [copy(base + i - 1, low, low, g.a_peer(i)) for i in steps]
            return out + [copy(base + g.a_count - 1, high, high, g.b_peer)]
        base += g.a_count
        if kind == 2:
            low = self.ring.at[u, :, core, low_b]
            high = self.ring.at[u, :, mine, pl.ds(g.half, g.half)]
            out = [copy(base + i - 1, high, high, g.a_peer(i)) for i in steps]
            return out + [copy(base + g.a_count - 1, low, low, g.b_peer)]
        part = self.ring.at[u, :, core, :]
        return [copy(base + g.a_count, part, part, g.other_core)]

    def event(self, kind, u):
        if kind > 0:
            for copy in self.copies(kind - 1, u):
                copy.wait_recv()
        if kind < 4:
            for copy in self.copies(kind, u):
                copy.start()
            self.open.append((kind, u))

    def finish(self):
        for kind, u in self.open:
            for copy in self.copies(kind, u):
                copy.wait_send()


def add_rows(dst, parts, tile):
    count, rows = dst.shape[0], dst.shape[1]
    tile = min(tile, rows)
    per = rows // tile

    def body(i, carry):
        k, r = i // per, pl.multiple_of(lax.rem(i, per) * tile, tile)
        total = parts[0](k, r, tile).astype(F32)
        for part in parts[1:]:
            total = total + part(k, r, tile).astype(F32)
        dst[k, pl.ds(r, tile), :] = total.astype(dst.dtype)
        return carry

    lax.fori_loop(0, count * per, body, 0)


class Reduce:
    slots = 2
    held = 3
    landing = 6
    late = 4
    early = (3, 8)
    stages = ("C", "P1", "P2", "Z", "Q1", "Q2", "QC")
    stages_early = ("C", "Z", "P1", "P2", "Q1", "Q2", "QC")
    steps = (0, 1, 3, 5, 8, 9, 10, 11)
    steps_early = (0, 1, 6, 8, 10, 11, 12, 13)

    def __init__(self, geo, bufs, out, order):
        self.geo, self.out, self.order = geo, out, order
        names = [name for name, _ in self.shapes(geo)]
        self.bufs = dict(zip(names, bufs))
        self.gbuf = self.bufs["gbuf"]
        self.send, self.recv, self.local, self.credit = bufs[len(names) :]
        self.open = set()

    @classmethod
    def shapes(cls, geo):
        g, n, w = geo, geo.narrow, geo.width
        peers = max(g.a_count - 1, 1)
        r, c, p, h, q = g.rows, g.core_rows, g.piece_rows, g.half, g.quarter
        out = [("gbuf", (cls.slots, n, r, w)), ("rc", (cls.slots, n, c, w)), ("fin", (cls.slots, p, h))]
        for tag, count, many, m in (("", cls.held, cls.landing, n), ("e", len(cls.early), len(cls.early), 1)):
            out += [
                ("s1" + tag, (count, m, c, w)),
                ("s2a" + tag, (count, m, p, h)),
                ("s2b" + tag, (count, m, c, q)),
                ("p1a" + tag, (many, peers, m, p, h)),
                ("p1b" + tag, (many, m, c, q)),
                ("p2a" + tag, (many, m, p, q)),
                ("p2b" + tag, (many, peers, m, p, q)),
                ("s3" + tag, (max(count, cls.late), m, p, h)),
            ]
        early = len(cls.early)
        out += [("zr", (geo.units, n - 1, p, h)), ("zre", (early, n - 1, c, w)), ("s0e", (early, n, c, w))]
        return out

    @classmethod
    def scratch(cls, geo):
        count = 1 + 4 * geo.a_count + (geo.narrow - 1) + 1
        return [pltpu.VMEM(shape, BF16) for _, shape in cls.shapes(geo)] + [
            pltpu.SemaphoreType.DMA((geo.units, count)),
            pltpu.SemaphoreType.DMA((geo.units, count)),
            pltpu.SemaphoreType.DMA((2,)),
            pltpu.SemaphoreType.REGULAR,
        ]

    def buf(self, name, q):
        if q in self.early and name not in ("rc", "fin"):
            return self.bufs[name + "e"].at[self.early.index(q)]
        ref = self.bufs[name]
        return ref.at[q % ref.shape[0]]

    def stage(self, q, i):
        return (self.stages_early if q in self.early else self.stages)[i]

    def due(self, s):
        out = []
        for i in range(8):
            for q in range(self.geo.units):
                if q + (self.steps_early if q in self.early else self.steps)[i] == s:
                    out.append((i, q))
        return out

    @property
    def last(self):
        units = self.geo.units
        return max(units + self.steps[-1], max(self.early, default=0) + self.steps_early[-1] + 1)

    def copies(self, stage, q):
        g = self.geo
        u = self.order[q]
        na = g.a_count
        steps = range(1, na)
        mine = pl.ds(g.mine, g.piece_rows)
        core = pl.ds(g.core_at, g.core_rows)
        low_b = pl.ds(g.b_at, g.quarter)
        high_b = pl.ds(pl.multiple_of(g.half + g.b_at, g.quarter), g.quarter)
        peer_b = pl.multiple_of((1 - g.b) * g.quarter, g.quarter)

        def copy(s, src, dst, peer):
            return remote(src, dst, self.send.at[q, s], self.recv.at[q, s], peer)

        def in_core(a):
            return pl.ds(pl.multiple_of(a * g.piece_rows, g.piece_rows), g.piece_rows)

        if stage == "C":
            other = pl.ds(pl.multiple_of((1 - g.c) * g.core_rows, g.core_rows), g.core_rows)
            return [copy(0, self.gbuf.at[q % self.slots, :, other, :], self.buf("rc", q), g.other_core)]
        if stage == "P1":
            s1 = self.buf("s1", q)
            out = [
                copy(i, s1.at[:, in_core(g.a_of(i)), pl.ds(0, g.half)], self.buf("p1a", q).at[na - i - 1], g.a_peer(i))
                for i in steps
            ]
            cols = pl.ds(pl.multiple_of(g.half + peer_b, g.quarter), g.quarter)
            return out + [copy(na, s1.at[:, :, cols], self.buf("p1b", q), g.b_peer)]
        if stage == "P2":
            s2a, s2b = self.buf("s2a", q), self.buf("s2b", q)
            out = [
                copy(na + i, s2b.at[:, in_core(g.a_of(i)), :], self.buf("p2b", q).at[na - i - 1], g.a_peer(i))
                for i in steps
            ]
            return out + [copy(2 * na, s2a.at[:, :, pl.ds(peer_b, g.quarter)], self.buf("p2a", q), g.b_peer)]
        if stage == "Z":
            src, dst = (self.buf("s0", q) if q in self.early else self.buf("s3", q)), self.buf("zr", q)
            return [
                copy(2 * na + k, src.at[g.z_of(k)], dst.at[g.narrow - k - 1], g.z_peer(k)) for k in range(1, g.narrow)
            ]
        base = 2 * na + g.narrow
        if stage == "Q1":
            low, high = self.out.at[u, mine, low_b], self.out.at[u, mine, high_b]
            out = [copy(base + i - 1, low, low, g.a_peer(i)) for i in steps]
            return out + [copy(base + na - 1, high, high, g.b_peer)]
        base += na
        if stage == "Q2":
            low, high = self.out.at[u, core, low_b], self.out.at[u, mine, pl.ds(g.half, g.half)]
            out = [copy(base + i - 1, high, high, g.a_peer(i)) for i in steps]
            return out + [copy(base + na - 1, low, low, g.b_peer)]
        part = self.out.at[u, core, :]
        return [copy(base + na, part, part, g.other_core)]

    def begin(self, stage, q):
        for copy in self.copies(stage, q):
            copy.start()
        self.open.add((stage, q))

    def sent_before(self, stage, q, turn):
        if q not in self.early:
            for earlier in range(q % turn, q, turn):
                if earlier not in self.early:
                    self.sent(stage, earlier)

    def sent(self, stage, q):
        if (stage, q) in self.open:
            for copy in self.copies(stage, q):
                copy.wait_send()
            self.open.remove((stage, q))

    def event(self, i, q):
        g = self.geo
        if i == 0:
            if q >= self.slots:
                pl.semaphore_wait(self.credit, 1)
            self.begin("C", q)
            return
        done = self.stage(q, i - 1)
        for copy in self.copies(done, q):
            copy.wait_recv()
        self.combine(done, q)
        if i < 7:
            self.begin(self.stage(q, i), q)

    def combine(self, done, q):
        g = self.geo
        na = g.a_count
        early = q in self.early
        own = pl.multiple_of(g.a * g.piece_rows, g.piece_rows)
        low_b = pl.ds(g.b_at, g.quarter)
        high_b = pl.ds(pl.multiple_of(g.half + g.b_at, g.quarter), g.quarter)
        if done == "C":
            self.sent_before("P1", q, self.held)
            gbuf, rc = self.gbuf.at[q % self.slots], self.buf("rc", q)
            add_rows(
                self.buf("s0" if early else "s1", q),
                [
                    lambda k, r, t: gbuf[k, pl.ds(pl.multiple_of(g.core_at + r, 16), t), :],
                    lambda k, r, t: rc[k, pl.ds(r, t), :],
                ],
                32,
            )
            if q + self.slots < g.units:
                pl.semaphore_signal(self.credit, inc=1, device_id=g.other_core, device_id_type=MESH)
        elif done == "P1":
            self.sent_before("P2", q, self.held)
            s1, p1a, p1b = self.buf("s1", q), self.buf("p1a", q), self.buf("p1b", q)
            add_rows(
                self.buf("s2a", q),
                [lambda k, r, t: s1[k, pl.ds(pl.multiple_of(own + r, 16), t), pl.ds(0, g.half)]]
                + [lambda k, r, t, i=i: p1a[i, k, pl.ds(r, t), :] for i in range(na - 1)],
                64,
            )
            add_rows(
                self.buf("s2b", q),
                [lambda k, r, t: s1[k, pl.ds(r, t), high_b], lambda k, r, t: p1b[k, pl.ds(r, t), :]],
                128,
            )
        elif done == "P2":
            self.sent_before("Z", q, self.late)
            s2a, s2b, p2a, p2b, s3 = (self.buf(name, q) for name in ("s2a", "s2b", "p2a", "p2b", "s3"))
            add_rows(
                s3.at[:, :, pl.ds(0, g.quarter)],
                [lambda k, r, t: s2a[k, pl.ds(r, t), low_b], lambda k, r, t: p2a[k, pl.ds(r, t), :]],
                64,
            )
            add_rows(
                s3.at[:, :, pl.ds(g.quarter, g.quarter)],
                [lambda k, r, t: s2b[k, pl.ds(pl.multiple_of(own + r, 16), t), :]]
                + [lambda k, r, t, i=i: p2b[i, k, pl.ds(r, t), :] for i in range(na - 1)],
                64,
            )
            if early:
                self.place(s3.at[0], q)
        elif done == "Z":
            zr = self.buf("zr", q)
            if early:
                s0 = self.buf("s0", q)
                add_rows(
                    self.buf("s1", q),
                    [lambda k, r, t: s0[g.n, pl.ds(r, t), :]]
                    + [lambda k, r, t, i=i: zr[i, pl.ds(r, t), :] for i in range(g.narrow - 1)],
                    32,
                )
                return
            total = self.buf("s3", q)[g.n].astype(F32)
            for k in range(g.narrow - 1):
                total = total + zr[k].astype(F32)
            fin = self.buf("fin", q)
            fin[...] = total.astype(BF16)
            self.place(fin, q)

    def place(self, piece, q):
        g, u = self.geo, self.order[q]
        stores = []
        for h in range(2):
            cols = pl.ds(pl.multiple_of(h * g.half + g.b_at, g.quarter), g.quarter)
            dst = self.out.at[u, pl.ds(g.mine, g.piece_rows), cols]
            src = piece.at[:, pl.ds(h * g.quarter, g.quarter)]
            stores.append(pltpu.make_async_copy(src, dst, self.local.at[h]))
        for store in stores:
            store.start()
        for store in stores:
            store.wait()

    def finish(self):
        for stage, q in sorted(self.open):
            for copy in self.copies(stage, q):
                copy.wait_send()
        self.open = set()


class Weights:
    def __init__(self, geo, shard, ring, buf, sem):
        self.geo, self.shard, self.ring, self.buf, self.sem = geo, shard, ring, buf, sem

    def copies(self, u, slot):
        g = self.geo
        out = []
        for k in range(g.narrow):
            parts = self.shard.parts(u, 0, g.rows, 0, g.width) if k == 0 else [(self.ring.at[u, k - 1], 0, g.width)]
            rows = pl.ds(pl.multiple_of(g.z_of(k) * g.rows, g.rows), g.rows)
            for src, col, cols in parts:
                dst = self.buf.at[slot, rows, pl.ds(col, cols)]
                out.append(pltpu.make_async_copy(src, dst, self.sem.at[slot, len(out)]))
        return out

    def start(self, u, slot):
        for copy in self.copies(u, slot):
            copy.start()

    def wait(self, u, slot):
        for copy in self.copies(u, slot):
            copy.wait()
        return self.buf.at[slot]


def dot_nn(left, right):
    return jnp.dot(left, right, preferred_element_type=F32)


def dot_nt(left, right):
    return lax.dot_general(left, right, (((1,), (1,)), ((), ())), preferred_element_type=F32)


def dot_tn(left, right):
    return lax.dot_general(left, right, (((0,), (0,)), ((), ())), preferred_element_type=F32)


def over(count, body):
    def step(i, carry):
        body(i)
        return carry

    lax.fori_loop(0, count, step, 0)


def tiles(total, tile, body):
    over(total // tile, lambda i: body(pl.ds(pl.multiple_of(i * tile, tile), tile)))


def normalized(x):
    centered = x - jnp.mean(x, axis=-1, keepdims=True)
    variance = jnp.mean(centered * centered, axis=-1, keepdims=True)
    scale = lax.rsqrt(variance + EPS)
    return centered * scale, scale


def pair_cols(i):
    return pl.ds(pl.multiple_of(i * 128, 128), 128)


def lane_half(rows):
    return lax.broadcasted_iota(jnp.int32, (rows, 128), 1) // 64


def keep_half(values, side, half):
    return jnp.where(side == half, values, jnp.zeros_like(values))


def put_lane(ref, rows, lane, column):
    lanes = lax.broadcasted_iota(jnp.int32, (column.shape[0], 128), 1)
    ref[rows, :] = jnp.where(lanes == lane, column, ref[rows, :])


def take_lane(ref, rows, lane):
    values = ref[rows, :]
    lanes = lax.broadcasted_iota(jnp.int32, values.shape, 1)
    return jnp.sum(jnp.where(lanes == lane, values, 0.0), axis=-1, keepdims=True)


def softmax(scores):
    top = jnp.max(scores, axis=-1, keepdims=True)
    expo = jnp.exp(scores - top)
    total = jnp.sum(expo, axis=-1, keepdims=True)
    return (expo * (1.0 / total)).astype(BF16), top + jnp.log(total)


def fill_self_bias(bias, seg_col, seg_row):
    tokens = bias.shape[0]

    def body(rows):
        count = rows.size
        query = rows.start + lax.broadcasted_iota(jnp.int32, (count, tokens), 0)
        key = lax.broadcasted_iota(jnp.int32, (count, tokens), 1)
        allowed = (seg_col[rows, :] == seg_row[...]) & (key <= query)
        bias[rows, :] = jnp.where(allowed, 0.0, MASKED)

    tiles(tokens, 128, body)


def second_image(seg_col, images, rows):
    pages = seg_col[rows, :]
    image = jnp.zeros_like(pages)
    for page in range(images.shape[1]):
        image = jnp.where(pages == page, images[0, page], image)
    return image


def self_forward(i, q, k, v, bias, o, lse):
    cols = pair_cols(i)
    tokens = q.shape[0]
    block = tokens // 2
    side = lane_half(block)
    for at in range(0, tokens, block):
        rows, keys = pl.ds(at, block), pl.ds(0, at + block)
        queries, key, value = q[rows, cols], k[keys, cols], v[keys, cols]
        mixed = []
        for half in range(2):
            scores = dot_nt(keep_half(queries, side, half), key) + bias[rows, keys]
            probs, total = softmax(scores)
            put_lane(lse, rows, 2 * i + half, total)
            mixed.append(dot_nn(probs, value))
        o[rows, cols] = jnp.where(side == 0, mixed[0], mixed[1]).astype(BF16)


def self_backward(i, q, k, v, do, o, bias, lse):
    cols = pair_cols(i)
    tokens = q.shape[0]
    block = tokens // 2
    side = lane_half(block)
    grads_k, grads_v, grads_q = [], [], []
    for at in range(0, tokens, block):
        rows, keys = pl.ds(at, block), pl.ds(0, at + block)
        queries, key, value, grad, mix = q[rows, cols], k[keys, cols], v[keys, cols], do[rows, cols], o[rows, cols]
        product = grad.astype(F32) * mix.astype(F32)
        parts, grad_k, grad_v = [], 0.0, 0.0
        for half in range(2):
            own_q, own_g = keep_half(queries, side, half), keep_half(grad, side, half)
            scores = dot_nt(own_q, key) + bias[rows, keys]
            probs = jnp.exp(scores - take_lane(lse, rows, 2 * i + half))
            inner = jnp.sum(keep_half(product, side, half), axis=-1, keepdims=True)
            slopes = (probs * (dot_nt(own_g, value) - inner)).astype(BF16)
            parts.append(dot_nn(slopes, key))
            grad_k = grad_k + dot_tn(slopes, own_q)
            grad_v = grad_v + dot_tn(probs.astype(BF16), own_g)
        grads_q.append((rows, jnp.where(side == 0, parts[0], parts[1])))
        grads_k.append(grad_k)
        grads_v.append(grad_v)
    low = pl.ds(0, block)
    high = pl.ds(block, block)
    k[low, cols] = (grads_k[0] + grads_k[1][:block]).astype(BF16)
    k[high, cols] = grads_k[1][block:].astype(BF16)
    v[low, cols] = (grads_v[0] + grads_v[1][:block]).astype(BF16)
    v[high, cols] = grads_v[1][block:].astype(BF16)
    for rows, grad in grads_q:
        q[rows, cols] = grad.astype(BF16)


def both_images(ref, cols):
    keys = ref.shape[0] // 2
    return jnp.concatenate([ref[pl.ds(0, keys), cols], ref[pl.ds(keys, keys), cols]], axis=1)


def by_image(values, second):
    zero = jnp.zeros_like(values)
    return jnp.concatenate([jnp.where(second, zero, values), jnp.where(second, values, zero)], axis=1)


def pick_image(values, second):
    return jnp.where(second, values[:, 128:], values[:, :128])


def cross_forward(i, q, k, v, second_at, key_bias, o, lse, block=256):
    cols = pair_cols(i)
    key, value = both_images(k, cols), both_images(v, cols)
    side = lane_half(block)
    for at in range(0, q.shape[0], block):
        rows = pl.ds(at, block)
        queries = q[rows, cols]
        second = second_at[rows, :] == 1
        mixed = []
        for half in range(2):
            scores = dot_nt(by_image(keep_half(queries, side, half), second), key) + key_bias
            probs, total = softmax(scores)
            put_lane(lse, rows, 2 * i + half, total)
            mixed.append(pick_image(dot_nn(probs, value), second))
        o[rows, cols] = jnp.where(side == 0, mixed[0], mixed[1]).astype(BF16)


def cross_backward(i, q, k, v, do, o, second_at, key_bias, lse, block=256):
    cols = pair_cols(i)
    key, value = both_images(k, cols), both_images(v, cols)
    side = lane_half(block)
    grad_k, grad_v, grads_q = 0.0, 0.0, []
    for at in range(0, q.shape[0], block):
        rows = pl.ds(at, block)
        queries, grad, mix = q[rows, cols], do[rows, cols], o[rows, cols]
        second = second_at[rows, :] == 1
        product = grad.astype(F32) * mix.astype(F32)
        parts = []
        for half in range(2):
            own_q = by_image(keep_half(queries, side, half), second)
            own_g = by_image(keep_half(grad, side, half), second)
            scores = dot_nt(own_q, key) + key_bias
            probs = jnp.exp(scores - take_lane(lse, rows, 2 * i + half))
            inner = jnp.sum(keep_half(product, side, half), axis=-1, keepdims=True)
            slopes = (probs * (dot_nt(own_g, value) - inner)).astype(BF16)
            parts.append(pick_image(dot_nn(slopes, key), second))
            grad_k = grad_k + dot_tn(slopes, own_q)
            grad_v = grad_v + dot_tn(probs.astype(BF16), own_g)
        grads_q.append((rows, jnp.where(side == 0, parts[0], parts[1])))
    keys = k.shape[0] // 2
    for ref, total in ((k, grad_k), (v, grad_v)):
        ref[pl.ds(0, keys), cols] = total[:, :128].astype(BF16)
        ref[pl.ds(keys, keys), cols] = total[:, 128:].astype(BF16)
    for rows, grad in grads_q:
        q[rows, cols] = grad.astype(BF16)


class Saver:
    def __init__(self, sems):
        self.sems, self.open, self.used = sems, {}, 0

    def save(self, src, dst):
        at = self.used
        self.used += 1
        pltpu.make_async_copy(src, dst, self.sems.at[at]).start()
        self.open[at] = (src, dst)
        return at

    def wait(self, at):
        if at in self.open:
            src, dst = self.open.pop(at)
            pltpu.make_async_copy(src, dst, self.sems.at[at]).wait()

    def finish(self):
        for at in list(self.open):
            self.wait(at)


def forward(geo, tokens_in, memory, mem_tokens, seg_col, seg_row, images, attn_in, attn_out, mlp_in, mlp_out, small):
    tokens, width = tokens_in.shape
    keys = memory.shape[0]
    units, n = geo.units, geo.narrow
    first, cross_at = geo.n_in, geo.n_in + 1
    order = [0, 1, 2, first, 3, 4, 5, cross_at] + list(range(geo.up_at, units))
    wslots = 4
    scale = (width // HEADS) ** -0.5
    ups = geo.n_up
    f32, b16 = functools.partial(jax.ShapeDtypeStruct, dtype=F32), functools.partial(jax.ShapeDtypeStruct, dtype=BF16)

    def kernel(
        x_ref, mem_ref, seg_col, seg_row, images, ai, ao, mi, mo, small_ref,
        ring, layer_out, acts_out, kv_out, mlp_out_acts, xs_out, lse_out, vec,
        wbuf, x0, xs, acc, acts, kv, mlp_acts, mem, bias, second, low_out, small_buf,
        gsend, grecv, ssend, srecv, wsem, lsem, osem,
    ):
        g = geo
        g.place()
        load_x = pltpu.make_async_copy(x_ref, x0, lsem.at[0])
        load_m = pltpu.make_async_copy(mem_ref, mem, lsem.at[1])
        load_x.start()
        load_m.start()

        g.greet()
        shard = Shard(g, ai, ao, mi, mo)
        gather = Gather(g, shard, ring, gsend, grecv)
        weights = Weights(g, shard, ring, wbuf, wsem)

        def small_copy(k):
            return remote(small_ref, small_buf.at[n - k - 1], ssend.at[k - 1], srecv.at[k - 1], g.z_peer(k))

        for k in range(1, n):
            small_copy(k).start()
        gather.event(0, order[0])
        gather.event(0, order[1])
        saver = Saver(osem)
        cursor = [0]
        used = [0]

        def step():
            s = cursor[0]
            cursor[0] += 1
            if s + 2 < units:
                gather.event(0, order[s + 2])
            for kind in range(1, 5):
                q = s - Gather.lags[kind - 1]
                if 0 <= q < units:
                    gather.event(kind, order[q])
                    if kind == 4:
                        assert q - wslots < used[0]
                        weights.start(order[q], q % wslots)

        def weight():
            q = used[0]
            while cursor[0] <= q + Gather.lags[3]:
                step()
            return weights.wait(order[q], q % wslots)

        def done():
            used[0] += 1

        def project(left, finish, tile=512, row_tile=640):
            w = weight()
            row_tile = min(row_tile, left.shape[0])
            tiles(width, tile, lambda cols: tiles(
                left.shape[0], row_tile, lambda rows: finish(dot_nn(left[rows, :], w[:, cols]), rows, cols)
            ))
            done()

        def looped(count, body, hooks):
            def inner(i):
                body(i)
                for at in hooks:
                    @pl.when(i == at)
                    def _():
                        step()

            over(count, inner)

        h1, q, k, v, o, h2, q2, o2, h3 = (acts.at[i] for i in range(9))
        for k_ in range(1, n):
            small_copy(k_).wait_recv()
        place_n = [small_ref] + [small_buf.at[i] for i in range(n - 1)]
        for i in range(n):
            vec[:, pl.ds(pl.multiple_of(g.z_of(i) * g.rows, g.rows), g.rows)] = place_n[i][...]

        def gain(i):
            return vec[pl.ds(i, 1), :]

        def shift(i, cols=slice(None)):
            return vec[pl.ds(3 + i, 1), cols]

        def norm(read, h, gain_at, shift_at):
            def body(rows):
                unit, _ = normalized(read(rows))
                h[rows, :] = (unit * gain(gain_at) + shift(shift_at)).astype(BF16)

            tiles(tokens, 64, body)

        fill_self_bias(bias, seg_col, seg_row)
        load_x.wait()
        step()
        norm(lambda rows: x0[rows, :].astype(F32), h1, 0, 6)
        second[...] = jnp.broadcast_to(second_image(seg_col, images, pl.ds(0, tokens)), second.shape)
        lse_out[...] = jnp.zeros_like(lse_out)

        def put(ref, shift_at=None, factor=None):
            def finish(value, rows, cols):
                if shift_at is not None:
                    value = value + shift(shift_at, cols)
                if factor is not None:
                    value = value * factor
                ref[rows, cols] = value.astype(BF16)

            return finish

        def save_act(i):
            saver.save(acts.at[i], acts_out.at[i])

        project(h1, put(q, 0, scale))
        project(h1, put(k))
        project(h1, put(v, 1))
        for i in range(4):
            save_act(i)
        self_lse, cross_lse = lse_out.at[0], lse_out.at[1]
        looped(HEADS // 2, lambda i: self_forward(i, q, k, v, bias, o, self_lse), (2, 6))
        save_act(4)
        x1, x2 = xs.at[0], xs.at[1]

        def after_self(value, rows, cols):
            x1[rows, cols] = x0[rows, cols].astype(F32) + value + shift(2, cols)

        project(o, after_self)
        saver.save(x1, xs_out.at[0])
        norm(lambda rows: x1[rows, :], h2, 1, 7)
        save_act(5)
        project(h2, put(q2, 3, scale))
        save_act(6)
        load_m.wait()
        k2, v2 = kv.at[0], kv.at[1]
        project(mem, put(k2))
        project(mem, put(v2, 4))
        saver.save(k2, kv_out.at[0])
        saver.save(v2, kv_out.at[1])
        per_image = keys // 2
        key_bias = jnp.where(lax.broadcasted_iota(jnp.int32, (1, per_image), 1) < mem_tokens, 0.0, MASKED)
        looped(
            HEADS // 2, lambda i: cross_forward(i, q2, k2, v2, second, key_bias, o2, cross_lse), (1, 4, 6)
        )
        save_act(7)

        def after_cross(value, rows, cols):
            x2[rows, cols] = x1[rows, cols] + value + shift(5, cols)

        project(o2, after_cross)
        saver.save(x2, xs_out.at[1])
        norm(lambda rows: x2[rows, :], h3, 2, 8)
        save_act(8)
        for j in range(ups):
            def activate(value, rows, cols, j=j):
                z = value + vec[pl.ds(13 + j, 1), cols]
                cdf = 0.5 + 0.5 * lax.erf(z * ROOT_HALF)
                mlp_acts[0, j, rows, cols] = (z * cdf).astype(BF16)
                slope = cdf + z * (jnp.exp(-0.5 * z * z) * ROOT_TWO_PI)
                mlp_acts[1, j, rows, cols] = slope.astype(BF16)

            project(h3, activate, 256)
            saver.save(mlp_acts.at[0, j], mlp_out_acts.at[0, j])
            saver.save(mlp_acts.at[1, j], mlp_out_acts.at[1, j])
        for j in range(ups):
            def add(value, rows, cols, j=j):
                base = x2[rows, cols] + shift(9, cols) if j == 0 else acc[rows, cols]
                if j < ups - 1:
                    acc[rows, cols] = base + value
                else:
                    low_out[rows, cols] = (base + value).astype(BF16)

            project(mlp_acts.at[0, j], add)
        saver.save(low_out, layer_out)
        while cursor[0] < units + Gather.lags[3]:
            step()
        saver.finish()
        gather.finish()
        for k_ in range(1, n):
            small_copy(k_).wait_send()

    count = Gather.sems(geo)
    dma = pltpu.SemaphoreType.DMA
    return pl.pallas_call(
        kernel,
        out_shape=[
            b16((units, n - 1, geo.rows, width)),
            b16((tokens, width)),
            b16((9, tokens, width)),
            b16((2, keys, width)),
            b16((2, ups, tokens, width)),
            f32((2, tokens, width)),
            f32((2, tokens, 128)),
            f32((SMALL, width)),
        ],
        in_specs=[HBM, HBM, VMEM, VMEM, SMEM, HBM, HBM, HBM, HBM, VMEM],
        out_specs=[HBM] * 6 + [VMEM] * 2,
        scratch_shapes=[
            pltpu.VMEM((wslots, width, width), BF16),
            pltpu.VMEM((tokens, width), BF16),
            pltpu.VMEM((2, tokens, width), F32),
            pltpu.VMEM((tokens, width), F32),
            pltpu.VMEM((9, tokens, width), BF16),
            pltpu.VMEM((2, keys, width), BF16),
            pltpu.VMEM((2, ups, tokens, width), BF16),
            pltpu.VMEM((keys, width), BF16),
            pltpu.VMEM((tokens, tokens), F32),
            pltpu.VMEM((tokens, 128), jnp.int32),
            pltpu.VMEM((tokens, width), BF16),
            pltpu.VMEM((n - 1, SMALL, geo.rows), F32),
            dma((units, count)),
            dma((units, count)),
            dma((n - 1,)),
            dma((n - 1,)),
            dma((wslots, 2 * n)),
            dma((2,)),
            dma((32,)),
        ],
        compiler_params=pltpu.CompilerParams(
            collective_id=0, has_side_effects=True, vmem_limit_bytes=58 * MIB
        ),
    )(tokens_in, memory, seg_col, seg_row, images, attn_in, attn_out, mlp_in, mlp_out, small)


def backward(geo, mem_tokens, tokens_in, cotangent, memory, seg_col, seg_row, images, attn_in, attn_out, mlp_in, mlp_out, saved):
    ring, acts, kv_acts, mlp_acts, xs, lse_all, vectors = saved
    tokens, width = cotangent.shape
    keys = memory.shape[0]
    units, n, ups = geo.units, geo.narrow, geo.n_up
    first, cross_at = geo.n_in, geo.n_in + 1
    order = list(range(geo.down_at, units)) + list(range(geo.up_at, geo.down_at))
    order += [cross_at, 3, 4, 5, first, 0, 1, 2]
    fetch = [geo.down_at + j for j in range(ups)] + [geo.up_at + j for j in range(ups)]
    fetch += [cross_at, 3, 4, 5, first, 0, 1, 2]
    scale = (width // HEADS) ** -0.5
    per_image = keys // 2
    f32, b16 = functools.partial(jax.ShapeDtypeStruct, dtype=F32), functools.partial(jax.ShapeDtypeStruct, dtype=BF16)

    def kernel(*refs):
        (
            x_ref, g_ref, mem_ref, seg_col, seg_row, images, ai, ao, mi, mo,
            ring, acts_in, kv_in, mlp_in_acts, xs_in, lse, vec,
            out, dx_out, dmem_out, small_out, dz_out, gb_out, gq_out, gkv_out,
        ) = refs[:25]
        scratch = list(refs[25:])
        (
            wbuf, lhs, rhs, pool, kv, dxs, xbuf, gm, bias, second, sums,
            zsmall, tsmall, core_small, b_small, a_small,
            wsem, lsem, osem, gmsem, opsem, ssend, srecv,
        ) = scratch[:23]
        g = geo
        g.place()
        gy, do, tile_q, tile_o, gq = (pool.at[i] for i in range(5))
        dz = [kv.at[j % 2, pl.ds(j // 2 * tokens, tokens)] for j in range(ups)]
        slope = [do, tile_q]
        acc, dx = dxs.at[0], dxs.at[1]

        def load(pairs):
            copies = [pltpu.make_async_copy(src, dst, lsem.at[i]) for i, (src, dst) in enumerate(pairs)]
            for copy in copies:
                copy.start()
            return copies

        def wait(copies):
            for copy in copies:
                copy.wait()

        shard = Shard(g, ai, ao, mi, mo)
        weights = Weights(g, shard, ring, wbuf, wsem)
        fetched = [0, 0]

        def prefetch():
            if fetched[0] < len(fetch):
                weights.start(fetch[fetched[0]], fetched[0] % 2)
                fetched[0] += 1

        def weight(u):
            at = fetched[1]
            assert fetch[at] == u
            fetched[1] += 1
            return weights.wait(u, at % 2)

        start = load([(g_ref, gy), (mlp_in_acts.at[1, 0], slope[0])])
        prefetch()
        prefetch()
        g.greet()
        red = Reduce(g, scratch[23:], out, order)
        h1, h2, o2, h3, o1 = acts_in.at[0], acts_in.at[5], acts_in.at[7], acts_in.at[8], acts_in.at[4]
        operands = {}
        for j in range(ups):
            operands[g.down_at + j] = (mlp_in_acts.at[0, j], g_ref)
            operands[g.up_at + j] = (h3, dz_out.at[j])
        operands[cross_at] = (o2, gb_out.at[0])
        operands[3] = (h2, gq_out.at[0])
        operands[4] = (mem_ref, gkv_out.at[0])
        operands[5] = (mem_ref, gkv_out.at[1])
        operands[first] = (o1, gb_out.at[1])
        for i in range(3):
            operands[i] = (h1, gq_out.at[1 + i])
        saver = Saver(osem)
        ready = {u: () for u in range(g.down_at, units)}
        cursor = [0]

        loaded = {}

        def operand_copies(q):
            left, right = operands[order[q]]
            count = left.shape[0]
            return count, [
                pltpu.make_async_copy(left, lhs.at[pl.ds(0, count), :], opsem.at[0]),
                pltpu.make_async_copy(right, rhs.at[pl.ds(0, count), :], opsem.at[1]),
            ]

        def load_operands(q):
            if q < units and q not in loaded and order[q] in ready:
                loaded[q] = True
                for at in ready[order[q]]:
                    saver.wait(at)
                for copy in operand_copies(q)[1]:
                    copy.start()

        def produce(q):
            load_operands(q)
            assert loaded[q]
            count, copies = operand_copies(q)
            for copy in copies:
                copy.wait()
            red.sent("C", q - red.slots)
            slot = q % red.slots
            blocks = (width // 2) // g.rows

            def block(i):
                cols = pl.ds(pl.multiple_of(i * (width // 2), width // 2), width // 2)
                value = dot_tn(lhs[pl.ds(0, count), cols], rhs[pl.ds(0, count), :])
                red.gbuf[slot, pl.ds(i * blocks, blocks)] = value.astype(BF16).reshape(blocks, g.rows, width)

            over(2, block)
            load_operands(q + 1)

        def step():
            s = cursor[0]
            cursor[0] += 1
            if s < units:
                produce(s)
            for i, q in red.due(s):
                red.event(i, q)

        def looped(count, body, hooks):
            def inner(i):
                body(i)
                for at in hooks:
                    @pl.when(i == at)
                    def _():
                        step()

            over(count, inner)

        def gain(i):
            return vec[pl.ds(i, 1), :]

        def column_sum(ref, row, count=tokens, tile=64):
            def body(i, total):
                part = ref[pl.ds(pl.multiple_of(i * tile, tile), tile), :].astype(F32)
                return total + jnp.sum(part, axis=0, keepdims=True)

            sums[pl.ds(row, 1), :] = lax.fori_loop(0, count // tile, body, jnp.zeros((1, width), F32))

        def norm_back(read_x, read_base, gain_at, shift_at, base_shift, low, write):
            tile = 64

            def body(i, totals):
                rows = pl.ds(pl.multiple_of(i * tile, tile), tile)
                grad = acc[rows, :]
                unit, factor = normalized(read_x(rows))
                d_unit = grad * gain(gain_at)
                mean = jnp.mean(d_unit, axis=-1, keepdims=True)
                along = jnp.mean(d_unit * unit, axis=-1, keepdims=True)
                total = read_base(rows) + factor * (d_unit - mean - unit * along)
                write(rows, total)
                if low is not None:
                    low[rows, :] = total.astype(BF16)
                return (
                    totals[0] + jnp.sum(grad * unit, axis=0, keepdims=True),
                    totals[1] + jnp.sum(grad, axis=0, keepdims=True),
                    totals[2] + jnp.sum(total, axis=0, keepdims=True),
                )

            zero = jnp.zeros((1, width), F32)
            d_gain, d_shift, d_base = lax.fori_loop(0, tokens // tile, body, (zero, zero, zero))
            sums[pl.ds(gain_at, 1), :] = d_gain
            sums[pl.ds(3 + shift_at, 1), :] = d_shift
            if base_shift is not None:
                sums[pl.ds(3 + base_shift, 1), :] = d_base

        def back_project(grad, u, begin, tile=512):
            w = weight(u)

            def body(cols):
                value = dot_nt(grad[...], w[cols, :])
                acc[:, cols] = value if begin else acc[:, cols] + value

            tiles(width, tile, body)
            prefetch()

        def branch_grad(w, low, cols):
            do[:, cols] = dot_nt(low[...], w[cols, :]).astype(BF16)

        small_open = []

        def small_copy(at, src, dst, peer):
            copy = remote(src, dst, ssend.at[at], srecv.at[at], peer)
            copy.start()
            small_open.append(copy)
            return copy

        def small_stages():
            spots = [pl.ds(pl.multiple_of(g.z_of(k) * g.rows, g.rows), g.rows) for k in range(n)]
            copies = [small_copy(k - 1, sums.at[:, spots[k]], zsmall.at[n - k - 1], g.z_peer(k)) for k in range(1, n)]
            yield
            for copy in copies:
                copy.wait_recv()
            total = sums[:, spots[0]]
            for k in range(n - 1):
                total = total + zsmall[k]
            tsmall[0] = total
            copy = small_copy(n - 1, tsmall.at[0], core_small, g.other_core)
            yield
            copy.wait_recv()
            tsmall[1] = tsmall[0] + core_small[...]
            copy = small_copy(n, tsmall.at[1], b_small, g.b_peer)
            yield
            copy.wait_recv()
            tsmall[2] = tsmall[1] + b_small[...]
            a_small[g.a] = tsmall[2]
            copies = [small_copy(n + i, tsmall.at[2], a_small.at[g.a], g.a_peer(i)) for i in range(1, g.a_count)]
            yield
            for copy in copies:
                copy.wait_recv()
            total = a_small[0]
            for i in range(1, g.a_count):
                total = total + a_small[i]
            small_out[...] = total
            yield

        sums[...] = jnp.zeros_like(sums)
        step()
        step()
        step()
        wait(start)
        column_sum(gy, 3 + 9)
        for j in range(ups):
            w = weight(g.down_at + j)
            following = load([(mlp_in_acts.at[1, j + 1], slope[(j + 1) % 2])]) if j + 1 < ups else []

            def body(cols, j=j, w=w):
                value = (dot_nt(gy[...], w[cols, :]) * slope[j % 2][:, cols].astype(F32)).astype(BF16)
                dz[j][:, cols] = value
                sums[pl.ds(13 + j, 1), cols] = jnp.sum(value.astype(F32), axis=0, keepdims=True)

            tiles(width, 256, body)
            prefetch()
            at = saver.save(dz[j], dz_out.at[j])
            ready[g.up_at + j] = (at,)
            wait(following)
        load_x2 = pltpu.make_async_copy(xs_in.at[1], xbuf, lsem.at[6])
        load_x2.start()
        step()
        for j in range(ups):
            back_project(dz[j], g.up_at + j, j == 0)
        step()
        load_x2.wait()

        def put_dx(rows, total):
            dx[rows, :] = total

        gb = tile_o
        norm_back(lambda r: xbuf[r, :], lambda r: gy[r, :].astype(F32), 2, 8, 5, gb, put_dx)
        at = saver.save(gb, gb_out.at[0])
        ready[cross_at] = (at,)
        for j in range(ups):
            saver.wait(ready[g.up_at + j][0])
        loads = load([
            (xs_in.at[0], xbuf), (acts_in.at[6], tile_q), (kv_in.at[0], kv.at[0]), (kv_in.at[1], kv.at[1]),
        ])
        w = weight(cross_at)
        tiles(width, 512, functools.partial(branch_grad, w, gb))
        prefetch()
        step()
        saver.wait(at)
        wait(loads)
        wait(load([(o2, tile_o)]))
        second[...] = jnp.broadcast_to(second_image(seg_col, images, pl.ds(0, tokens)), second.shape)
        key_bias = jnp.where(lax.broadcasted_iota(jnp.int32, (1, per_image), 1) < mem_tokens, 0.0, MASKED)
        k2, v2 = kv.at[0], kv.at[1]
        looped(
            HEADS // 2,
            lambda i: cross_backward(i, tile_q, k2, v2, do, tile_o, second, key_bias, lse.at[1]),
            (1, 4, 6),
        )
        ready[4] = (saver.save(k2, gkv_out.at[0]),)
        ready[5] = (saver.save(v2, gkv_out.at[1]),)

        def scaled(src, dst, row):
            def body(i, total):
                rows = pl.ds(pl.multiple_of(i * 64, 64), 64)
                value = src[rows, :].astype(F32) * scale
                dst[rows, :] = value.astype(BF16)
                return total + jnp.sum(value, axis=0, keepdims=True)

            sums[pl.ds(row, 1), :] = lax.fori_loop(0, tokens // 64, body, jnp.zeros((1, width), F32))

        scaled(tile_q, gq, 3 + 3)
        ready[3] = (saver.save(gq, gq_out.at[0]),)
        back_project(gq, 3, True)
        step()
        column_sum(v2, 3 + 4, keys)
        w4 = weight(4)
        w5 = weight(5)
        mem_tile, mem_rows = 256, per_image
        spots = [(r, c) for r in range(keys // mem_rows) for c in range(width // mem_tile)]

        def gm_copy(i):
            r, c = spots[i]
            dst = dmem_out.at[pl.ds(r * mem_rows, mem_rows), pl.ds(c * mem_tile, mem_tile)]
            return pltpu.make_async_copy(gm.at[i % 2], dst, gmsem.at[i % 2])

        for i, (r, c) in enumerate(spots):
            rows, cols = pl.ds(r * mem_rows, mem_rows), pl.ds(c * mem_tile, mem_tile)
            if i >= 2:
                gm_copy(i - 2).wait()
            gm[i % 2] = dot_nt(k2[rows, :], w4[cols, :]) + dot_nt(v2[rows, :], w5[cols, :])
            gm_copy(i).start()
        for i in range(max(len(spots) - 2, 0), len(spots)):
            gm_copy(i).wait()
        prefetch()
        prefetch()
        step()
        gb = tile_o
        norm_back(lambda r: xbuf[r, :], lambda r: dx[r, :], 1, 7, 2, gb, put_dx)
        at = saver.save(gb, gb_out.at[1])
        ready[first] = (at,)
        for kind in (3, 4, 5):
            saver.wait(ready[kind][0])
        q1, k1, v1 = tile_q, kv.at[0, pl.ds(0, tokens)], kv.at[1, pl.ds(0, tokens)]
        loads = load([(acts_in.at[1], q1), (acts_in.at[2], k1), (acts_in.at[3], v1)])
        w = weight(first)
        tiles(width, 512, functools.partial(branch_grad, w, gb))
        prefetch()
        fill_self_bias(bias, seg_col, seg_row)
        step()
        saver.wait(at)
        wait(loads)
        wait(load([(o1, tile_o)]))
        looped(
            HEADS // 2,
            lambda i: self_backward(i, q1, k1, v1, do, tile_o, bias, lse.at[0]),
            (3,),
        )
        loads = load([(x_ref, tile_o)])
        scaled(q1, gq, 3 + 0)
        ready[0] = (saver.save(gq, gq_out.at[1]),)
        ready[1] = (saver.save(k1, gq_out.at[2]),)
        ready[2] = (saver.save(v1, gq_out.at[3]),)
        step()
        step()
        step()
        column_sum(v1, 3 + 1)
        back_project(gq, 0, True)
        step()
        back_project(k1, 1, False)
        step()
        back_project(v1, 2, False)
        wait(loads)
        step()
        norm_back(lambda r: tile_o[r, :].astype(F32), lambda r: dx[r, :], 0, 6, None, None, put_dx)
        saver.save(dx, dx_out)
        small = small_stages()
        next(small)
        while cursor[0] < red.last:
            step()
            next(small, None)
        for _ in small:
            pass
        saver.finish()
        red.finish()
        for copy in small_open:
            copy.wait_send()

    small_steps = n - 1 + 2 + max(geo.a_count - 1, 1)
    dma = pltpu.SemaphoreType.DMA
    tile = (tokens, width)
    return pl.pallas_call(
        kernel,
        out_shape=[
            b16((units, geo.rows, width)),
            f32(tile),
            f32((keys, width)),
            f32((SMALL, geo.rows)),
            b16((ups,) + tile),
            b16((2,) + tile),
            b16((4,) + tile),
            b16((2, keys, width)),
        ],
        in_specs=[HBM] * 3 + [VMEM, VMEM, SMEM] + [HBM] * 9 + [VMEM] * 2,
        out_specs=[HBM] * 3 + [VMEM] + [HBM] * 4,
        scratch_shapes=[
            pltpu.VMEM((2, width, width), BF16),
            pltpu.VMEM((keys, width), BF16),
            pltpu.VMEM((keys, width), BF16),
            pltpu.VMEM((5,) + tile, BF16),
            pltpu.VMEM((2, keys, width), BF16),
            pltpu.VMEM((2,) + tile, F32),
            pltpu.VMEM(tile, F32),
            pltpu.VMEM((2, per_image, width // 4), F32),
            pltpu.VMEM((tokens, tokens), F32),
            pltpu.VMEM((tokens, 128), jnp.int32),
            pltpu.VMEM((SMALL, width), F32),
            pltpu.VMEM((n - 1, SMALL, geo.rows), F32),
            pltpu.VMEM((3, SMALL, geo.rows), F32),
            pltpu.VMEM((SMALL, geo.rows), F32),
            pltpu.VMEM((SMALL, geo.rows), F32),
            pltpu.VMEM((geo.a_count, SMALL, geo.rows), F32),
            dma((2, 2 * n)),
            dma((8,)),
            dma((32,)),
            dma((2,)),
            dma((2,)),
            dma((small_steps,)),
            dma((small_steps,)),
        ]
        + Reduce.scratch(geo),
        compiler_params=pltpu.CompilerParams(
            collective_id=1, has_side_effects=True, vmem_limit_bytes=60 * MIB
        ),
    )(
        tokens_in, cotangent, memory, seg_col, seg_row, images, attn_in, attn_out, mlp_in, mlp_out,
        ring, acts, kv_acts, mlp_acts, xs, lse_all, vectors,
    )


def finish(geo, total, dmem, dx, layer_out, mem_tokens):
    units, rows, width = total.shape
    n, ups = geo.narrow, geo.n_up
    images, per_image = dmem.shape[:2]
    tokens = dx.shape[0]
    span, lot = width // (units // images), tokens // units

    def kernel(total_ref, dmem_ref, dx_ref, low_ref, attn_in, attn_out, up, down, dmem_out, dx_out, low_out):
        u = pl.program_id(0)
        value = total_ref[0].astype(F32)

        @pl.when(u < geo.n_in)
        def _():
            attn_in[0] = value

        @pl.when((u >= geo.n_in) & (u < geo.up_at))
        def _():
            attn_out[0] = value

        @pl.when((u >= geo.up_at) & (u < geo.down_at))
        def _():
            for k in range(n):
                start = pl.multiple_of((k * ups + u - geo.up_at) * rows, rows)
                up[:, pl.ds(start, rows)] = value[:, k * rows : (k + 1) * rows]

        @pl.when(u >= geo.down_at)
        def _():
            down[...] = value

        dmem_out[0] = dmem_ref[0, :mem_tokens, :]
        dx_out[...] = dx_ref[...]
        low_out[...] = low_ref[...]

    def unit_at(first, count):
        return lambda u: (jnp.clip(u - first, 0, count - 1), 0, 0)

    def image_at(u):
        return (u // (units // images), 0, lax.rem(u, units // images))

    shape = jax.ShapeDtypeStruct
    per_lot = pl.BlockSpec((lot, width), lambda u: (u, 0))
    return pl.pallas_call(
        kernel,
        grid=(units,),
        out_shape=[
            shape((geo.n_in, rows, width), F32),
            shape((geo.n_out, rows, width), F32),
            shape((rows, ups * width), F32),
            shape((ups * rows, width), F32),
            shape((images, mem_tokens, width), F32),
            shape((tokens, width), F32),
            shape((tokens, width), BF16),
        ],
        in_specs=[
            pl.BlockSpec((1, rows, width), lambda u: (u, 0, 0)),
            pl.BlockSpec((1, per_image, span), image_at),
            per_lot,
            per_lot,
        ],
        out_specs=[
            pl.BlockSpec((1, rows, width), unit_at(0, geo.n_in)),
            pl.BlockSpec((1, rows, width), unit_at(geo.n_in, geo.n_out)),
            pl.BlockSpec((rows, ups * width), lambda u: (0, 0)),
            pl.BlockSpec((rows, width), lambda u: (jnp.clip(u - geo.down_at, 0, ups - 1), 0)),
            pl.BlockSpec((1, mem_tokens, span), image_at),
            per_lot,
            per_lot,
        ],
        compiler_params=pltpu.CompilerParams(vmem_limit_bytes=40 * MIB),
    )(total, dmem, dx, layer_out)


def per_device(
    mesh, hidden_in, memory, segment_ids, image_ids, attn_in, attn_out, mlp_in, mlp_out, gains, shifts, mlp_bias,
    cotangent,
):
    width = hidden_in.shape[2]
    n_in, n_out = attn_in.shape[0], attn_out.shape[0]
    geo = Geometry(mesh, width, n_in, n_out, mlp_in.shape[1])
    rows, n = geo.rows, geo.narrow
    images, mem_tokens = memory.shape[1], memory.shape[2]
    per_image = -(-mem_tokens // 128) * 128
    padded = jnp.pad(memory[0], ((0, 0), (0, per_image - mem_tokens), (0, 0))).reshape(images * per_image, width)
    small = jnp.concatenate([gains, shifts, mlp_bias.reshape(geo.n_up, rows)], axis=0).astype(F32)
    used = small.shape[0]
    small = jnp.pad(small, ((0, SMALL - used), (0, 0)))
    seg_col, seg_row = segment_ids.reshape(-1, 1), segment_ids
    ring, layer_out, acts, kv, mlp_acts, xs, lse, vec = forward(
        geo, hidden_in[0], padded, mem_tokens, seg_col, seg_row, image_ids, attn_in, attn_out, mlp_in, mlp_out, small
    )
    total, dx, dmem, small_total, *_ = backward(
        geo, mem_tokens, hidden_in[0], cotangent[0], padded, seg_col, seg_row, image_ids, attn_in, attn_out, mlp_in, mlp_out,
        (ring, acts, kv, mlp_acts, xs, lse, vec),
    )
    big = finish(geo, total, dmem.reshape(images, per_image, width), dx, layer_out, mem_tokens)
    return (
        big[6][None], big[5][None], big[4][None], big[0], big[1], big[2], big[3],
        small_total[:3], small_total[3:13], small_total[13:used].reshape(-1),
    )


def solution(mesh):
    split = ("wide", "narrow")
    return jax.shard_map(
        functools.partial(per_device, mesh),
        mesh=mesh,
        in_specs=(
            P(split, None, None), P(split, None, None, None), P(split, None), P(split, None), P(None, "narrow", None),
            P(None, "narrow", None), P("narrow", None), P("narrow", None), P(None, "narrow"), P(None, "narrow"),
            P("narrow"), P(split, None, None),
        ),
        out_specs=(
            P(split, None, None), P(split, None, None), P(split, None, None, None), P(None, "narrow", None),
            P(None, "narrow", None), P("narrow", None), P("narrow", None), P(None, "narrow"), P(None, "narrow"),
            P("narrow"),
        ),
        check_vma=False,
    )
```

```python
import functools

import jax
import jax.numpy as jnp
from jax import lax
from jax.experimental import pallas as pl
from jax.experimental.pallas import tpu as pltpu
from jax.sharding import PartitionSpec as P

HEADS = 16
MESH = pl.DeviceIdType.MESH
F32 = jnp.float32
BF16 = jnp.bfloat16
MIB = 1 << 20
EPS = 1e-5
MASKED = -1e30
SMALL = 24
ROOT_HALF = 0.7071067811865476
ROOT_TWO_PI = 0.3989422804014327
HBM = pl.BlockSpec(memory_space=pltpu.HBM)
VMEM = pl.BlockSpec(memory_space=pltpu.VMEM)
SMEM = pl.BlockSpec(memory_space=pltpu.SMEM)


class Geometry:
    def __init__(self, mesh, width, n_in, n_out, hidden):
        self.wide = mesh.shape["wide"]
        self.narrow = mesh.shape["narrow"]
        self.a_count = self.wide // 4
        self.width = width
        self.rows = width // self.narrow
        self.core_rows = self.rows // 2
        self.piece_rows = self.core_rows // self.a_count
        self.half = width // 2
        self.quarter = width // 4
        self.n_in, self.n_out, self.n_up = n_in, n_out, hidden // width
        self.up_at = n_in + n_out
        self.down_at = self.up_at + self.n_up
        self.units = self.down_at + self.n_up

    def place(self):
        w = lax.axis_index("wide")
        n = lax.axis_index("narrow")
        self.w, self.n = w, n
        self.a, self.b, self.c = w // 4, lax.rem(w // 2, 2), lax.rem(w, 2)
        self.core_at = pl.multiple_of(self.c * self.core_rows, self.core_rows)
        self.b_at = pl.multiple_of(self.b * self.quarter, self.quarter)
        self.mine = pl.multiple_of(self.c * self.core_rows + self.a * self.piece_rows, self.piece_rows)
        self.other_core = (w + 1 - 2 * self.c, n)
        self.b_peer = (w + 2 - 4 * self.b, n)

    def a_of(self, step):
        return lax.rem(self.a + step, self.a_count)

    def a_peer(self, step):
        return (self.w + 4 * (self.a_of(step) - self.a), self.n)

    def z_of(self, step):
        return lax.rem(self.n + step, self.narrow)

    def z_peer(self, step):
        return (self.w, self.z_of(step))

    def greet(self):
        barrier = pltpu.get_barrier_semaphore()
        peers = [self.other_core, self.b_peer]
        peers += [self.a_peer(i) for i in range(1, self.a_count)]
        peers += [self.z_peer(i) for i in range(1, self.narrow)]
        for peer in peers:
            pl.semaphore_signal(barrier, inc=1, device_id=peer, device_id_type=MESH)
        pl.semaphore_wait(barrier, len(peers))


def remote(src, dst, send, recv, peer):
    return pltpu.make_async_remote_copy(
        src_ref=src, dst_ref=dst, send_sem=send, recv_sem=recv, device_id=peer, device_id_type=MESH
    )


class Shard:
    def __init__(self, geo, attn_in, attn_out, up, down):
        self.geo, self.attn_in, self.attn_out, self.up, self.down = geo, attn_in, attn_out, up, down

    def parts(self, u, row, rows, col, cols):
        g = self.geo
        at = pl.ds(row, rows)
        if u < g.n_in:
            return [(self.attn_in.at[u, at, pl.ds(col, cols)], 0, cols)]
        if u < g.up_at:
            return [(self.attn_out.at[u - g.n_in, at, pl.ds(col, cols)], 0, cols)]
        if u < g.down_at:
            j, out = u - g.up_at, []
            for p in range(cols // g.rows):
                start = (col // g.rows + p) * (g.n_up * g.rows) + j * g.rows
                if not isinstance(start, int):
                    start = pl.multiple_of(start, g.rows)
                out.append((self.up.at[at, pl.ds(start, g.rows)], p * g.rows, g.rows))
            return out
        start = (u - g.down_at) * g.rows + row
        if not isinstance(start, int):
            start = pl.multiple_of(start, g.piece_rows)
        return [(self.down.at[pl.ds(start, rows), pl.ds(col, cols)], 0, cols)]


class Gather:
    def __init__(self, geo, shard, ring, send, recv):
        self.geo, self.shard, self.ring, self.send, self.recv = geo, shard, ring, send, recv
        self.open = []

    lags = (0, 1, 3, 4)

    @staticmethod
    def z_sems(geo):
        return 2 * (geo.narrow - 1) * (geo.quarter // geo.rows)

    @classmethod
    def sems(cls, geo):
        return cls.z_sems(geo) + 2 * geo.a_count + 1

    def copies(self, kind, u):
        g = self.geo

        def copy(slot, src, dst, peer):
            return remote(src, dst, self.send.at[u, slot], self.recv.at[u, slot], peer)

        mine = pl.ds(g.mine, g.piece_rows)
        low_b = pl.ds(g.b_at, g.quarter)
        high_b = pl.ds(pl.multiple_of(g.half + g.b_at, g.quarter), g.quarter)
        core = pl.ds(g.core_at, g.core_rows)
        if kind == 0:
            out = []
            for k in range(1, g.narrow):
                for start in (low_b.start, high_b.start):
                    for src, col, cols in self.shard.parts(u, g.mine, g.piece_rows, start, g.quarter):
                        cols = pl.ds(pl.multiple_of(start + col, g.rows), cols)
                        dst = self.ring.at[u, g.narrow - k - 1, mine, cols]
                        out.append(copy(len(out), src, dst, g.z_peer(k)))
            return out
        base = self.z_sems(g)
        steps = range(1, g.a_count)
        if kind == 1:
            low = self.ring.at[u, :, mine, low_b]
            high = self.ring.at[u, :, mine, high_b]
            out = [copy(base + i - 1, low, low, g.a_peer(i)) for i in steps]
            return out + [copy(base + g.a_count - 1, high, high, g.b_peer)]
        base += g.a_count
        if kind == 2:
            low = self.ring.at[u, :, core, low_b]
            high = self.ring.at[u, :, mine, pl.ds(g.half, g.half)]
            out = [copy(base + i - 1, high, high, g.a_peer(i)) for i in steps]
            return out + [copy(base + g.a_count - 1, low, low, g.b_peer)]
        part = self.ring.at[u, :, core, :]
        return [copy(base + g.a_count, part, part, g.other_core)]

    def event(self, kind, u):
        if kind > 0:
            for copy in self.copies(kind - 1, u):
                copy.wait_recv()
        if kind < 4:
            for copy in self.copies(kind, u):
                copy.start()
            self.open.append((kind, u))

    def finish(self):
        for kind, u in self.open:
            for copy in self.copies(kind, u):
                copy.wait_send()


def add_rows(dst, parts, tile):
    count, rows = dst.shape[0], dst.shape[1]
    tile = min(tile, rows)
    per = rows // tile

    def body(i, carry):
        k, r = i // per, pl.multiple_of(lax.rem(i, per) * tile, tile)
        total = parts[0](k, r, tile).astype(F32)
        for part in parts[1:]:
            total = total + part(k, r, tile).astype(F32)
        dst[k, pl.ds(r, tile), :] = total.astype(dst.dtype)
        return carry

    lax.fori_loop(0, count * per, body, 0)


class Reduce:
    slots = 2
    held = 3
    landing = 6
    late = 4
    early = (3, 8)
    stages = ("C", "P1", "P2", "Z", "Q1", "Q2", "QC")
    stages_early = ("C", "Z", "P1", "P2", "Q1", "Q2", "QC")
    steps = (0, 1, 3, 5, 8, 9, 10, 11)
    steps_early = (0, 1, 6, 8, 10, 11, 12, 13)

    def __init__(self, geo, bufs, out, order):
        self.geo, self.out, self.order = geo, out, order
        names = [name for name, _ in self.shapes(geo)]
        self.bufs = dict(zip(names, bufs))
        self.gbuf = self.bufs["gbuf"]
        self.send, self.recv, self.local, self.credit = bufs[len(names) :]
        self.open = set()

    @classmethod
    def shapes(cls, geo):
        g, n, w = geo, geo.narrow, geo.width
        peers = max(g.a_count - 1, 1)
        r, c, p, h, q = g.rows, g.core_rows, g.piece_rows, g.half, g.quarter
        out = [("gbuf", (cls.slots, n, r, w)), ("rc", (cls.slots, n, c, w)), ("fin", (cls.slots, p, h))]
        for tag, count, many, m in (("", cls.held, cls.landing, n), ("e", len(cls.early), len(cls.early), 1)):
            out += [
                ("s1" + tag, (count, m, c, w)),
                ("s2a" + tag, (count, m, p, h)),
                ("s2b" + tag, (count, m, c, q)),
                ("p1a" + tag, (many, peers, m, p, h)),
                ("p1b" + tag, (many, m, c, q)),
                ("p2a" + tag, (many, m, p, q)),
                ("p2b" + tag, (many, peers, m, p, q)),
                ("s3" + tag, (max(count, cls.late), m, p, h)),
            ]
        early = len(cls.early)
        out += [("zr", (geo.units, n - 1, p, h)), ("zre", (early, n - 1, c, w)), ("s0e", (early, n, c, w))]
        return out

    @classmethod
    def scratch(cls, geo):
        count = 1 + 4 * geo.a_count + (geo.narrow - 1) + 1
        return [pltpu.VMEM(shape, BF16) for _, shape in cls.shapes(geo)] + [
            pltpu.SemaphoreType.DMA((geo.units, count)),
            pltpu.SemaphoreType.DMA((geo.units, count)),
            pltpu.SemaphoreType.DMA((2,)),
            pltpu.SemaphoreType.REGULAR,
        ]

    def buf(self, name, q):
        if q in self.early and name not in ("rc", "fin"):
            return self.bufs[name + "e"].at[self.early.index(q)]
        ref = self.bufs[name]
        return ref.at[q % ref.shape[0]]

    def stage(self, q, i):
        return (self.stages_early if q in self.early else self.stages)[i]

    def due(self, s):
        out = []
        for i in range(8):
            for q in range(self.geo.units):
                if q + (self.steps_early if q in self.early else self.steps)[i] == s:
                    out.append((i, q))
        return out

    @property
    def last(self):
        units = self.geo.units
        return max(units + self.steps[-1], max(self.early, default=0) + self.steps_early[-1] + 1)

    def copies(self, stage, q):
        g = self.geo
        u = self.order[q]
        na = g.a_count
        steps = range(1, na)
        mine = pl.ds(g.mine, g.piece_rows)
        core = pl.ds(g.core_at, g.core_rows)
        low_b = pl.ds(g.b_at, g.quarter)
        high_b = pl.ds(pl.multiple_of(g.half + g.b_at, g.quarter), g.quarter)
        peer_b = pl.multiple_of((1 - g.b) * g.quarter, g.quarter)

        def copy(s, src, dst, peer):
            return remote(src, dst, self.send.at[q, s], self.recv.at[q, s], peer)

        def in_core(a):
            return pl.ds(pl.multiple_of(a * g.piece_rows, g.piece_rows), g.piece_rows)

        if stage == "C":
            other = pl.ds(pl.multiple_of((1 - g.c) * g.core_rows, g.core_rows), g.core_rows)
            return [copy(0, self.gbuf.at[q % self.slots, :, other, :], self.buf("rc", q), g.other_core)]
        if stage == "P1":
            s1 = self.buf("s1", q)
            out = [
                copy(i, s1.at[:, in_core(g.a_of(i)), pl.ds(0, g.half)], self.buf("p1a", q).at[na - i - 1], g.a_peer(i))
                for i in steps
            ]
            cols = pl.ds(pl.multiple_of(g.half + peer_b, g.quarter), g.quarter)
            return out + [copy(na, s1.at[:, :, cols], self.buf("p1b", q), g.b_peer)]
        if stage == "P2":
            s2a, s2b = self.buf("s2a", q), self.buf("s2b", q)
            out = [
                copy(na + i, s2b.at[:, in_core(g.a_of(i)), :], self.buf("p2b", q).at[na - i - 1], g.a_peer(i))
                for i in steps
            ]
            return out + [copy(2 * na, s2a.at[:, :, pl.ds(peer_b, g.quarter)], self.buf("p2a", q), g.b_peer)]
        if stage == "Z":
            src, dst = (self.buf("s0", q) if q in self.early else self.buf("s3", q)), self.buf("zr", q)
            return [
                copy(2 * na + k, src.at[g.z_of(k)], dst.at[g.narrow - k - 1], g.z_peer(k)) for k in range(1, g.narrow)
            ]
        base = 2 * na + g.narrow
        if stage == "Q1":
            low, high = self.out.at[u, mine, low_b], self.out.at[u, mine, high_b]
            out = [copy(base + i - 1, low, low, g.a_peer(i)) for i in steps]
            return out + [copy(base + na - 1, high, high, g.b_peer)]
        base += na
        if stage == "Q2":
            low, high = self.out.at[u, core, low_b], self.out.at[u, mine, pl.ds(g.half, g.half)]
            out = [copy(base + i - 1, high, high, g.a_peer(i)) for i in steps]
            return out + [copy(base + na - 1, low, low, g.b_peer)]
        part = self.out.at[u, core, :]
        return [copy(base + na, part, part, g.other_core)]

    def begin(self, stage, q):
        for copy in self.copies(stage, q):
            copy.start()
        self.open.add((stage, q))

    def sent_before(self, stage, q, turn):
        if q not in self.early:
            for earlier in range(q % turn, q, turn):
                if earlier not in self.early:
                    self.sent(stage, earlier)

    def sent(self, stage, q):
        if (stage, q) in self.open:
            for copy in self.copies(stage, q):
                copy.wait_send()
            self.open.remove((stage, q))

    def event(self, i, q):
        g = self.geo
        if i == 0:
            if q >= self.slots:
                pl.semaphore_wait(self.credit, 1)
            self.begin("C", q)
            return
        done = self.stage(q, i - 1)
        for copy in self.copies(done, q):
            copy.wait_recv()
        self.combine(done, q)
        if i < 7:
            self.begin(self.stage(q, i), q)

    def combine(self, done, q):
        g = self.geo
        na = g.a_count
        early = q in self.early
        own = pl.multiple_of(g.a * g.piece_rows, g.piece_rows)
        low_b = pl.ds(g.b_at, g.quarter)
        high_b = pl.ds(pl.multiple_of(g.half + g.b_at, g.quarter), g.quarter)
        if done == "C":
            self.sent_before("P1", q, self.held)
            gbuf, rc = self.gbuf.at[q % self.slots], self.buf("rc", q)
            add_rows(
                self.buf("s0" if early else "s1", q),
                [
                    lambda k, r, t: gbuf[k, pl.ds(pl.multiple_of(g.core_at + r, 16), t), :],
                    lambda k, r, t: rc[k, pl.ds(r, t), :],
                ],
                32,
            )
            if q + self.slots < g.units:
                pl.semaphore_signal(self.credit, inc=1, device_id=g.other_core, device_id_type=MESH)
        elif done == "P1":
            self.sent_before("P2", q, self.held)
            s1, p1a, p1b = self.buf("s1", q), self.buf("p1a", q), self.buf("p1b", q)
            add_rows(
                self.buf("s2a", q),
                [lambda k, r, t: s1[k, pl.ds(pl.multiple_of(own + r, 16), t), pl.ds(0, g.half)]]
                + [lambda k, r, t, i=i: p1a[i, k, pl.ds(r, t), :] for i in range(na - 1)],
                64,
            )
            add_rows(
                self.buf("s2b", q),
                [lambda k, r, t: s1[k, pl.ds(r, t), high_b], lambda k, r, t: p1b[k, pl.ds(r, t), :]],
                128,
            )
        elif done == "P2":
            self.sent_before("Z", q, self.late)
            s2a, s2b, p2a, p2b, s3 = (self.buf(name, q) for name in ("s2a", "s2b", "p2a", "p2b", "s3"))
            add_rows(
                s3.at[:, :, pl.ds(0, g.quarter)],
                [lambda k, r, t: s2a[k, pl.ds(r, t), low_b], lambda k, r, t: p2a[k, pl.ds(r, t), :]],
                64,
            )
            add_rows(
                s3.at[:, :, pl.ds(g.quarter, g.quarter)],
                [lambda k, r, t: s2b[k, pl.ds(pl.multiple_of(own + r, 16), t), :]]
                + [lambda k, r, t, i=i: p2b[i, k, pl.ds(r, t), :] for i in range(na - 1)],
                64,
            )
            if early:
                self.place(s3.at[0], q)
        elif done == "Z":
            zr = self.buf("zr", q)
            if early:
                s0 = self.buf("s0", q)
                add_rows(
                    self.buf("s1", q),
                    [lambda k, r, t: s0[g.n, pl.ds(r, t), :]]
                    + [lambda k, r, t, i=i: zr[i, pl.ds(r, t), :] for i in range(g.narrow - 1)],
                    32,
                )
                return
            total = self.buf("s3", q)[g.n].astype(F32)
            for k in range(g.narrow - 1):
                total = total + zr[k].astype(F32)
            fin = self.buf("fin", q)
            fin[...] = total.astype(BF16)
            self.place(fin, q)

    def place(self, piece, q):
        g, u = self.geo, self.order[q]
        stores = []
        for h in range(2):
            cols = pl.ds(pl.multiple_of(h * g.half + g.b_at, g.quarter), g.quarter)
            dst = self.out.at[u, pl.ds(g.mine, g.piece_rows), cols]
            src = piece.at[:, pl.ds(h * g.quarter, g.quarter)]
            stores.append(pltpu.make_async_copy(src, dst, self.local.at[h]))
        for store in stores:
            store.start()
        for store in stores:
            store.wait()

    def finish(self):
        for stage, q in sorted(self.open):
            for copy in self.copies(stage, q):
                copy.wait_send()
        self.open = set()


class Weights:
    def __init__(self, geo, shard, ring, buf, sem):
        self.geo, self.shard, self.ring, self.buf, self.sem = geo, shard, ring, buf, sem

    def copies(self, u, slot):
        g = self.geo
        out = []
        for k in range(g.narrow):
            parts = self.shard.parts(u, 0, g.rows, 0, g.width) if k == 0 else [(self.ring.at[u, k - 1], 0, g.width)]
            rows = pl.ds(pl.multiple_of(g.z_of(k) * g.rows, g.rows), g.rows)
            for src, col, cols in parts:
                dst = self.buf.at[slot, rows, pl.ds(col, cols)]
                out.append(pltpu.make_async_copy(src, dst, self.sem.at[slot, len(out)]))
        return out

    def start(self, u, slot):
        for copy in self.copies(u, slot):
            copy.start()

    def wait(self, u, slot):
        for copy in self.copies(u, slot):
            copy.wait()
        return self.buf.at[slot]


def dot_nn(left, right):
    return jnp.dot(left, right, preferred_element_type=F32)


def dot_nt(left, right):
    return lax.dot_general(left, right, (((1,), (1,)), ((), ())), preferred_element_type=F32)


def dot_tn(left, right):
    return lax.dot_general(left, right, (((0,), (0,)), ((), ())), preferred_element_type=F32)


def over(count, body):
    def step(i, carry):
        body(i)
        return carry

    lax.fori_loop(0, count, step, 0)


def tiles(total, tile, body):
    over(total // tile, lambda i: body(pl.ds(pl.multiple_of(i * tile, tile), tile)))


def normalized(x):
    centered = x - jnp.mean(x, axis=-1, keepdims=True)
    variance = jnp.mean(centered * centered, axis=-1, keepdims=True)
    scale = lax.rsqrt(variance + EPS)
    return centered * scale, scale


def pair_cols(i):
    return pl.ds(pl.multiple_of(i * 128, 128), 128)


def lane_half(rows):
    return lax.broadcasted_iota(jnp.int32, (rows, 128), 1) // 64


def keep_half(values, side, half):
    return jnp.where(side == half, values, jnp.zeros_like(values))


def put_lane(ref, rows, lane, column):
    lanes = lax.broadcasted_iota(jnp.int32, (column.shape[0], 128), 1)
    ref[rows, :] = jnp.where(lanes == lane, column, ref[rows, :])


def take_lane(ref, rows, lane):
    values = ref[rows, :]
    lanes = lax.broadcasted_iota(jnp.int32, values.shape, 1)
    return jnp.sum(jnp.where(lanes == lane, values, 0.0), axis=-1, keepdims=True)


def softmax(scores):
    top = jnp.max(scores, axis=-1, keepdims=True)
    expo = jnp.exp(scores - top)
    total = jnp.sum(expo, axis=-1, keepdims=True)
    return (expo * (1.0 / total)).astype(BF16), top + jnp.log(total)


def fill_self_bias(bias, seg_col, seg_row):
    tokens = bias.shape[0]

    def body(rows):
        count = rows.size
        query = rows.start + lax.broadcasted_iota(jnp.int32, (count, tokens), 0)
        key = lax.broadcasted_iota(jnp.int32, (count, tokens), 1)
        allowed = (seg_col[rows, :] == seg_row[...]) & (key <= query)
        bias[rows, :] = jnp.where(allowed, 0.0, MASKED)

    tiles(tokens, 128, body)


def second_image(seg_col, images, rows):
    pages = seg_col[rows, :]
    image = jnp.zeros_like(pages)
    for page in range(images.shape[1]):
        image = jnp.where(pages == page, images[0, page], image)
    return image


def self_forward(i, q, k, v, bias, o, lse):
    cols = pair_cols(i)
    tokens = q.shape[0]
    block = tokens // 2
    side = lane_half(block)
    for at in range(0, tokens, block):
        rows, keys = pl.ds(at, block), pl.ds(0, at + block)
        queries, key, value = q[rows, cols], k[keys, cols], v[keys, cols]
        mixed = []
        for half in range(2):
            scores = dot_nt(keep_half(queries, side, half), key) + bias[rows, keys]
            probs, total = softmax(scores)
            put_lane(lse, rows, 2 * i + half, total)
            mixed.append(dot_nn(probs, value))
        o[rows, cols] = jnp.where(side == 0, mixed[0], mixed[1]).astype(BF16)


def self_backward(i, q, k, v, do, o, bias, lse):
    cols = pair_cols(i)
    tokens = q.shape[0]
    block = tokens // 2
    side = lane_half(block)
    grads_k, grads_v, grads_q = [], [], []
    for at in range(0, tokens, block):
        rows, keys = pl.ds(at, block), pl.ds(0, at + block)
        queries, key, value, grad, mix = q[rows, cols], k[keys, cols], v[keys, cols], do[rows, cols], o[rows, cols]
        product = grad.astype(F32) * mix.astype(F32)
        parts, grad_k, grad_v = [], 0.0, 0.0
        for half in range(2):
            own_q, own_g = keep_half(queries, side, half), keep_half(grad, side, half)
            scores = dot_nt(own_q, key) + bias[rows, keys]
            probs = jnp.exp(scores - take_lane(lse, rows, 2 * i + half))
            inner = jnp.sum(keep_half(product, side, half), axis=-1, keepdims=True)
            slopes = (probs * (dot_nt(own_g, value) - inner)).astype(BF16)
            parts.append(dot_nn(slopes, key))
            grad_k = grad_k + dot_tn(slopes, own_q)
            grad_v = grad_v + dot_tn(probs.astype(BF16), own_g)
        grads_q.append((rows, jnp.where(side == 0, parts[0], parts[1])))
        grads_k.append(grad_k)
        grads_v.append(grad_v)
    low = pl.ds(0, block)
    high = pl.ds(block, block)
    k[low, cols] = (grads_k[0] + grads_k[1][:block]).astype(BF16)
    k[high, cols] = grads_k[1][block:].astype(BF16)
    v[low, cols] = (grads_v[0] + grads_v[1][:block]).astype(BF16)
    v[high, cols] = grads_v[1][block:].astype(BF16)
    for rows, grad in grads_q:
        q[rows, cols] = grad.astype(BF16)


def both_images(ref, cols):
    keys = ref.shape[0] // 2
    return jnp.concatenate([ref[pl.ds(0, keys), cols], ref[pl.ds(keys, keys), cols]], axis=1)


def by_image(values, second):
    zero = jnp.zeros_like(values)
    return jnp.concatenate([jnp.where(second, zero, values), jnp.where(second, values, zero)], axis=1)


def pick_image(values, second):
    return jnp.where(second, values[:, 128:], values[:, :128])


def cross_forward(i, q, k, v, second_at, key_bias, o, lse, block=256):
    cols = pair_cols(i)
    key, value = both_images(k, cols), both_images(v, cols)
    side = lane_half(block)
    for at in range(0, q.shape[0], block):
        rows = pl.ds(at, block)
        queries = q[rows, cols]
        second = second_at[rows, :] == 1
        mixed = []
        for half in range(2):
            scores = dot_nt(by_image(keep_half(queries, side, half), second), key) + key_bias
            probs, total = softmax(scores)
            put_lane(lse, rows, 2 * i + half, total)
            mixed.append(pick_image(dot_nn(probs, value), second))
        o[rows, cols] = jnp.where(side == 0, mixed[0], mixed[1]).astype(BF16)


def cross_backward(i, q, k, v, do, o, second_at, key_bias, lse, block=256):
    cols = pair_cols(i)
    key, value = both_images(k, cols), both_images(v, cols)
    side = lane_half(block)
    grad_k, grad_v, grads_q = 0.0, 0.0, []
    for at in range(0, q.shape[0], block):
        rows = pl.ds(at, block)
        queries, grad, mix = q[rows, cols], do[rows, cols], o[rows, cols]
        second = second_at[rows, :] == 1
        product = grad.astype(F32) * mix.astype(F32)
        parts = []
        for half in range(2):
            own_q = by_image(keep_half(queries, side, half), second)
            own_g = by_image(keep_half(grad, side, half), second)
            scores = dot_nt(own_q, key) + key_bias
            probs = jnp.exp(scores - take_lane(lse, rows, 2 * i + half))
            inner = jnp.sum(keep_half(product, side, half), axis=-1, keepdims=True)
            slopes = (probs * (dot_nt(own_g, value) - inner)).astype(BF16)
            parts.append(pick_image(dot_nn(slopes, key), second))
            grad_k = grad_k + dot_tn(slopes, own_q)
            grad_v = grad_v + dot_tn(probs.astype(BF16), own_g)
        grads_q.append((rows, jnp.where(side == 0, parts[0], parts[1])))
    keys = k.shape[0] // 2
    for ref, total in ((k, grad_k), (v, grad_v)):
        ref[pl.ds(0, keys), cols] = total[:, :128].astype(BF16)
        ref[pl.ds(keys, keys), cols] = total[:, 128:].astype(BF16)
    for rows, grad in grads_q:
        q[rows, cols] = grad.astype(BF16)


class Saver:
    def __init__(self, sems):
        self.sems, self.open, self.used = sems, {}, 0

    def save(self, src, dst):
        at = self.used
        self.used += 1
        pltpu.make_async_copy(src, dst, self.sems.at[at]).start()
        self.open[at] = (src, dst)
        return at

    def wait(self, at):
        if at in self.open:
            src, dst = self.open.pop(at)
            pltpu.make_async_copy(src, dst, self.sems.at[at]).wait()

    def finish(self):
        for at in list(self.open):
            self.wait(at)


def forward(geo, tokens_in, memory, mem_tokens, seg_col, seg_row, images, attn_in, attn_out, mlp_in, mlp_out, small):
    tokens, width = tokens_in.shape
    keys = memory.shape[0]
    units, n = geo.units, geo.narrow
    first, cross_at = geo.n_in, geo.n_in + 1
    order = [0, 1, 2, first, 3, 4, 5, cross_at] + list(range(geo.up_at, units))
    wslots = 4
    scale = (width // HEADS) ** -0.5
    ups = geo.n_up
    f32, b16 = functools.partial(jax.ShapeDtypeStruct, dtype=F32), functools.partial(jax.ShapeDtypeStruct, dtype=BF16)

    def kernel(
        x_ref, mem_ref, seg_col, seg_row, images, ai, ao, mi, mo, small_ref,
        ring, layer_out, acts_out, kv_out, mlp_out_acts, xs_out, lse_out, vec,
        wbuf, x0, xs, acc, acts, kv, mlp_acts, mem, bias, second, low_out, small_buf,
        gsend, grecv, ssend, srecv, wsem, lsem, osem,
    ):
        g = geo
        g.place()
        load_x = pltpu.make_async_copy(x_ref, x0, lsem.at[0])
        load_m = pltpu.make_async_copy(mem_ref, mem, lsem.at[1])
        load_x.start()
        load_m.start()

        g.greet()
        shard = Shard(g, ai, ao, mi, mo)
        gather = Gather(g, shard, ring, gsend, grecv)
        weights = Weights(g, shard, ring, wbuf, wsem)

        def small_copy(k):
            return remote(small_ref, small_buf.at[n - k - 1], ssend.at[k - 1], srecv.at[k - 1], g.z_peer(k))

        for k in range(1, n):
            small_copy(k).start()
        gather.event(0, order[0])
        gather.event(0, order[1])
        saver = Saver(osem)
        cursor = [0]
        used = [0]

        def step():
            s = cursor[0]
            cursor[0] += 1
            if s + 2 < units:
                gather.event(0, order[s + 2])
            for kind in range(1, 5):
                q = s - Gather.lags[kind - 1]
                if 0 <= q < units:
                    gather.event(kind, order[q])
                    if kind == 4:
                        assert q - wslots < used[0]
                        weights.start(order[q], q % wslots)

        def weight():
            q = used[0]
            while cursor[0] <= q + Gather.lags[3]:
                step()
            return weights.wait(order[q], q % wslots)

        def done():
            used[0] += 1

        def project(left, finish, tile=512, row_tile=640):
            w = weight()
            row_tile = min(row_tile, left.shape[0])
            tiles(width, tile, lambda cols: tiles(
                left.shape[0], row_tile, lambda rows: finish(dot_nn(left[rows, :], w[:, cols]), rows, cols)
            ))
            done()

        def looped(count, body, hooks):
            def inner(i):
                body(i)
                for at in hooks:
                    @pl.when(i == at)
                    def _():
                        step()

            over(count, inner)

        h1, q, k, v, o, h2, q2, o2, h3 = (acts.at[i] for i in range(9))
        for k_ in range(1, n):
            small_copy(k_).wait_recv()
        place_n = [small_ref] + [small_buf.at[i] for i in range(n - 1)]
        for i in range(n):
            vec[:, pl.ds(pl.multiple_of(g.z_of(i) * g.rows, g.rows), g.rows)] = place_n[i][...]

        def gain(i):
            return vec[pl.ds(i, 1), :]

        def shift(i, cols=slice(None)):
            return vec[pl.ds(3 + i, 1), cols]

        def norm(read, h, gain_at, shift_at):
            def body(rows):
                unit, _ = normalized(read(rows))
                h[rows, :] = (unit * gain(gain_at) + shift(shift_at)).astype(BF16)

            tiles(tokens, 64, body)

        fill_self_bias(bias, seg_col, seg_row)
        load_x.wait()
        step()
        norm(lambda rows: x0[rows, :].astype(F32), h1, 0, 6)
        second[...] = jnp.broadcast_to(second_image(seg_col, images, pl.ds(0, tokens)), second.shape)
        lse_out[...] = jnp.zeros_like(lse_out)

        def put(ref, shift_at=None, factor=None):
            def finish(value, rows, cols):
                if shift_at is not None:
                    value = value + shift(shift_at, cols)
                if factor is not None:
                    value = value * factor
                ref[rows, cols] = value.astype(BF16)

            return finish

        def save_act(i):
            saver.save(acts.at[i], acts_out.at[i])

        project(h1, put(q, 0, scale))
        project(h1, put(k))
        project(h1, put(v, 1))
        for i in range(4):
            save_act(i)
        self_lse, cross_lse = lse_out.at[0], lse_out.at[1]
        looped(HEADS // 2, lambda i: self_forward(i, q, k, v, bias, o, self_lse), (2, 6))
        save_act(4)
        x1, x2 = xs.at[0], xs.at[1]

        def after_self(value, rows, cols):
            x1[rows, cols] = x0[rows, cols].astype(F32) + value + shift(2, cols)

        project(o, after_self)
        saver.save(x1, xs_out.at[0])
        norm(lambda rows: x1[rows, :], h2, 1, 7)
        save_act(5)
        project(h2, put(q2, 3, scale))
        save_act(6)
        load_m.wait()
        k2, v2 = kv.at[0], kv.at[1]
        project(mem, put(k2))
        project(mem, put(v2, 4))
        saver.save(k2, kv_out.at[0])
        saver.save(v2, kv_out.at[1])
        per_image = keys // 2
        key_bias = jnp.where(lax.broadcasted_iota(jnp.int32, (1, per_image), 1) < mem_tokens, 0.0, MASKED)
        looped(
            HEADS // 2, lambda i: cross_forward(i, q2, k2, v2, second, key_bias, o2, cross_lse), (1, 4, 6)
        )
        save_act(7)

        def after_cross(value, rows, cols):
            x2[rows, cols] = x1[rows, cols] + value + shift(5, cols)

        project(o2, after_cross)
        saver.save(x2, xs_out.at[1])
        norm(lambda rows: x2[rows, :], h3, 2, 8)
        save_act(8)
        for j in range(ups):
            def activate(value, rows, cols, j=j):
                z = value + vec[pl.ds(13 + j, 1), cols]
                cdf = 0.5 + 0.5 * lax.erf(z * ROOT_HALF)
                mlp_acts[0, j, rows, cols] = (z * cdf).astype(BF16)
                slope = cdf + z * (jnp.exp(-0.5 * z * z) * ROOT_TWO_PI)
                mlp_acts[1, j, rows, cols] = slope.astype(BF16)

            project(h3, activate, 256)
            saver.save(mlp_acts.at[0, j], mlp_out_acts.at[0, j])
            saver.save(mlp_acts.at[1, j], mlp_out_acts.at[1, j])
        for j in range(ups):
            def add(value, rows, cols, j=j):
                base = x2[rows, cols] + shift(9, cols) if j == 0 else acc[rows, cols]
                if j < ups - 1:
                    acc[rows, cols] = base + value
                else:
                    low_out[rows, cols] = (base + value).astype(BF16)

            project(mlp_acts.at[0, j], add)
        saver.save(low_out, layer_out)
        while cursor[0] < units + Gather.lags[3]:
            step()
        saver.finish()
        gather.finish()
        for k_ in range(1, n):
            small_copy(k_).wait_send()

    count = Gather.sems(geo)
    dma = pltpu.SemaphoreType.DMA
    return pl.pallas_call(
        kernel,
        out_shape=[
            b16((units, n - 1, geo.rows, width)),
            b16((tokens, width)),
            b16((9, tokens, width)),
            b16((2, keys, width)),
            b16((2, ups, tokens, width)),
            f32((2, tokens, width)),
            f32((2, tokens, 128)),
            f32((SMALL, width)),
        ],
        in_specs=[HBM, HBM, VMEM, VMEM, SMEM, HBM, HBM, HBM, HBM, VMEM],
        out_specs=[HBM] * 6 + [VMEM] * 2,
        scratch_shapes=[
            pltpu.VMEM((wslots, width, width), BF16),
            pltpu.VMEM((tokens, width), BF16),
            pltpu.VMEM((2, tokens, width), F32),
            pltpu.VMEM((tokens, width), F32),
            pltpu.VMEM((9, tokens, width), BF16),
            pltpu.VMEM((2, keys, width), BF16),
            pltpu.VMEM((2, ups, tokens, width), BF16),
            pltpu.VMEM((keys, width), BF16),
            pltpu.VMEM((tokens, tokens), F32),
            pltpu.VMEM((tokens, 128), jnp.int32),
            pltpu.VMEM((tokens, width), BF16),
            pltpu.VMEM((n - 1, SMALL, geo.rows), F32),
            dma((units, count)),
            dma((units, count)),
            dma((n - 1,)),
            dma((n - 1,)),
            dma((wslots, 2 * n)),
            dma((2,)),
            dma((32,)),
        ],
        compiler_params=pltpu.CompilerParams(
            collective_id=0, has_side_effects=True, vmem_limit_bytes=58 * MIB
        ),
    )(tokens_in, memory, seg_col, seg_row, images, attn_in, attn_out, mlp_in, mlp_out, small)


def backward(geo, mem_tokens, tokens_in, cotangent, memory, seg_col, seg_row, images, attn_in, attn_out, mlp_in, mlp_out, saved):
    ring, acts, kv_acts, mlp_acts, xs, lse_all, vectors = saved
    tokens, width = cotangent.shape
    keys = memory.shape[0]
    units, n, ups = geo.units, geo.narrow, geo.n_up
    first, cross_at = geo.n_in, geo.n_in + 1
    order = list(range(geo.down_at, units)) + list(range(geo.up_at, geo.down_at))
    order += [cross_at, 3, 4, 5, first, 0, 1, 2]
    fetch = [geo.down_at + j for j in range(ups)] + [geo.up_at + j for j in range(ups)]
    fetch += [cross_at, 3, 4, 5, first, 0, 1, 2]
    scale = (width // HEADS) ** -0.5
    per_image = keys // 2
    f32, b16 = functools.partial(jax.ShapeDtypeStruct, dtype=F32), functools.partial(jax.ShapeDtypeStruct, dtype=BF16)

    def kernel(*refs):
        (
            x_ref, g_ref, mem_ref, seg_col, seg_row, images, ai, ao, mi, mo,
            ring, acts_in, kv_in, mlp_in_acts, xs_in, lse, vec,
            out, dx_out, dmem_out, small_out, dz_out, gb_out, gq_out, gkv_out,
        ) = refs[:25]
        scratch = list(refs[25:])
        (
            wbuf, lhs, rhs, pool, kv, dxs, xbuf, gm, bias, second, sums,
            zsmall, tsmall, core_small, b_small, a_small,
            wsem, lsem, osem, gmsem, opsem, ssend, srecv,
        ) = scratch[:23]
        g = geo
        g.place()
        gy, do, tile_q, tile_o, gq = (pool.at[i] for i in range(5))
        dz = [kv.at[j % 2, pl.ds(j // 2 * tokens, tokens)] for j in range(ups)]
        slope = [do, tile_q]
        acc, dx = dxs.at[0], dxs.at[1]

        def load(pairs):
            copies = [pltpu.make_async_copy(src, dst, lsem.at[i]) for i, (src, dst) in enumerate(pairs)]
            for copy in copies:
                copy.start()
            return copies

        def wait(copies):
            for copy in copies:
                copy.wait()

        shard = Shard(g, ai, ao, mi, mo)
        weights = Weights(g, shard, ring, wbuf, wsem)
        fetched = [0, 0]

        def prefetch():
            if fetched[0] < len(fetch):
                weights.start(fetch[fetched[0]], fetched[0] % 2)
                fetched[0] += 1

        def weight(u):
            at = fetched[1]
            assert fetch[at] == u
            fetched[1] += 1
            return weights.wait(u, at % 2)

        start = load([(g_ref, gy), (mlp_in_acts.at[1, 0], slope[0])])
        prefetch()
        prefetch()
        g.greet()
        red = Reduce(g, scratch[23:], out, order)
        h1, h2, o2, h3, o1 = acts_in.at[0], acts_in.at[5], acts_in.at[7], acts_in.at[8], acts_in.at[4]
        operands = {}
        for j in range(ups):
            operands[g.down_at + j] = (mlp_in_acts.at[0, j], g_ref)
            operands[g.up_at + j] = (h3, dz_out.at[j])
        operands[cross_at] = (o2, gb_out.at[0])
        operands[3] = (h2, gq_out.at[0])
        operands[4] = (mem_ref, gkv_out.at[0])
        operands[5] = (mem_ref, gkv_out.at[1])
        operands[first] = (o1, gb_out.at[1])
        for i in range(3):
            operands[i] = (h1, gq_out.at[1 + i])
        saver = Saver(osem)
        ready = {u: () for u in range(g.down_at, units)}
        cursor = [0]

        loaded = {}

        def operand_copies(q):
            left, right = operands[order[q]]
            count = left.shape[0]
            return count, [
                pltpu.make_async_copy(left, lhs.at[pl.ds(0, count), :], opsem.at[0]),
                pltpu.make_async_copy(right, rhs.at[pl.ds(0, count), :], opsem.at[1]),
            ]

        def load_operands(q):
            if q < units and q not in loaded and order[q] in ready:
                loaded[q] = True
                for at in ready[order[q]]:
                    saver.wait(at)
                for copy in operand_copies(q)[1]:
                    copy.start()

        def produce(q):
            load_operands(q)
            assert loaded[q]
            count, copies = operand_copies(q)
            for copy in copies:
                copy.wait()
            red.sent("C", q - red.slots)
            slot = q % red.slots
            blocks = (width // 2) // g.rows

            def block(i):
                cols = pl.ds(pl.multiple_of(i * (width // 2), width // 2), width // 2)
                value = dot_tn(lhs[pl.ds(0, count), cols], rhs[pl.ds(0, count), :])
                red.gbuf[slot, pl.ds(i * blocks, blocks)] = value.astype(BF16).reshape(blocks, g.rows, width)

            over(2, block)
            load_operands(q + 1)

        def step():
            s = cursor[0]
            cursor[0] += 1
            if s < units:
                produce(s)
            for i, q in red.due(s):
                red.event(i, q)

        def looped(count, body, hooks):
            def inner(i):
                body(i)
                for at in hooks:
                    @pl.when(i == at)
                    def _():
                        step()

            over(count, inner)

        def gain(i):
            return vec[pl.ds(i, 1), :]

        def column_sum(ref, row, count=tokens, tile=64):
            def body(i, total):
                part = ref[pl.ds(pl.multiple_of(i * tile, tile), tile), :].astype(F32)
                return total + jnp.sum(part, axis=0, keepdims=True)

            sums[pl.ds(row, 1), :] = lax.fori_loop(0, count // tile, body, jnp.zeros((1, width), F32))

        def norm_back(read_x, read_base, gain_at, shift_at, base_shift, low, write):
            tile = 64

            def body(i, totals):
                rows = pl.ds(pl.multiple_of(i * tile, tile), tile)
                grad = acc[rows, :]
                unit, factor = normalized(read_x(rows))
                d_unit = grad * gain(gain_at)
                mean = jnp.mean(d_unit, axis=-1, keepdims=True)
                along = jnp.mean(d_unit * unit, axis=-1, keepdims=True)
                total = read_base(rows) + factor * (d_unit - mean - unit * along)
                write(rows, total)
                if low is not None:
                    low[rows, :] = total.astype(BF16)
                return (
                    totals[0] + jnp.sum(grad * unit, axis=0, keepdims=True),
                    totals[1] + jnp.sum(grad, axis=0, keepdims=True),
                    totals[2] + jnp.sum(total, axis=0, keepdims=True),
                )

            zero = jnp.zeros((1, width), F32)
            d_gain, d_shift, d_base = lax.fori_loop(0, tokens // tile, body, (zero, zero, zero))
            sums[pl.ds(gain_at, 1), :] = d_gain
            sums[pl.ds(3 + shift_at, 1), :] = d_shift
            if base_shift is not None:
                sums[pl.ds(3 + base_shift, 1), :] = d_base

        def back_project(grad, u, begin, tile=512):
            w = weight(u)

            def body(cols):
                value = dot_nt(grad[...], w[cols, :])
                acc[:, cols] = value if begin else acc[:, cols] + value

            tiles(width, tile, body)
            prefetch()

        def branch_grad(w, low, cols):
            do[:, cols] = dot_nt(low[...], w[cols, :]).astype(BF16)

        small_open = []

        def small_copy(at, src, dst, peer):
            copy = remote(src, dst, ssend.at[at], srecv.at[at], peer)
            copy.start()
            small_open.append(copy)
            return copy

        def small_stages():
            spots = [pl.ds(pl.multiple_of(g.z_of(k) * g.rows, g.rows), g.rows) for k in range(n)]
            copies = [small_copy(k - 1, sums.at[:, spots[k]], zsmall.at[n - k - 1], g.z_peer(k)) for k in range(1, n)]
            yield
            for copy in copies:
                copy.wait_recv()
            total = sums[:, spots[0]]
            for k in range(n - 1):
                total = total + zsmall[k]
            tsmall[0] = total
            copy = small_copy(n - 1, tsmall.at[0], core_small, g.other_core)
            yield
            copy.wait_recv()
            tsmall[1] = tsmall[0] + core_small[...]
            copy = small_copy(n, tsmall.at[1], b_small, g.b_peer)
            yield
            copy.wait_recv()
            tsmall[2] = tsmall[1] + b_small[...]
            a_small[g.a] = tsmall[2]
            copies = [small_copy(n + i, tsmall.at[2], a_small.at[g.a], g.a_peer(i)) for i in range(1, g.a_count)]
            yield
            for copy in copies:
                copy.wait_recv()
            total = a_small[0]
            for i in range(1, g.a_count):
                total = total + a_small[i]
            small_out[...] = total
            yield

        sums[...] = jnp.zeros_like(sums)
        step()
        step()
        step()
        wait(start)
        column_sum(gy, 3 + 9)
        for j in range(ups):
            w = weight(g.down_at + j)
            following = load([(mlp_in_acts.at[1, j + 1], slope[(j + 1) % 2])]) if j + 1 < ups else []

            def body(cols, j=j, w=w):
                value = (dot_nt(gy[...], w[cols, :]) * slope[j % 2][:, cols].astype(F32)).astype(BF16)
                dz[j][:, cols] = value
                sums[pl.ds(13 + j, 1), cols] = jnp.sum(value.astype(F32), axis=0, keepdims=True)

            tiles(width, 256, body)
            prefetch()
            at = saver.save(dz[j], dz_out.at[j])
            ready[g.up_at + j] = (at,)
            wait(following)
            if j == ups // 2 - 1:
                step()
        load_x2 = pltpu.make_async_copy(xs_in.at[1], xbuf, lsem.at[6])
        load_x2.start()
        step()
        for j in range(ups):
            back_project(dz[j], g.up_at + j, j == 0)
        step()
        load_x2.wait()

        def put_dx(rows, total):
            dx[rows, :] = total

        gb = tile_o
        norm_back(lambda r: xbuf[r, :], lambda r: gy[r, :].astype(F32), 2, 8, 5, gb, put_dx)
        at = saver.save(gb, gb_out.at[0])
        ready[cross_at] = (at,)
        for j in range(ups):
            saver.wait(ready[g.up_at + j][0])
        loads = load([
            (xs_in.at[0], xbuf), (acts_in.at[6], tile_q), (kv_in.at[0], kv.at[0]), (kv_in.at[1], kv.at[1]),
        ])
        w = weight(cross_at)
        tiles(width, 512, functools.partial(branch_grad, w, gb))
        prefetch()
        step()
        saver.wait(at)
        wait(loads)
        wait(load([(o2, tile_o)]))
        second[...] = jnp.broadcast_to(second_image(seg_col, images, pl.ds(0, tokens)), second.shape)
        key_bias = jnp.where(lax.broadcasted_iota(jnp.int32, (1, per_image), 1) < mem_tokens, 0.0, MASKED)
        k2, v2 = kv.at[0], kv.at[1]
        looped(
            HEADS // 2,
            lambda i: cross_backward(i, tile_q, k2, v2, do, tile_o, second, key_bias, lse.at[1]),
            (1, 5),
        )
        ready[4] = (saver.save(k2, gkv_out.at[0]),)
        ready[5] = (saver.save(v2, gkv_out.at[1]),)

        def scaled(src, dst, row):
            def body(i, total):
                rows = pl.ds(pl.multiple_of(i * 64, 64), 64)
                value = src[rows, :].astype(F32) * scale
                dst[rows, :] = value.astype(BF16)
                return total + jnp.sum(value, axis=0, keepdims=True)

            sums[pl.ds(row, 1), :] = lax.fori_loop(0, tokens // 64, body, jnp.zeros((1, width), F32))

        scaled(tile_q, gq, 3 + 3)
        ready[3] = (saver.save(gq, gq_out.at[0]),)
        back_project(gq, 3, True)
        step()
        column_sum(v2, 3 + 4, keys)
        w4 = weight(4)
        w5 = weight(5)
        mem_tile, mem_rows = 256, per_image
        spots = [(r, c) for r in range(keys // mem_rows) for c in range(width // mem_tile)]

        def gm_copy(i):
            r, c = spots[i]
            dst = dmem_out.at[pl.ds(r * mem_rows, mem_rows), pl.ds(c * mem_tile, mem_tile)]
            return pltpu.make_async_copy(gm.at[i % 2], dst, gmsem.at[i % 2])

        for i, (r, c) in enumerate(spots):
            rows, cols = pl.ds(r * mem_rows, mem_rows), pl.ds(c * mem_tile, mem_tile)
            if i >= 2:
                gm_copy(i - 2).wait()
            gm[i % 2] = dot_nt(k2[rows, :], w4[cols, :]) + dot_nt(v2[rows, :], w5[cols, :])
            gm_copy(i).start()
        for i in range(max(len(spots) - 2, 0), len(spots)):
            gm_copy(i).wait()
        prefetch()
        prefetch()
        step()
        gb = tile_o
        norm_back(lambda r: xbuf[r, :], lambda r: dx[r, :], 1, 7, 2, gb, put_dx)
        at = saver.save(gb, gb_out.at[1])
        ready[first] = (at,)
        for kind in (3, 4, 5):
            saver.wait(ready[kind][0])
        q1, k1, v1 = tile_q, kv.at[0, pl.ds(0, tokens)], kv.at[1, pl.ds(0, tokens)]
        loads = load([(acts_in.at[1], q1), (acts_in.at[2], k1), (acts_in.at[3], v1)])
        w = weight(first)
        tiles(width, 512, functools.partial(branch_grad, w, gb))
        prefetch()
        fill_self_bias(bias, seg_col, seg_row)
        step()
        saver.wait(at)
        wait(loads)
        wait(load([(o1, tile_o)]))
        looped(
            HEADS // 2,
            lambda i: self_backward(i, q1, k1, v1, do, tile_o, bias, lse.at[0]),
            (3,),
        )
        loads = load([(x_ref, tile_o)])
        scaled(q1, gq, 3 + 0)
        ready[0] = (saver.save(gq, gq_out.at[1]),)
        ready[1] = (saver.save(k1, gq_out.at[2]),)
        ready[2] = (saver.save(v1, gq_out.at[3]),)
        step()
        step()
        step()
        column_sum(v1, 3 + 1)
        back_project(gq, 0, True)
        step()
        back_project(k1, 1, False)
        step()
        back_project(v1, 2, False)
        wait(loads)
        step()
        norm_back(lambda r: tile_o[r, :].astype(F32), lambda r: dx[r, :], 0, 6, None, None, put_dx)
        saver.save(dx, dx_out)
        small = small_stages()
        next(small)
        while cursor[0] < red.last:
            step()
            next(small, None)
        for _ in small:
            pass
        saver.finish()
        red.finish()
        for copy in small_open:
            copy.wait_send()

    small_steps = n - 1 + 2 + max(geo.a_count - 1, 1)
    dma = pltpu.SemaphoreType.DMA
    tile = (tokens, width)
    return pl.pallas_call(
        kernel,
        out_shape=[
            b16((units, geo.rows, width)),
            f32(tile),
            f32((keys, width)),
            f32((SMALL, geo.rows)),
            b16((ups,) + tile),
            b16((2,) + tile),
            b16((4,) + tile),
            b16((2, keys, width)),
        ],
        in_specs=[HBM] * 3 + [VMEM, VMEM, SMEM] + [HBM] * 9 + [VMEM] * 2,
        out_specs=[HBM] * 3 + [VMEM] + [HBM] * 4,
        scratch_shapes=[
            pltpu.VMEM((2, width, width), BF16),
            pltpu.VMEM((keys, width), BF16),
            pltpu.VMEM((keys, width), BF16),
            pltpu.VMEM((5,) + tile, BF16),
            pltpu.VMEM((2, keys, width), BF16),
            pltpu.VMEM((2,) + tile, F32),
            pltpu.VMEM(tile, F32),
            pltpu.VMEM((2, per_image, width // 4), F32),
            pltpu.VMEM((tokens, tokens), F32),
            pltpu.VMEM((tokens, 128), jnp.int32),
            pltpu.VMEM((SMALL, width), F32),
            pltpu.VMEM((n - 1, SMALL, geo.rows), F32),
            pltpu.VMEM((3, SMALL, geo.rows), F32),
            pltpu.VMEM((SMALL, geo.rows), F32),
            pltpu.VMEM((SMALL, geo.rows), F32),
            pltpu.VMEM((geo.a_count, SMALL, geo.rows), F32),
            dma((2, 2 * n)),
            dma((8,)),
            dma((32,)),
            dma((2,)),
            dma((2,)),
            dma((small_steps,)),
            dma((small_steps,)),
        ]
        + Reduce.scratch(geo),
        compiler_params=pltpu.CompilerParams(
            collective_id=1, has_side_effects=True, vmem_limit_bytes=60 * MIB
        ),
    )(
        tokens_in, cotangent, memory, seg_col, seg_row, images, attn_in, attn_out, mlp_in, mlp_out,
        ring, acts, kv_acts, mlp_acts, xs, lse_all, vectors,
    )


def finish(geo, total, dmem, dx, layer_out, small, mem_tokens, counts):
    units, rows, width = total.shape
    n, ups = geo.narrow, geo.n_up
    images, per_image = dmem.shape[:2]
    tokens = dx.shape[0]
    span, lot = 128, tokens // units
    lanes = width // span

    def kernel(
        total_ref, dmem_ref, dx_ref, low_ref, small_ref,
        attn_in, attn_out, up, down, dmem_out, dx_out, low_out, *small_outs,
    ):
        u = pl.program_id(0)
        value = total_ref[0].astype(F32)

        @pl.when(u < geo.n_in)
        def _():
            attn_in[0] = value

        @pl.when((u >= geo.n_in) & (u < geo.up_at))
        def _():
            attn_out[0] = value

        @pl.when((u >= geo.up_at) & (u < geo.down_at))
        def _():
            for k in range(n):
                start = pl.multiple_of((k * ups + u - geo.up_at) * rows, rows)
                up[:, pl.ds(start, rows)] = value[:, k * rows : (k + 1) * rows]

        @pl.when(u >= geo.down_at)
        def _():
            down[...] = value

        @pl.when(u < lanes)
        def _():
            for i in range(images):
                dmem_out[:, i, :] = dmem_ref[i, :mem_tokens, :]
        dx_out[...] = dx_ref[...]
        low_out[...] = low_ref[...]
        at = 0
        for ref in small_outs:
            ref[...] = small_ref[pl.ds(at, ref.shape[0]), :]
            at += ref.shape[0]

    def unit_at(first, count):
        return lambda u: (jnp.clip(u - first, 0, count - 1), 0, 0)

    def lanes_at(u):
        return (0, 0, jnp.minimum(u, lanes - 1))

    shape = jax.ShapeDtypeStruct
    per_lot = pl.BlockSpec((lot, width), lambda u: (u, 0))
    return pl.pallas_call(
        kernel,
        grid=(units,),
        out_shape=[
            shape((geo.n_in, rows, width), F32),
            shape((geo.n_out, rows, width), F32),
            shape((rows, ups * width), F32),
            shape((ups * rows, width), F32),
            shape((mem_tokens, images, width), F32),
            shape((tokens, width), F32),
            shape((tokens, width), BF16),
        ]
        + [shape((count, rows), F32) for count in counts],
        in_specs=[
            pl.BlockSpec((1, rows, width), lambda u: (u, 0, 0)),
            pl.BlockSpec((images, per_image, span), lanes_at),
            per_lot,
            per_lot,
            pl.BlockSpec(small.shape, lambda u: (0, 0)),
        ],
        out_specs=[
            pl.BlockSpec((1, rows, width), unit_at(0, geo.n_in)),
            pl.BlockSpec((1, rows, width), unit_at(geo.n_in, geo.n_out)),
            pl.BlockSpec((rows, ups * width), lambda u: (0, 0)),
            pl.BlockSpec((rows, width), lambda u: (jnp.clip(u - geo.down_at, 0, ups - 1), 0)),
            pl.BlockSpec((mem_tokens, images, span), lanes_at),
            per_lot,
            per_lot,
        ]
        + [pl.BlockSpec((count, rows), lambda u: (0, 0)) for count in counts],
        compiler_params=pltpu.CompilerParams(vmem_limit_bytes=40 * MIB),
    )(total, dmem, dx, layer_out, small)


def per_device(
    mesh, hidden_in, memory, segment_ids, image_ids, attn_in, attn_out, mlp_in, mlp_out, gains, shifts, mlp_bias,
    cotangent,
):
    width = hidden_in.shape[2]
    n_in, n_out = attn_in.shape[0], attn_out.shape[0]
    geo = Geometry(mesh, width, n_in, n_out, mlp_in.shape[1])
    rows, n = geo.rows, geo.narrow
    images, mem_tokens = memory.shape[1], memory.shape[2]
    per_image = -(-mem_tokens // 128) * 128
    padded = jnp.pad(memory[0], ((0, 0), (0, per_image - mem_tokens), (0, 0))).reshape(images * per_image, width)
    small = jnp.concatenate([gains, shifts, mlp_bias.reshape(geo.n_up, rows)], axis=0).astype(F32)
    used = small.shape[0]
    small = jnp.pad(small, ((0, SMALL - used), (0, 0)))
    seg_col, seg_row = segment_ids.reshape(-1, 1), segment_ids
    ring, layer_out, acts, kv, mlp_acts, xs, lse, vec = forward(
        geo, hidden_in[0], padded, mem_tokens, seg_col, seg_row, image_ids, attn_in, attn_out, mlp_in, mlp_out, small
    )
    total, dx, dmem, small_total, *_ = backward(
        geo, mem_tokens, hidden_in[0], cotangent[0], padded, seg_col, seg_row, image_ids, attn_in, attn_out, mlp_in, mlp_out,
        (ring, acts, kv, mlp_acts, xs, lse, vec),
    )
    big = finish(
        geo, total, dmem.reshape(images, per_image, width), dx, layer_out, small_total, mem_tokens,
        (gains.shape[0], shifts.shape[0], geo.n_up),
    )
    return (
        big[6][None], big[5][None], big[4].transpose(1, 0, 2)[None], big[0], big[1], big[2], big[3],
        big[7], big[8], big[9].reshape(-1),
    )


def solution(mesh):
    split = ("wide", "narrow")
    return jax.shard_map(
        functools.partial(per_device, mesh),
        mesh=mesh,
        in_specs=(
            P(split, None, None), P(split, None, None, None), P(split, None), P(split, None), P(None, "narrow", None),
            P(None, "narrow", None), P("narrow", None), P("narrow", None), P(None, "narrow"), P(None, "narrow"),
            P("narrow"), P(split, None, None),
        ),
        out_specs=(
            P(split, None, None), P(split, None, None), P(split, None, None, None), P(None, "narrow", None),
            P(None, "narrow", None), P("narrow", None), P("narrow", None), P(None, "narrow"), P(None, "narrow"),
            P("narrow"),
        ),
        check_vma=False,
    )
```

```python
import functools

import jax
import jax.numpy as jnp
from jax import lax
from jax.experimental import pallas as pl
from jax.experimental.pallas import tpu as pltpu
from jax.sharding import PartitionSpec as P

HEADS = 16
MESH = pl.DeviceIdType.MESH
F32 = jnp.float32
BF16 = jnp.bfloat16
MIB = 1 << 20
EPS = 1e-5
MASKED = -1e30
SMALL = 24
ROOT_HALF = 0.7071067811865476
ROOT_TWO_PI = 0.3989422804014327
HBM = pl.BlockSpec(memory_space=pltpu.HBM)
VMEM = pl.BlockSpec(memory_space=pltpu.VMEM)
SMEM = pl.BlockSpec(memory_space=pltpu.SMEM)


class Geometry:
    def __init__(self, mesh, width, n_in, n_out, hidden):
        self.wide = mesh.shape["wide"]
        self.narrow = mesh.shape["narrow"]
        self.a_count = self.wide // 4
        self.width = width
        self.rows = width // self.narrow
        self.core_rows = self.rows // 2
        self.piece_rows = self.core_rows // self.a_count
        self.half = width // 2
        self.quarter = width // 4
        self.n_in, self.n_out, self.n_up = n_in, n_out, hidden // width
        self.up_at = n_in + n_out
        self.down_at = self.up_at + self.n_up
        self.units = self.down_at + self.n_up

    def place(self):
        w = lax.axis_index("wide")
        n = lax.axis_index("narrow")
        self.w, self.n = w, n
        self.a, self.b, self.c = w // 4, lax.rem(w // 2, 2), lax.rem(w, 2)
        self.core_at = pl.multiple_of(self.c * self.core_rows, self.core_rows)
        self.b_at = pl.multiple_of(self.b * self.quarter, self.quarter)
        self.mine = pl.multiple_of(self.c * self.core_rows + self.a * self.piece_rows, self.piece_rows)
        self.other_core = (w + 1 - 2 * self.c, n)
        self.b_peer = (w + 2 - 4 * self.b, n)

    def a_of(self, step):
        return lax.rem(self.a + step, self.a_count)

    def a_peer(self, step):
        return (self.w + 4 * (self.a_of(step) - self.a), self.n)

    def z_of(self, step):
        return lax.rem(self.n + step, self.narrow)

    def z_peer(self, step):
        return (self.w, self.z_of(step))

    def greet(self):
        barrier = pltpu.get_barrier_semaphore()
        peers = [self.other_core, self.b_peer]
        peers += [self.a_peer(i) for i in range(1, self.a_count)]
        peers += [self.z_peer(i) for i in range(1, self.narrow)]
        for peer in peers:
            pl.semaphore_signal(barrier, inc=1, device_id=peer, device_id_type=MESH)
        pl.semaphore_wait(barrier, len(peers))


def remote(src, dst, send, recv, peer):
    return pltpu.make_async_remote_copy(
        src_ref=src, dst_ref=dst, send_sem=send, recv_sem=recv, device_id=peer, device_id_type=MESH
    )


class Shard:
    def __init__(self, geo, attn_in, attn_out, up, down):
        self.geo, self.attn_in, self.attn_out, self.up, self.down = geo, attn_in, attn_out, up, down

    def parts(self, u, row, rows, col, cols):
        g = self.geo
        at = pl.ds(row, rows)
        if u < g.n_in:
            return [(self.attn_in.at[u, at, pl.ds(col, cols)], 0, cols)]
        if u < g.up_at:
            return [(self.attn_out.at[u - g.n_in, at, pl.ds(col, cols)], 0, cols)]
        if u < g.down_at:
            j, out = u - g.up_at, []
            for p in range(cols // g.rows):
                start = (col // g.rows + p) * (g.n_up * g.rows) + j * g.rows
                if not isinstance(start, int):
                    start = pl.multiple_of(start, g.rows)
                out.append((self.up.at[at, pl.ds(start, g.rows)], p * g.rows, g.rows))
            return out
        start = (u - g.down_at) * g.rows + row
        if not isinstance(start, int):
            start = pl.multiple_of(start, g.piece_rows)
        return [(self.down.at[pl.ds(start, rows), pl.ds(col, cols)], 0, cols)]


class Gather:
    def __init__(self, geo, shard, ring, send, recv):
        self.geo, self.shard, self.ring, self.send, self.recv = geo, shard, ring, send, recv
        self.open = []

    lags = (0, 1, 3, 4)

    @staticmethod
    def z_sems(geo):
        return 2 * (geo.narrow - 1) * (geo.quarter // geo.rows)

    @classmethod
    def sems(cls, geo):
        return cls.z_sems(geo) + 2 * geo.a_count + 1

    def copies(self, kind, u):
        g = self.geo

        def copy(slot, src, dst, peer):
            return remote(src, dst, self.send.at[u, slot], self.recv.at[u, slot], peer)

        mine = pl.ds(g.mine, g.piece_rows)
        low_b = pl.ds(g.b_at, g.quarter)
        high_b = pl.ds(pl.multiple_of(g.half + g.b_at, g.quarter), g.quarter)
        core = pl.ds(g.core_at, g.core_rows)
        if kind == 0:
            out = []
            for k in range(1, g.narrow):
                for start in (low_b.start, high_b.start):
                    for src, col, cols in self.shard.parts(u, g.mine, g.piece_rows, start, g.quarter):
                        cols = pl.ds(pl.multiple_of(start + col, g.rows), cols)
                        dst = self.ring.at[u, g.narrow - k - 1, mine, cols]
                        out.append(copy(len(out), src, dst, g.z_peer(k)))
            return out
        base = self.z_sems(g)
        steps = range(1, g.a_count)
        if kind == 1:
            low = self.ring.at[u, :, mine, low_b]
            high = self.ring.at[u, :, mine, high_b]
            out = [copy(base + i - 1, low, low, g.a_peer(i)) for i in steps]
            return out + [copy(base + g.a_count - 1, high, high, g.b_peer)]
        base += g.a_count
        if kind == 2:
            low = self.ring.at[u, :, core, low_b]
            high = self.ring.at[u, :, mine, pl.ds(g.half, g.half)]
            out = [copy(base + i - 1, high, high, g.a_peer(i)) for i in steps]
            return out + [copy(base + g.a_count - 1, low, low, g.b_peer)]
        part = self.ring.at[u, :, core, :]
        return [copy(base + g.a_count, part, part, g.other_core)]

    def event(self, kind, u):
        if kind > 0:
            for copy in self.copies(kind - 1, u):
                copy.wait_recv()
        if kind < 4:
            for copy in self.copies(kind, u):
                copy.start()
            self.open.append((kind, u))

    def finish(self):
        for kind, u in self.open:
            for copy in self.copies(kind, u):
                copy.wait_send()


def add_rows(dst, parts, tile):
    count, rows = dst.shape[0], dst.shape[1]
    tile = min(tile, rows)
    per = rows // tile

    def body(i, carry):
        k, r = i // per, pl.multiple_of(lax.rem(i, per) * tile, tile)
        total = parts[0](k, r, tile).astype(F32)
        for part in parts[1:]:
            total = total + part(k, r, tile).astype(F32)
        dst[k, pl.ds(r, tile), :] = total.astype(dst.dtype)
        return carry

    lax.fori_loop(0, count * per, body, 0)


class Reduce:
    slots = 2
    held = 3
    landing = 6
    late = 4
    early = (6,)
    stages = ("C", "P1", "P2", "Z", "Q1", "Q2", "QC")
    stages_early = ("C", "Z", "P1", "P2", "Q1", "Q2", "QC")
    steps = (0, 1, 3, 5, 8, 9, 10, 11)
    steps_early = (0, 1, 6, 8, 10, 11, 12, 13)

    def __init__(self, geo, bufs, out, order):
        self.geo, self.out, self.order = geo, out, order
        names = [name for name, _ in self.shapes(geo)]
        self.bufs = dict(zip(names, bufs))
        self.gbuf = self.bufs["gbuf"]
        self.send, self.recv, self.local, self.credit = bufs[len(names) :]
        self.open = set()

    @classmethod
    def shapes(cls, geo):
        g, n, w = geo, geo.narrow, geo.width
        peers = max(g.a_count - 1, 1)
        r, c, p, h, q = g.rows, g.core_rows, g.piece_rows, g.half, g.quarter
        out = [("gbuf", (cls.slots, n, r, w)), ("rc", (cls.slots, n, c, w)), ("fin", (cls.slots, p, h))]
        for tag, count, many, m in (("", cls.held, cls.landing, n), ("e", len(cls.early), len(cls.early), 1)):
            out += [
                ("s1" + tag, (count, m, c, w)),
                ("s2a" + tag, (count, m, p, h)),
                ("s2b" + tag, (count, m, c, q)),
                ("p1a" + tag, (many, peers, m, p, h)),
                ("p1b" + tag, (many, m, c, q)),
                ("p2a" + tag, (many, m, p, q)),
                ("p2b" + tag, (many, peers, m, p, q)),
                ("s3" + tag, (max(count, cls.late), m, p, h)),
            ]
        early = len(cls.early)
        out += [("zr", (geo.units, n - 1, p, h)), ("zre", (early, n - 1, c, w)), ("s0e", (early, n, c, w))]
        return out

    @classmethod
    def scratch(cls, geo):
        count = 1 + 4 * geo.a_count + (geo.narrow - 1) + 1
        return [pltpu.VMEM(shape, BF16) for _, shape in cls.shapes(geo)] + [
            pltpu.SemaphoreType.DMA((geo.units, count)),
            pltpu.SemaphoreType.DMA((geo.units, count)),
            pltpu.SemaphoreType.DMA((2,)),
            pltpu.SemaphoreType.REGULAR,
        ]

    def buf(self, name, q):
        if q in self.early and name not in ("rc", "fin"):
            return self.bufs[name + "e"].at[self.early.index(q)]
        ref = self.bufs[name]
        return ref.at[q % ref.shape[0]]

    def stage(self, q, i):
        return (self.stages_early if q in self.early else self.stages)[i]

    def due(self, s):
        out = []
        for i in range(8):
            for q in range(self.geo.units):
                if q + (self.steps_early if q in self.early else self.steps)[i] == s:
                    out.append((i, q))
        return out

    @property
    def last(self):
        units = self.geo.units
        return max(units + self.steps[-1], max(self.early, default=0) + self.steps_early[-1] + 1)

    def copies(self, stage, q):
        g = self.geo
        u = self.order[q]
        na = g.a_count
        steps = range(1, na)
        mine = pl.ds(g.mine, g.piece_rows)
        core = pl.ds(g.core_at, g.core_rows)
        low_b = pl.ds(g.b_at, g.quarter)
        high_b = pl.ds(pl.multiple_of(g.half + g.b_at, g.quarter), g.quarter)
        peer_b = pl.multiple_of((1 - g.b) * g.quarter, g.quarter)

        def copy(s, src, dst, peer):
            return remote(src, dst, self.send.at[q, s], self.recv.at[q, s], peer)

        def in_core(a):
            return pl.ds(pl.multiple_of(a * g.piece_rows, g.piece_rows), g.piece_rows)

        if stage == "C":
            other = pl.ds(pl.multiple_of((1 - g.c) * g.core_rows, g.core_rows), g.core_rows)
            return [copy(0, self.gbuf.at[q % self.slots, :, other, :], self.buf("rc", q), g.other_core)]
        if stage == "P1":
            s1 = self.buf("s1", q)
            out = [
                copy(i, s1.at[:, in_core(g.a_of(i)), pl.ds(0, g.half)], self.buf("p1a", q).at[na - i - 1], g.a_peer(i))
                for i in steps
            ]
            cols = pl.ds(pl.multiple_of(g.half + peer_b, g.quarter), g.quarter)
            return out + [copy(na, s1.at[:, :, cols], self.buf("p1b", q), g.b_peer)]
        if stage == "P2":
            s2a, s2b = self.buf("s2a", q), self.buf("s2b", q)
            out = [
                copy(na + i, s2b.at[:, in_core(g.a_of(i)), :], self.buf("p2b", q).at[na - i - 1], g.a_peer(i))
                for i in steps
            ]
            return out + [copy(2 * na, s2a.at[:, :, pl.ds(peer_b, g.quarter)], self.buf("p2a", q), g.b_peer)]
        if stage == "Z":
            src, dst = (self.buf("s0", q) if q in self.early else self.buf("s3", q)), self.buf("zr", q)
            return [
                copy(2 * na + k, src.at[g.z_of(k)], dst.at[g.narrow - k - 1], g.z_peer(k)) for k in range(1, g.narrow)
            ]
        base = 2 * na + g.narrow
        if stage == "Q1":
            low, high = self.out.at[u, mine, low_b], self.out.at[u, mine, high_b]
            out = [copy(base + i - 1, low, low, g.a_peer(i)) for i in steps]
            return out + [copy(base + na - 1, high, high, g.b_peer)]
        base += na
        if stage == "Q2":
            low, high = self.out.at[u, core, low_b], self.out.at[u, mine, pl.ds(g.half, g.half)]
            out = [copy(base + i - 1, high, high, g.a_peer(i)) for i in steps]
            return out + [copy(base + na - 1, low, low, g.b_peer)]
        part = self.out.at[u, core, :]
        return [copy(base + na, part, part, g.other_core)]

    def begin(self, stage, q):
        for copy in self.copies(stage, q):
            copy.start()
        self.open.add((stage, q))

    def sent_before(self, stage, q, turn):
        if q not in self.early:
            for earlier in range(q % turn, q, turn):
                if earlier not in self.early:
                    self.sent(stage, earlier)

    def sent(self, stage, q):
        if (stage, q) in self.open:
            for copy in self.copies(stage, q):
                copy.wait_send()
            self.open.remove((stage, q))

    def event(self, i, q):
        g = self.geo
        if i == 0:
            if q >= self.slots:
                pl.semaphore_wait(self.credit, 1)
            self.begin("C", q)
            return
        done = self.stage(q, i - 1)
        for copy in self.copies(done, q):
            copy.wait_recv()
        self.combine(done, q)
        if i < 7:
            self.begin(self.stage(q, i), q)

    def combine(self, done, q):
        g = self.geo
        na = g.a_count
        early = q in self.early
        own = pl.multiple_of(g.a * g.piece_rows, g.piece_rows)
        low_b = pl.ds(g.b_at, g.quarter)
        high_b = pl.ds(pl.multiple_of(g.half + g.b_at, g.quarter), g.quarter)
        if done == "C":
            self.sent_before("P1", q, self.held)
            gbuf, rc = self.gbuf.at[q % self.slots], self.buf("rc", q)
            add_rows(
                self.buf("s0" if early else "s1", q),
                [
                    lambda k, r, t: gbuf[k, pl.ds(pl.multiple_of(g.core_at + r, 16), t), :],
                    lambda k, r, t: rc[k, pl.ds(r, t), :],
                ],
                32,
            )
            if q + self.slots < g.units:
                pl.semaphore_signal(self.credit, inc=1, device_id=g.other_core, device_id_type=MESH)
        elif done == "P1":
            self.sent_before("P2", q, self.held)
            s1, p1a, p1b = self.buf("s1", q), self.buf("p1a", q), self.buf("p1b", q)
            add_rows(
                self.buf("s2a", q),
                [lambda k, r, t: s1[k, pl.ds(pl.multiple_of(own + r, 16), t), pl.ds(0, g.half)]]
                + [lambda k, r, t, i=i: p1a[i, k, pl.ds(r, t), :] for i in range(na - 1)],
                64,
            )
            add_rows(
                self.buf("s2b", q),
                [lambda k, r, t: s1[k, pl.ds(r, t), high_b], lambda k, r, t: p1b[k, pl.ds(r, t), :]],
                128,
            )
        elif done == "P2":
            self.sent_before("Z", q, self.late)
            s2a, s2b, p2a, p2b, s3 = (self.buf(name, q) for name in ("s2a", "s2b", "p2a", "p2b", "s3"))
            add_rows(
                s3.at[:, :, pl.ds(0, g.quarter)],
                [lambda k, r, t: s2a[k, pl.ds(r, t), low_b], lambda k, r, t: p2a[k, pl.ds(r, t), :]],
                64,
            )
            add_rows(
                s3.at[:, :, pl.ds(g.quarter, g.quarter)],
                [lambda k, r, t: s2b[k, pl.ds(pl.multiple_of(own + r, 16), t), :]]
                + [lambda k, r, t, i=i: p2b[i, k, pl.ds(r, t), :] for i in range(na - 1)],
                64,
            )
            if early:
                self.place(s3.at[0], q)
        elif done == "Z":
            zr = self.buf("zr", q)
            if early:
                s0 = self.buf("s0", q)
                add_rows(
                    self.buf("s1", q),
                    [lambda k, r, t: s0[g.n, pl.ds(r, t), :]]
                    + [lambda k, r, t, i=i: zr[i, pl.ds(r, t), :] for i in range(g.narrow - 1)],
                    32,
                )
                return
            total = self.buf("s3", q)[g.n].astype(F32)
            for k in range(g.narrow - 1):
                total = total + zr[k].astype(F32)
            fin = self.buf("fin", q)
            fin[...] = total.astype(BF16)
            self.place(fin, q)

    def place(self, piece, q):
        g, u = self.geo, self.order[q]
        stores = []
        for h in range(2):
            cols = pl.ds(pl.multiple_of(h * g.half + g.b_at, g.quarter), g.quarter)
            dst = self.out.at[u, pl.ds(g.mine, g.piece_rows), cols]
            src = piece.at[:, pl.ds(h * g.quarter, g.quarter)]
            stores.append(pltpu.make_async_copy(src, dst, self.local.at[h]))
        for store in stores:
            store.start()
        for store in stores:
            store.wait()

    def finish(self):
        for stage, q in sorted(self.open):
            for copy in self.copies(stage, q):
                copy.wait_send()
        self.open = set()


class Weights:
    def __init__(self, geo, shard, ring, buf, sem):
        self.geo, self.shard, self.ring, self.buf, self.sem = geo, shard, ring, buf, sem

    def copies(self, u, slot):
        g = self.geo
        out = []
        for k in range(g.narrow):
            parts = self.shard.parts(u, 0, g.rows, 0, g.width) if k == 0 else [(self.ring.at[u, k - 1], 0, g.width)]
            rows = pl.ds(pl.multiple_of(g.z_of(k) * g.rows, g.rows), g.rows)
            for src, col, cols in parts:
                dst = self.buf.at[slot, rows, pl.ds(col, cols)]
                out.append(pltpu.make_async_copy(src, dst, self.sem.at[slot, len(out)]))
        return out

    def start(self, u, slot):
        for copy in self.copies(u, slot):
            copy.start()

    def wait(self, u, slot):
        for copy in self.copies(u, slot):
            copy.wait()
        return self.buf.at[slot]


def dot_nn(left, right):
    return jnp.dot(left, right, preferred_element_type=F32)


def dot_nt(left, right):
    return lax.dot_general(left, right, (((1,), (1,)), ((), ())), preferred_element_type=F32)


def dot_tn(left, right):
    return lax.dot_general(left, right, (((0,), (0,)), ((), ())), preferred_element_type=F32)


def over(count, body):
    def step(i, carry):
        body(i)
        return carry

    lax.fori_loop(0, count, step, 0)


def tiles(total, tile, body):
    over(total // tile, lambda i: body(pl.ds(pl.multiple_of(i * tile, tile), tile)))


def normalized(x):
    centered = x - jnp.mean(x, axis=-1, keepdims=True)
    variance = jnp.mean(centered * centered, axis=-1, keepdims=True)
    scale = lax.rsqrt(variance + EPS)
    return centered * scale, scale


def pair_cols(i):
    return pl.ds(pl.multiple_of(i * 128, 128), 128)


def lane_half(rows):
    return lax.broadcasted_iota(jnp.int32, (rows, 128), 1) // 64


def keep_half(values, side, half):
    return jnp.where(side == half, values, jnp.zeros_like(values))


def put_lane(ref, rows, lane, column):
    lanes = lax.broadcasted_iota(jnp.int32, (column.shape[0], 128), 1)
    ref[rows, :] = jnp.where(lanes == lane, column, ref[rows, :])


def take_lane(ref, rows, lane):
    values = ref[rows, :]
    lanes = lax.broadcasted_iota(jnp.int32, values.shape, 1)
    return jnp.sum(jnp.where(lanes == lane, values, 0.0), axis=-1, keepdims=True)


def softmax(scores):
    top = jnp.max(scores, axis=-1, keepdims=True)
    expo = jnp.exp(scores - top)
    total = jnp.sum(expo, axis=-1, keepdims=True)
    return (expo * (1.0 / total)).astype(BF16), top + jnp.log(total)


def fill_self_bias(bias, seg_col, seg_row):
    tokens = bias.shape[0]

    def body(rows):
        count = rows.size
        query = rows.start + lax.broadcasted_iota(jnp.int32, (count, tokens), 0)
        key = lax.broadcasted_iota(jnp.int32, (count, tokens), 1)
        allowed = (seg_col[rows, :] == seg_row[...]) & (key <= query)
        bias[rows, :] = jnp.where(allowed, 0.0, MASKED)

    tiles(tokens, 128, body)


def second_image(seg_col, images, rows):
    pages = seg_col[rows, :]
    image = jnp.zeros_like(pages)
    for page in range(images.shape[1]):
        image = jnp.where(pages == page, images[0, page], image)
    return image


def self_forward(i, q, k, v, bias, o, lse):
    cols = pair_cols(i)
    tokens = q.shape[0]
    block = tokens // 2
    side = lane_half(block)
    for at in range(0, tokens, block):
        rows, keys = pl.ds(at, block), pl.ds(0, at + block)
        queries, key, value = q[rows, cols], k[keys, cols], v[keys, cols]
        mixed = []
        for half in range(2):
            scores = dot_nt(keep_half(queries, side, half), key) + bias[rows, keys]
            probs, total = softmax(scores)
            put_lane(lse, rows, 2 * i + half, total)
            mixed.append(dot_nn(probs, value))
        o[rows, cols] = jnp.where(side == 0, mixed[0], mixed[1]).astype(BF16)


def self_backward(i, q, k, v, do, o, bias, lse):
    cols = pair_cols(i)
    tokens = q.shape[0]
    block = tokens // 2
    side = lane_half(block)
    grads_k, grads_v, grads_q = [], [], []
    for at in range(0, tokens, block):
        rows, keys = pl.ds(at, block), pl.ds(0, at + block)
        queries, key, value, grad, mix = q[rows, cols], k[keys, cols], v[keys, cols], do[rows, cols], o[rows, cols]
        product = grad.astype(F32) * mix.astype(F32)
        parts, grad_k, grad_v = [], 0.0, 0.0
        for half in range(2):
            own_q, own_g = keep_half(queries, side, half), keep_half(grad, side, half)
            scores = dot_nt(own_q, key) + bias[rows, keys]
            probs = jnp.exp(scores - take_lane(lse, rows, 2 * i + half))
            inner = jnp.sum(keep_half(product, side, half), axis=-1, keepdims=True)
            slopes = (probs * (dot_nt(own_g, value) - inner)).astype(BF16)
            parts.append(dot_nn(slopes, key))
            grad_k = grad_k + dot_tn(slopes, own_q)
            grad_v = grad_v + dot_tn(probs.astype(BF16), own_g)
        grads_q.append((rows, jnp.where(side == 0, parts[0], parts[1])))
        grads_k.append(grad_k)
        grads_v.append(grad_v)
    low = pl.ds(0, block)
    high = pl.ds(block, block)
    k[low, cols] = (grads_k[0] + grads_k[1][:block]).astype(BF16)
    k[high, cols] = grads_k[1][block:].astype(BF16)
    v[low, cols] = (grads_v[0] + grads_v[1][:block]).astype(BF16)
    v[high, cols] = grads_v[1][block:].astype(BF16)
    for rows, grad in grads_q:
        q[rows, cols] = grad.astype(BF16)


def both_images(ref, cols):
    keys = ref.shape[0] // 2
    return jnp.concatenate([ref[pl.ds(0, keys), cols], ref[pl.ds(keys, keys), cols]], axis=1)


def by_image(values, second):
    zero = jnp.zeros_like(values)
    return jnp.concatenate([jnp.where(second, zero, values), jnp.where(second, values, zero)], axis=1)


def pick_image(values, second):
    return jnp.where(second, values[:, 128:], values[:, :128])


def cross_forward(i, q, k, v, second_at, key_bias, o, lse, block=256):
    cols = pair_cols(i)
    key, value = both_images(k, cols), both_images(v, cols)
    side = lane_half(block)
    for at in range(0, q.shape[0], block):
        rows = pl.ds(at, block)
        queries = q[rows, cols]
        second = second_at[rows, :] == 1
        mixed = []
        for half in range(2):
            scores = dot_nt(by_image(keep_half(queries, side, half), second), key) + key_bias
            probs, total = softmax(scores)
            put_lane(lse, rows, 2 * i + half, total)
            mixed.append(pick_image(dot_nn(probs, value), second))
        o[rows, cols] = jnp.where(side == 0, mixed[0], mixed[1]).astype(BF16)


def cross_backward(i, q, k, v, do, o, second_at, key_bias, lse, block=256):
    cols = pair_cols(i)
    key, value = both_images(k, cols), both_images(v, cols)
    side = lane_half(block)
    grad_k, grad_v, grads_q = 0.0, 0.0, []
    for at in range(0, q.shape[0], block):
        rows = pl.ds(at, block)
        queries, grad, mix = q[rows, cols], do[rows, cols], o[rows, cols]
        second = second_at[rows, :] == 1
        product = grad.astype(F32) * mix.astype(F32)
        parts = []
        for half in range(2):
            own_q = by_image(keep_half(queries, side, half), second)
            own_g = by_image(keep_half(grad, side, half), second)
            scores = dot_nt(own_q, key) + key_bias
            probs = jnp.exp(scores - take_lane(lse, rows, 2 * i + half))
            inner = jnp.sum(keep_half(product, side, half), axis=-1, keepdims=True)
            slopes = (probs * (dot_nt(own_g, value) - inner)).astype(BF16)
            parts.append(pick_image(dot_nn(slopes, key), second))
            grad_k = grad_k + dot_tn(slopes, own_q)
            grad_v = grad_v + dot_tn(probs.astype(BF16), own_g)
        grads_q.append((rows, jnp.where(side == 0, parts[0], parts[1])))
    keys = k.shape[0] // 2
    for ref, total in ((k, grad_k), (v, grad_v)):
        ref[pl.ds(0, keys), cols] = total[:, :128].astype(BF16)
        ref[pl.ds(keys, keys), cols] = total[:, 128:].astype(BF16)
    for rows, grad in grads_q:
        q[rows, cols] = grad.astype(BF16)


class Saver:
    def __init__(self, sems):
        self.sems, self.open, self.used = sems, {}, 0

    def save(self, src, dst):
        at = self.used
        self.used += 1
        pltpu.make_async_copy(src, dst, self.sems.at[at]).start()
        self.open[at] = (src, dst)
        return at

    def wait(self, at):
        if at in self.open:
            src, dst = self.open.pop(at)
            pltpu.make_async_copy(src, dst, self.sems.at[at]).wait()

    def finish(self):
        for at in list(self.open):
            self.wait(at)


def forward(geo, tokens_in, memory, mem_tokens, seg_col, seg_row, images, attn_in, attn_out, mlp_in, mlp_out, small):
    tokens, width = tokens_in.shape
    keys = memory.shape[0]
    units, n = geo.units, geo.narrow
    first, cross_at = geo.n_in, geo.n_in + 1
    order = [0, 1, 2, first, 3, 4, 5, cross_at] + list(range(geo.up_at, units))
    wslots = 4
    scale = (width // HEADS) ** -0.5
    ups = geo.n_up
    f32, b16 = functools.partial(jax.ShapeDtypeStruct, dtype=F32), functools.partial(jax.ShapeDtypeStruct, dtype=BF16)

    def kernel(
        x_ref, mem_ref, seg_col, seg_row, images, ai, ao, mi, mo, small_ref,
        ring, layer_out, acts_out, kv_out, mlp_out_acts, xs_out, lse_out, vec,
        wbuf, x0, xs, acc, acts, kv, mlp_acts, mem, bias, second, low_out, small_buf,
        gsend, grecv, ssend, srecv, wsem, lsem, osem,
    ):
        g = geo
        g.place()
        load_x = pltpu.make_async_copy(x_ref, x0, lsem.at[0])
        load_m = pltpu.make_async_copy(mem_ref, mem, lsem.at[1])
        load_x.start()
        load_m.start()

        g.greet()
        shard = Shard(g, ai, ao, mi, mo)
        gather = Gather(g, shard, ring, gsend, grecv)
        weights = Weights(g, shard, ring, wbuf, wsem)

        def small_copy(k):
            return remote(small_ref, small_buf.at[n - k - 1], ssend.at[k - 1], srecv.at[k - 1], g.z_peer(k))

        for k in range(1, n):
            small_copy(k).start()
        gather.event(0, order[0])
        gather.event(0, order[1])
        saver = Saver(osem)
        cursor = [0]
        used = [0]

        def step():
            s = cursor[0]
            cursor[0] += 1
            if s + 2 < units:
                gather.event(0, order[s + 2])
            for kind in range(1, 5):
                q = s - Gather.lags[kind - 1]
                if 0 <= q < units:
                    gather.event(kind, order[q])
                    if kind == 4:
                        assert q - wslots < used[0]
                        weights.start(order[q], q % wslots)

        def weight():
            q = used[0]
            while cursor[0] <= q + Gather.lags[3]:
                step()
            return weights.wait(order[q], q % wslots)

        def done():
            used[0] += 1

        def project(left, finish, tile=512, row_tile=640):
            w = weight()
            row_tile = min(row_tile, left.shape[0])
            tiles(width, tile, lambda cols: tiles(
                left.shape[0], row_tile, lambda rows: finish(dot_nn(left[rows, :], w[:, cols]), rows, cols)
            ))
            done()

        def looped(count, body, hooks):
            def inner(i):
                body(i)
                for at in hooks:
                    @pl.when(i == at)
                    def _():
                        step()

            over(count, inner)

        h1, q, k, v, o, h2, q2, o2, h3 = (acts.at[i] for i in range(9))
        for k_ in range(1, n):
            small_copy(k_).wait_recv()
        place_n = [small_ref] + [small_buf.at[i] for i in range(n - 1)]
        for i in range(n):
            vec[:, pl.ds(pl.multiple_of(g.z_of(i) * g.rows, g.rows), g.rows)] = place_n[i][...]

        def gain(i):
            return vec[pl.ds(i, 1), :]

        def shift(i, cols=slice(None)):
            return vec[pl.ds(3 + i, 1), cols]

        def norm(read, h, gain_at, shift_at):
            def body(rows):
                unit, _ = normalized(read(rows))
                h[rows, :] = (unit * gain(gain_at) + shift(shift_at)).astype(BF16)

            tiles(tokens, 64, body)

        fill_self_bias(bias, seg_col, seg_row)
        load_x.wait()
        step()
        norm(lambda rows: x0[rows, :].astype(F32), h1, 0, 6)
        second[...] = jnp.broadcast_to(second_image(seg_col, images, pl.ds(0, tokens)), second.shape)
        lse_out[...] = jnp.zeros_like(lse_out)

        def put(ref, shift_at=None, factor=None):
            def finish(value, rows, cols):
                if shift_at is not None:
                    value = value + shift(shift_at, cols)
                if factor is not None:
                    value = value * factor
                ref[rows, cols] = value.astype(BF16)

            return finish

        def save_act(i):
            saver.save(acts.at[i], acts_out.at[i])

        project(h1, put(q, 0, scale))
        project(h1, put(k))
        project(h1, put(v, 1))
        for i in range(4):
            save_act(i)
        self_lse, cross_lse = lse_out.at[0], lse_out.at[1]
        looped(HEADS // 2, lambda i: self_forward(i, q, k, v, bias, o, self_lse), (2, 6))
        save_act(4)
        x1, x2 = xs.at[0], xs.at[1]

        def after_self(value, rows, cols):
            x1[rows, cols] = x0[rows, cols].astype(F32) + value + shift(2, cols)

        project(o, after_self)
        saver.save(x1, xs_out.at[0])
        norm(lambda rows: x1[rows, :], h2, 1, 7)
        save_act(5)
        project(h2, put(q2, 3, scale))
        save_act(6)
        load_m.wait()
        k2, v2 = kv.at[0], kv.at[1]
        project(mem, put(k2))
        project(mem, put(v2, 4))
        saver.save(k2, kv_out.at[0])
        saver.save(v2, kv_out.at[1])
        per_image = keys // 2
        key_bias = jnp.where(lax.broadcasted_iota(jnp.int32, (1, per_image), 1) < mem_tokens, 0.0, MASKED)
        looped(
            HEADS // 2, lambda i: cross_forward(i, q2, k2, v2, second, key_bias, o2, cross_lse), (1, 4, 6)
        )
        save_act(7)

        def after_cross(value, rows, cols):
            x2[rows, cols] = x1[rows, cols] + value + shift(5, cols)

        project(o2, after_cross)
        saver.save(x2, xs_out.at[1])
        norm(lambda rows: x2[rows, :], h3, 2, 8)
        save_act(8)
        for j in range(ups):
            def activate(value, rows, cols, j=j):
                z = value + vec[pl.ds(13 + j, 1), cols]
                cdf = 0.5 + 0.5 * lax.erf(z * ROOT_HALF)
                mlp_acts[0, j, rows, cols] = (z * cdf).astype(BF16)
                slope = cdf + z * (jnp.exp(-0.5 * z * z) * ROOT_TWO_PI)
                mlp_acts[1, j, rows, cols] = slope.astype(BF16)

            project(h3, activate, 256)
            saver.save(mlp_acts.at[0, j], mlp_out_acts.at[0, j])
            saver.save(mlp_acts.at[1, j], mlp_out_acts.at[1, j])
        for j in range(ups):
            def add(value, rows, cols, j=j):
                base = x2[rows, cols] + shift(9, cols) if j == 0 else acc[rows, cols]
                if j < ups - 1:
                    acc[rows, cols] = base + value
                else:
                    low_out[rows, cols] = (base + value).astype(BF16)

            project(mlp_acts.at[0, j], add)
        saver.save(low_out, layer_out)
        while cursor[0] < units + Gather.lags[3]:
            step()
        saver.finish()
        gather.finish()
        for k_ in range(1, n):
            small_copy(k_).wait_send()

    count = Gather.sems(geo)
    dma = pltpu.SemaphoreType.DMA
    return pl.pallas_call(
        kernel,
        out_shape=[
            b16((units, n - 1, geo.rows, width)),
            b16((tokens, width)),
            b16((9, tokens, width)),
            b16((2, keys, width)),
            b16((2, ups, tokens, width)),
            f32((2, tokens, width)),
            f32((2, tokens, 128)),
            f32((SMALL, width)),
        ],
        in_specs=[HBM, HBM, VMEM, VMEM, SMEM, HBM, HBM, HBM, HBM, VMEM],
        out_specs=[HBM] * 6 + [VMEM] * 2,
        scratch_shapes=[
            pltpu.VMEM((wslots, width, width), BF16),
            pltpu.VMEM((tokens, width), BF16),
            pltpu.VMEM((2, tokens, width), F32),
            pltpu.VMEM((tokens, width), F32),
            pltpu.VMEM((9, tokens, width), BF16),
            pltpu.VMEM((2, keys, width), BF16),
            pltpu.VMEM((2, ups, tokens, width), BF16),
            pltpu.VMEM((keys, width), BF16),
            pltpu.VMEM((tokens, tokens), F32),
            pltpu.VMEM((tokens, 128), jnp.int32),
            pltpu.VMEM((tokens, width), BF16),
            pltpu.VMEM((n - 1, SMALL, geo.rows), F32),
            dma((units, count)),
            dma((units, count)),
            dma((n - 1,)),
            dma((n - 1,)),
            dma((wslots, 2 * n)),
            dma((2,)),
            dma((32,)),
        ],
        compiler_params=pltpu.CompilerParams(
            collective_id=0, has_side_effects=True, vmem_limit_bytes=58 * MIB
        ),
    )(tokens_in, memory, seg_col, seg_row, images, attn_in, attn_out, mlp_in, mlp_out, small)


def backward(geo, mem_tokens, tokens_in, cotangent, memory, seg_col, seg_row, images, attn_in, attn_out, mlp_in, mlp_out, saved):
    ring, acts, kv_acts, mlp_acts, xs, lse_all, vectors = saved
    tokens, width = cotangent.shape
    keys = memory.shape[0]
    units, n, ups = geo.units, geo.narrow, geo.n_up
    first, cross_at = geo.n_in, geo.n_in + 1
    order = list(range(geo.down_at, units)) + list(range(geo.up_at, geo.down_at))
    order += [cross_at, 3, 4, 5, first, 0, 1, 2]
    fetch = [geo.down_at + j for j in range(ups)] + [geo.up_at + j for j in range(ups)]
    fetch += [cross_at, 3, 4, 5, first, 0, 1, 2]
    scale = (width // HEADS) ** -0.5
    per_image = keys // 2
    f32, b16 = functools.partial(jax.ShapeDtypeStruct, dtype=F32), functools.partial(jax.ShapeDtypeStruct, dtype=BF16)

    def kernel(*refs):
        (
            x_ref, g_ref, mem_ref, seg_col, seg_row, images, ai, ao, mi, mo,
            ring, acts_in, kv_in, mlp_in_acts, xs_in, lse, vec,
            out, dx_out, dmem_out, small_out, dz_out, gb_out, gq_out, gkv_out,
        ) = refs[:25]
        scratch = list(refs[25:])
        (
            wbuf, lhs, rhs, pool, kv, dxs, xbuf, gm, bias, second, sums,
            zsmall, tsmall, core_small, b_small, a_small,
            wsem, lsem, osem, gmsem, opsem, ssend, srecv,
        ) = scratch[:23]
        g = geo
        g.place()
        gy, do, tile_q, tile_o, gq = (pool.at[i] for i in range(5))
        dz = [kv.at[j % 2, pl.ds(j // 2 * tokens, tokens)] for j in range(ups)]
        slope = [do, tile_q]
        acc, dx = dxs.at[0], dxs.at[1]

        def load(pairs):
            copies = [pltpu.make_async_copy(src, dst, lsem.at[i]) for i, (src, dst) in enumerate(pairs)]
            for copy in copies:
                copy.start()
            return copies

        def wait(copies):
            for copy in copies:
                copy.wait()

        shard = Shard(g, ai, ao, mi, mo)
        weights = Weights(g, shard, ring, wbuf, wsem)
        fetched = [0, 0]

        def prefetch():
            if fetched[0] < len(fetch):
                weights.start(fetch[fetched[0]], fetched[0] % 2)
                fetched[0] += 1

        def weight(u):
            at = fetched[1]
            assert fetch[at] == u
            fetched[1] += 1
            return weights.wait(u, at % 2)

        start = load([(g_ref, gy), (mlp_in_acts.at[1, 0], slope[0])])
        prefetch()
        prefetch()
        g.greet()
        red = Reduce(g, scratch[23:], out, order)
        h1, h2, o2, h3, o1 = acts_in.at[0], acts_in.at[5], acts_in.at[7], acts_in.at[8], acts_in.at[4]
        operands = {}
        for j in range(ups):
            operands[g.down_at + j] = (mlp_in_acts.at[0, j], g_ref)
            operands[g.up_at + j] = (h3, dz_out.at[j])
        operands[cross_at] = (o2, gb_out.at[0])
        operands[3] = (h2, gq_out.at[0])
        operands[4] = (mem_ref, gkv_out.at[0])
        operands[5] = (mem_ref, gkv_out.at[1])
        operands[first] = (o1, gb_out.at[1])
        for i in range(3):
            operands[i] = (h1, gq_out.at[1 + i])
        saver = Saver(osem)
        ready = {u: () for u in range(g.down_at, units)}
        cursor = [0]

        loaded = {}

        def operand_copies(q):
            left, right = operands[order[q]]
            count = left.shape[0]
            return count, [
                pltpu.make_async_copy(left, lhs.at[pl.ds(0, count), :], opsem.at[0]),
                pltpu.make_async_copy(right, rhs.at[pl.ds(0, count), :], opsem.at[1]),
            ]

        def load_operands(q):
            if q < units and q not in loaded and order[q] in ready:
                loaded[q] = True
                for at in ready[order[q]]:
                    saver.wait(at)
                for copy in operand_copies(q)[1]:
                    copy.start()

        def produce(q):
            load_operands(q)
            assert loaded[q]
            count, copies = operand_copies(q)
            for copy in copies:
                copy.wait()
            red.sent("C", q - red.slots)
            slot = q % red.slots
            blocks = (width // 2) // g.rows

            def block(i):
                cols = pl.ds(pl.multiple_of(i * (width // 2), width // 2), width // 2)
                value = dot_tn(lhs[pl.ds(0, count), cols], rhs[pl.ds(0, count), :])
                red.gbuf[slot, pl.ds(i * blocks, blocks)] = value.astype(BF16).reshape(blocks, g.rows, width)

            over(2, block)
            load_operands(q + 1)

        def step():
            s = cursor[0]
            cursor[0] += 1
            if s < units:
                produce(s)
            for i, q in red.due(s):
                red.event(i, q)

        def looped(count, body, hooks):
            def inner(i):
                body(i)
                for at in hooks:
                    @pl.when(i == at)
                    def _():
                        step()

            over(count, inner)

        def gain(i):
            return vec[pl.ds(i, 1), :]

        def column_sum(ref, row, count=tokens, tile=64):
            def body(i, total):
                part = ref[pl.ds(pl.multiple_of(i * tile, tile), tile), :].astype(F32)
                return total + jnp.sum(part, axis=0, keepdims=True)

            sums[pl.ds(row, 1), :] = lax.fori_loop(0, count // tile, body, jnp.zeros((1, width), F32))

        def norm_back(read_x, read_base, gain_at, shift_at, base_shift, low, write):
            tile = 64

            def body(i, totals):
                rows = pl.ds(pl.multiple_of(i * tile, tile), tile)
                grad = acc[rows, :]
                unit, factor = normalized(read_x(rows))
                d_unit = grad * gain(gain_at)
                mean = jnp.mean(d_unit, axis=-1, keepdims=True)
                along = jnp.mean(d_unit * unit, axis=-1, keepdims=True)
                total = read_base(rows) + factor * (d_unit - mean - unit * along)
                write(rows, total)
                if low is not None:
                    low[rows, :] = total.astype(BF16)
                return (
                    totals[0] + jnp.sum(grad * unit, axis=0, keepdims=True),
                    totals[1] + jnp.sum(grad, axis=0, keepdims=True),
                    totals[2] + jnp.sum(total, axis=0, keepdims=True),
                )

            zero = jnp.zeros((1, width), F32)
            d_gain, d_shift, d_base = lax.fori_loop(0, tokens // tile, body, (zero, zero, zero))
            sums[pl.ds(gain_at, 1), :] = d_gain
            sums[pl.ds(3 + shift_at, 1), :] = d_shift
            if base_shift is not None:
                sums[pl.ds(3 + base_shift, 1), :] = d_base

        def back_project(grad, u, begin, tile=512):
            w = weight(u)

            def body(cols):
                value = dot_nt(grad[...], w[cols, :])
                acc[:, cols] = value if begin else acc[:, cols] + value

            tiles(width, tile, body)
            prefetch()

        def branch_grad(w, low, cols):
            do[:, cols] = dot_nt(low[...], w[cols, :]).astype(BF16)

        small_open = []

        def small_copy(at, src, dst, peer):
            copy = remote(src, dst, ssend.at[at], srecv.at[at], peer)
            copy.start()
            small_open.append(copy)
            return copy

        def small_stages():
            spots = [pl.ds(pl.multiple_of(g.z_of(k) * g.rows, g.rows), g.rows) for k in range(n)]
            copies = [small_copy(k - 1, sums.at[:, spots[k]], zsmall.at[n - k - 1], g.z_peer(k)) for k in range(1, n)]
            yield
            for copy in copies:
                copy.wait_recv()
            total = sums[:, spots[0]]
            for k in range(n - 1):
                total = total + zsmall[k]
            tsmall[0] = total
            copy = small_copy(n - 1, tsmall.at[0], core_small, g.other_core)
            yield
            copy.wait_recv()
            tsmall[1] = tsmall[0] + core_small[...]
            copy = small_copy(n, tsmall.at[1], b_small, g.b_peer)
            yield
            copy.wait_recv()
            tsmall[2] = tsmall[1] + b_small[...]
            a_small[g.a] = tsmall[2]
            copies = [small_copy(n + i, tsmall.at[2], a_small.at[g.a], g.a_peer(i)) for i in range(1, g.a_count)]
            yield
            for copy in copies:
                copy.wait_recv()
            total = a_small[0]
            for i in range(1, g.a_count):
                total = total + a_small[i]
            small_out[...] = total
            yield

        sums[...] = jnp.zeros_like(sums)
        step()
        step()
        step()
        wait(start)
        column_sum(gy, 3 + 9)
        for j in range(ups):
            w = weight(g.down_at + j)
            following = load([(mlp_in_acts.at[1, j + 1], slope[(j + 1) % 2])]) if j + 1 < ups else []

            def body(cols, j=j, w=w):
                value = (dot_nt(gy[...], w[cols, :]) * slope[j % 2][:, cols].astype(F32)).astype(BF16)
                dz[j][:, cols] = value
                sums[pl.ds(13 + j, 1), cols] = jnp.sum(value.astype(F32), axis=0, keepdims=True)

            tiles(width, 256, body)
            prefetch()
            at = saver.save(dz[j], dz_out.at[j])
            ready[g.up_at + j] = (at,)
            wait(following)
            if j == ups // 2 - 1:
                step()
        load_x2 = pltpu.make_async_copy(xs_in.at[1], xbuf, lsem.at[6])
        load_x2.start()
        step()
        for j in range(ups):
            back_project(dz[j], g.up_at + j, j == 0)
        step()
        load_x2.wait()

        def put_dx(rows, total):
            dx[rows, :] = total

        gb = tile_o
        norm_back(lambda r: xbuf[r, :], lambda r: gy[r, :].astype(F32), 2, 8, 5, gb, put_dx)
        at = saver.save(gb, gb_out.at[0])
        ready[cross_at] = (at,)
        for j in range(ups):
            saver.wait(ready[g.up_at + j][0])
        loads = load([
            (xs_in.at[0], xbuf), (acts_in.at[6], tile_q), (kv_in.at[0], kv.at[0]), (kv_in.at[1], kv.at[1]),
        ])
        w = weight(cross_at)
        tiles(width, 512, functools.partial(branch_grad, w, gb))
        prefetch()
        step()
        saver.wait(at)
        wait(loads)
        wait(load([(o2, tile_o)]))
        second[...] = jnp.broadcast_to(second_image(seg_col, images, pl.ds(0, tokens)), second.shape)
        key_bias = jnp.where(lax.broadcasted_iota(jnp.int32, (1, per_image), 1) < mem_tokens, 0.0, MASKED)
        k2, v2 = kv.at[0], kv.at[1]
        looped(
            HEADS // 2,
            lambda i: cross_backward(i, tile_q, k2, v2, do, tile_o, second, key_bias, lse.at[1]),
            (1, 5),
        )
        ready[4] = (saver.save(k2, gkv_out.at[0]),)
        ready[5] = (saver.save(v2, gkv_out.at[1]),)

        def scaled(src, dst, row):
            def body(i, total):
                rows = pl.ds(pl.multiple_of(i * 64, 64), 64)
                value = src[rows, :].astype(F32) * scale
                dst[rows, :] = value.astype(BF16)
                return total + jnp.sum(value, axis=0, keepdims=True)

            sums[pl.ds(row, 1), :] = lax.fori_loop(0, tokens // 64, body, jnp.zeros((1, width), F32))

        scaled(tile_q, gq, 3 + 3)
        ready[3] = (saver.save(gq, gq_out.at[0]),)
        back_project(gq, 3, True)
        step()
        column_sum(v2, 3 + 4, keys)
        w4 = weight(4)
        w5 = weight(5)
        mem_tile, mem_rows = 256, per_image
        spots = [(r, c) for r in range(keys // mem_rows) for c in range(width // mem_tile)]

        def gm_copy(i):
            r, c = spots[i]
            dst = dmem_out.at[pl.ds(r * mem_rows, mem_rows), pl.ds(c * mem_tile, mem_tile)]
            return pltpu.make_async_copy(gm.at[i % 2], dst, gmsem.at[i % 2])

        for i, (r, c) in enumerate(spots):
            rows, cols = pl.ds(r * mem_rows, mem_rows), pl.ds(c * mem_tile, mem_tile)
            if i >= 2:
                gm_copy(i - 2).wait()
            gm[i % 2] = dot_nt(k2[rows, :], w4[cols, :]) + dot_nt(v2[rows, :], w5[cols, :])
            gm_copy(i).start()
        for i in range(max(len(spots) - 2, 0), len(spots)):
            gm_copy(i).wait()
        prefetch()
        prefetch()
        step()
        gb = tile_o
        norm_back(lambda r: xbuf[r, :], lambda r: dx[r, :], 1, 7, 2, gb, put_dx)
        at = saver.save(gb, gb_out.at[1])
        ready[first] = (at,)
        for kind in (3, 4, 5):
            saver.wait(ready[kind][0])
        q1, k1, v1 = tile_q, kv.at[0, pl.ds(0, tokens)], kv.at[1, pl.ds(0, tokens)]
        loads = load([(acts_in.at[1], q1), (acts_in.at[2], k1), (acts_in.at[3], v1)])
        w = weight(first)
        tiles(width, 512, functools.partial(branch_grad, w, gb))
        prefetch()
        fill_self_bias(bias, seg_col, seg_row)
        step()
        saver.wait(at)
        wait(loads)
        wait(load([(o1, tile_o)]))
        looped(
            HEADS // 2,
            lambda i: self_backward(i, q1, k1, v1, do, tile_o, bias, lse.at[0]),
            (3,),
        )
        loads = load([(x_ref, tile_o)])
        scaled(q1, gq, 3 + 0)
        ready[0] = (saver.save(gq, gq_out.at[1]),)
        ready[1] = (saver.save(k1, gq_out.at[2]),)
        ready[2] = (saver.save(v1, gq_out.at[3]),)
        step()
        step()
        step()
        column_sum(v1, 3 + 1)
        back_project(gq, 0, True)
        step()
        back_project(k1, 1, False)
        step()
        back_project(v1, 2, False)
        wait(loads)
        step()
        norm_back(lambda r: tile_o[r, :].astype(F32), lambda r: dx[r, :], 0, 6, None, None, put_dx)
        saver.save(dx, dx_out)
        small = small_stages()
        next(small)
        while cursor[0] < red.last:
            step()
            next(small, None)
        for _ in small:
            pass
        saver.finish()
        red.finish()
        for copy in small_open:
            copy.wait_send()

    small_steps = n - 1 + 2 + max(geo.a_count - 1, 1)
    dma = pltpu.SemaphoreType.DMA
    tile = (tokens, width)
    return pl.pallas_call(
        kernel,
        out_shape=[
            b16((units, geo.rows, width)),
            f32(tile),
            f32((keys, width)),
            f32((SMALL, geo.rows)),
            b16((ups,) + tile),
            b16((2,) + tile),
            b16((4,) + tile),
            b16((2, keys, width)),
        ],
        in_specs=[HBM] * 3 + [VMEM, VMEM, SMEM] + [HBM] * 9 + [VMEM] * 2,
        out_specs=[HBM] * 3 + [VMEM] + [HBM] * 4,
        scratch_shapes=[
            pltpu.VMEM((2, width, width), BF16),
            pltpu.VMEM((keys, width), BF16),
            pltpu.VMEM((keys, width), BF16),
            pltpu.VMEM((5,) + tile, BF16),
            pltpu.VMEM((2, keys, width), BF16),
            pltpu.VMEM((2,) + tile, F32),
            pltpu.VMEM(tile, F32),
            pltpu.VMEM((2, per_image, width // 4), F32),
            pltpu.VMEM((tokens, tokens), F32),
            pltpu.VMEM((tokens, 128), jnp.int32),
            pltpu.VMEM((SMALL, width), F32),
            pltpu.VMEM((n - 1, SMALL, geo.rows), F32),
            pltpu.VMEM((3, SMALL, geo.rows), F32),
            pltpu.VMEM((SMALL, geo.rows), F32),
            pltpu.VMEM((SMALL, geo.rows), F32),
            pltpu.VMEM((geo.a_count, SMALL, geo.rows), F32),
            dma((2, 2 * n)),
            dma((8,)),
            dma((32,)),
            dma((2,)),
            dma((2,)),
            dma((small_steps,)),
            dma((small_steps,)),
        ]
        + Reduce.scratch(geo),
        compiler_params=pltpu.CompilerParams(
            collective_id=1, has_side_effects=True, vmem_limit_bytes=60 * MIB
        ),
    )(
        tokens_in, cotangent, memory, seg_col, seg_row, images, attn_in, attn_out, mlp_in, mlp_out,
        ring, acts, kv_acts, mlp_acts, xs, lse_all, vectors,
    )


def finish(geo, total, dmem, dx, layer_out, small, mem_tokens, counts):
    units, rows, width = total.shape
    n, ups = geo.narrow, geo.n_up
    images, per_image = dmem.shape[:2]
    tokens = dx.shape[0]
    span, lot = 128, tokens // units
    lanes = width // span

    def kernel(
        total_ref, dmem_ref, dx_ref, low_ref, small_ref,
        attn_in, attn_out, up, down, dmem_out, dx_out, low_out, *small_outs,
    ):
        u = pl.program_id(0)
        value = total_ref[0].astype(F32)

        @pl.when(u < geo.n_in)
        def _():
            attn_in[0] = value

        @pl.when((u >= geo.n_in) & (u < geo.up_at))
        def _():
            attn_out[0] = value

        @pl.when((u >= geo.up_at) & (u < geo.down_at))
        def _():
            for k in range(n):
                start = pl.multiple_of((k * ups + u - geo.up_at) * rows, rows)
                up[:, pl.ds(start, rows)] = value[:, k * rows : (k + 1) * rows]

        @pl.when(u >= geo.down_at)
        def _():
            down[...] = value

        @pl.when(u < lanes)
        def _():
            for i in range(images):
                dmem_out[:, i, :] = dmem_ref[i, :mem_tokens, :]
        dx_out[...] = dx_ref[...]
        low_out[...] = low_ref[...]
        at = 0
        for ref in small_outs:
            ref[...] = small_ref[pl.ds(at, ref.shape[0]), :]
            at += ref.shape[0]

    def unit_at(first, count):
        return lambda u: (jnp.clip(u - first, 0, count - 1), 0, 0)

    def lanes_at(u):
        return (0, 0, jnp.minimum(u, lanes - 1))

    shape = jax.ShapeDtypeStruct
    per_lot = pl.BlockSpec((lot, width), lambda u: (u, 0))
    return pl.pallas_call(
        kernel,
        grid=(units,),
        out_shape=[
            shape((geo.n_in, rows, width), F32),
            shape((geo.n_out, rows, width), F32),
            shape((rows, ups * width), F32),
            shape((ups * rows, width), F32),
            shape((mem_tokens, images, width), F32),
            shape((tokens, width), F32),
            shape((tokens, width), BF16),
        ]
        + [shape((count, rows), F32) for count in counts],
        in_specs=[
            pl.BlockSpec((1, rows, width), lambda u: (u, 0, 0)),
            pl.BlockSpec((images, per_image, span), lanes_at),
            per_lot,
            per_lot,
            pl.BlockSpec(small.shape, lambda u: (0, 0)),
        ],
        out_specs=[
            pl.BlockSpec((1, rows, width), unit_at(0, geo.n_in)),
            pl.BlockSpec((1, rows, width), unit_at(geo.n_in, geo.n_out)),
            pl.BlockSpec((rows, ups * width), lambda u: (0, 0)),
            pl.BlockSpec((rows, width), lambda u: (jnp.clip(u - geo.down_at, 0, ups - 1), 0)),
            pl.BlockSpec((mem_tokens, images, span), lanes_at),
            per_lot,
            per_lot,
        ]
        + [pl.BlockSpec((count, rows), lambda u: (0, 0)) for count in counts],
        compiler_params=pltpu.CompilerParams(vmem_limit_bytes=40 * MIB),
    )(total, dmem, dx, layer_out, small)


def per_device(
    mesh, hidden_in, memory, segment_ids, image_ids, attn_in, attn_out, mlp_in, mlp_out, gains, shifts, mlp_bias,
    cotangent,
):
    width = hidden_in.shape[2]
    n_in, n_out = attn_in.shape[0], attn_out.shape[0]
    geo = Geometry(mesh, width, n_in, n_out, mlp_in.shape[1])
    rows, n = geo.rows, geo.narrow
    images, mem_tokens = memory.shape[1], memory.shape[2]
    per_image = -(-mem_tokens // 128) * 128
    padded = jnp.pad(memory[0], ((0, 0), (0, per_image - mem_tokens), (0, 0))).reshape(images * per_image, width)
    small = jnp.concatenate([gains, shifts, mlp_bias.reshape(geo.n_up, rows)], axis=0).astype(F32)
    used = small.shape[0]
    small = jnp.pad(small, ((0, SMALL - used), (0, 0)))
    seg_col, seg_row = segment_ids.reshape(-1, 1), segment_ids
    ring, layer_out, acts, kv, mlp_acts, xs, lse, vec = forward(
        geo, hidden_in[0], padded, mem_tokens, seg_col, seg_row, image_ids, attn_in, attn_out, mlp_in, mlp_out, small
    )
    total, dx, dmem, small_total, *_ = backward(
        geo, mem_tokens, hidden_in[0], cotangent[0], padded, seg_col, seg_row, image_ids, attn_in, attn_out, mlp_in, mlp_out,
        (ring, acts, kv, mlp_acts, xs, lse, vec),
    )
    big = finish(
        geo, total, dmem.reshape(images, per_image, width), dx, layer_out, small_total, mem_tokens,
        (gains.shape[0], shifts.shape[0], geo.n_up),
    )
    return (
        big[6][None], big[5][None], big[4].transpose(1, 0, 2)[None], big[0], big[1], big[2], big[3],
        big[7], big[8], big[9].reshape(-1),
    )


def solution(mesh):
    split = ("wide", "narrow")
    return jax.shard_map(
        functools.partial(per_device, mesh),
        mesh=mesh,
        in_specs=(
            P(split, None, None), P(split, None, None, None), P(split, None), P(split, None), P(None, "narrow", None),
            P(None, "narrow", None), P("narrow", None), P("narrow", None), P(None, "narrow"), P(None, "narrow"),
            P("narrow"), P(split, None, None),
        ),
        out_specs=(
            P(split, None, None), P(split, None, None), P(split, None, None, None), P(None, "narrow", None),
            P(None, "narrow", None), P("narrow", None), P("narrow", None), P(None, "narrow"), P(None, "narrow"),
            P("narrow"),
        ),
        check_vma=False,
    )
```
